256 devices in a mesh: tok: 16 (over x, y), row: 4 (over z_hi, core), seq: 4 (over z_lo).
Axes of the slice: x: 4, y: 4, z: 8 (z_hi: 2, z_lo: 4; z = z_hi * 4 + z_lo), core: 2. Of those that a mesh axis runs over, the one named last changes fastest.
Arguments:
- reward_grad: bfloat16 [64, 256, 1024], P(None, 'tok', ('row', 'seq')), may hold values from -6 to 6
- embed_weight: bfloat16 [1024, 588], P(('row', 'seq')), may hold values from -0.25 to 0.25
- crop_offsets: int32 [64, 2], P('tok'), may hold values from 0 to 32
- features: bfloat16 [16, 128, 128, 512], P('tok', 'row', 'seq'), may hold values from -6 to 6
- conv_weight: bfloat16 [3, 3, 128, 128], replicated, may hold values from -0.1875 to 0.1875
- conv_bias: float32 [128], replicated, may hold values from -3 to 3
- out_weight: bfloat16 [3, 3, 128, 3], replicated, may hold values from -0.1875 to 0.1875
Outputs:
- features_grad: bfloat16 [16, 128, 128, 512], P('tok', 'row', 'seq')
The draws below stay inside these ranges and needn't reach their ends.
Inputs may be any that keep to these rules, and one draw needn't show every extreme that they name: crop_offsets[v] holds the first row and the first column of view v's 224 x 224 crop in frame v // 4.
All inputs are finite; a program needn't handle non-finite values.
Results may differ from the reference program's by a relative error of at most 0.0067.
Values may be sent and summed in bfloat16 or wider, within the bound.
No kernel may reach another device: no remote copies, remote signals or barrier semaphores. Data moves between devices by JAX's collectives and lax.ppermute only.
A program may use at most 128 MiB of HBM per device.

```python
import jax
import jax.numpy as jnp
from jax import lax

D = 1024
PATCH = 14
GRID = 16
CH = 128
VIEW_DEV = 4
PIX = 588
CROP = 224
PATCHES = 256
VIEWS = 64
FRAMES = 16
HEIGHT = 256
WIDTH = 256


def plant(result, own_key, smallest, high):
    longest = result.shape.index(max(result.shape))
    spots = []
    for shift in (0, 1):
        where = [jax.random.randint(jax.random.fold_in(own_key, axis), (), 0, length) for axis, length in enumerate(result.shape)]
        where[longest] = (where[longest] + shift) % result.shape[longest]
        spots.append(tuple(where))
    return result.at[spots[0]].set(smallest).at[spots[1]].set(high)


def level_of(own_key, dims, split, low, largest):
    loudness = 1.0
    for dim, shards_of in split:
        steps = jax.random.uniform(jax.random.fold_in(jax.random.fold_in(own_key, 6), dim), (shards_of,), jnp.float32, low / len(split), largest / len(split))
        loudness = loudness * jnp.repeat(jnp.exp(steps), dims[dim] // shards_of).reshape((-1,) + (1,) * (len(dims) - 1 - dim))
    return loudness


def gaussian(key, extent, deviation, reach, cuts=(), kind=jnp.bfloat16):
    values = jax.random.normal(key, extent, jnp.float32) * deviation
    if len(cuts) > 0:
        values = level_of(key, extent, cuts, -0.22, 0.18) * values
    return jnp.clip(values, min=-reach, max=reach).astype(kind)


def setup_inputs(seed: int = 0) -> dict:
    key_of = jax.random.split(jax.random.key(seed), 8)
    reward_grad = gaussian(key_of[0], (VIEWS, PATCHES, D), 1.0, 6.0, ((1, 16), (2, 16)))
    embed_weight = gaussian(key_of[1], (D, PIX), PIX ** -0.5, 0.25, ((0, 16),))
    crop_offsets = plant(jax.random.randint(key_of[2], (VIEWS, 2), 0, HEIGHT - CROP + 1), jax.random.fold_in(key_of[2], 1), 0, HEIGHT - CROP).astype(jnp.int32)
    features = gaussian(key_of[3], (FRAMES, HEIGHT // 2, WIDTH // 2, 4 * CH), 1.0, 6.0, ((0, 16), (1, 4), (2, 4)))
    conv_weight = gaussian(key_of[4], (3, 3, CH, CH), (9 * CH) ** -0.5, 0.1875)
    conv_bias = gaussian(key_of[5], (CH,), 0.5, 3.0, (), jnp.float32)
    out_weight = gaussian(key_of[6], (3, 3, CH, 3), (9 * CH) ** -0.5, 0.1875)
    return {"reward_grad": reward_grad, "embed_weight": embed_weight, "crop_offsets": crop_offsets, "features": features, "conv_weight": conv_weight, "conv_bias": conv_bias, "out_weight": out_weight}


PIXEL_STD = (0.26862954, 0.26130258, 0.27577711)


def inverse_haar(coarse):
    channels = coarse.shape[-1] // 4
    values = coarse.astype(jnp.float32)
    smooth = values[..., :channels]
    vertical = values[..., channels:2 * channels]
    horizontal = values[..., 2 * channels:3 * channels]
    diagonal = values[..., 3 * channels:]
    upper_sum = smooth + vertical
    lower_sum = smooth - vertical
    upper_diff = horizontal + diagonal
    lower_diff = horizontal - diagonal
    upper_row = 0.5 * jnp.stack([upper_sum + upper_diff, upper_sum - upper_diff], axis=2)
    lower_row = 0.5 * jnp.stack([lower_sum + lower_diff, lower_sum - lower_diff], axis=2)
    joined = jnp.stack([upper_row, lower_row], axis=1)
    return joined.reshape(2 * coarse.shape[0], 2 * coarse.shape[1], channels)


def haar_analysis(fine_grid):
    half_rows = fine_grid.shape[0] // 2
    half_cols = fine_grid.shape[1] // 2
    channels = fine_grid.shape[2]
    blocks = fine_grid.reshape(half_rows, 2, half_cols, 2, channels)
    top_left = blocks[:, 0, :, 0]
    top_right = blocks[:, 0, :, 1]
    bottom_left = blocks[:, 1, :, 0]
    bottom_right = blocks[:, 1, :, 1]
    smooth = 0.5 * (top_left + top_right + bottom_left + bottom_right)
    vertical = 0.5 * (top_left + top_right - bottom_left - bottom_right)
    horizontal = 0.5 * (top_left - top_right + bottom_left - bottom_right)
    diagonal = 0.5 * (top_left - top_right - bottom_left + bottom_right)
    return jnp.concatenate([smooth, vertical, horizontal, diagonal], axis=-1)


def correlate(image, kernel):
    return lax.conv_general_dilated(image[None], kernel, (1, 1), ((1, 1), (1, 1)), dimension_numbers=("NHWC", "HWIO", "NHWC"), precision=lax.Precision.HIGHEST)[0]


def flipped(kernel):
    return jnp.flip(kernel, (0, 1)).transpose(0, 1, 3, 2)


def to_bfloat(values):
    return lax.optimization_barrier(values.astype(jnp.bfloat16)).astype(jnp.float32)


def reference(reward_grad, embed_weight, crop_offsets, features, conv_weight, conv_bias, out_weight):
    patch_grad = jnp.einsum("vpd,dk->vpk", reward_grad.astype(jnp.float32), embed_weight.astype(jnp.float32), precision=lax.Precision.HIGHEST).astype(jnp.bfloat16)
    crop_grad = patch_grad.reshape(VIEWS, GRID, GRID, 3, PATCH, PATCH).transpose(0, 3, 1, 4, 2, 5).reshape(VIEWS, 3, CROP, CROP)
    pixel_std = jnp.array(PIXEL_STD, jnp.float32)[:, None, None]
    zero_index = jnp.zeros((), jnp.int32)

    def place(frame_index):
        canvas = jnp.zeros((3, HEIGHT, WIDTH), jnp.float32)
        for member in range(VIEW_DEV):
            view_index = frame_index * VIEW_DEV + member
            crop_piece = lax.dynamic_index_in_dim(crop_grad, view_index, 0, keepdims=False).astype(jnp.float32)
            corner = lax.dynamic_index_in_dim(crop_offsets, view_index, 0, keepdims=False)
            blank = jnp.zeros((3, HEIGHT, WIDTH), jnp.float32)
            canvas = canvas + lax.dynamic_update_slice(blank, crop_piece, (zero_index, corner[0], corner[1]))
        return (canvas / pixel_std).astype(jnp.bfloat16)

    pixel_grad = lax.map(place, jnp.arange(FRAMES, dtype=jnp.int32))
    conv_kernel = conv_weight.astype(jnp.float32)
    back_kernel = flipped(conv_kernel)
    out_kernel = flipped(out_weight.astype(jnp.float32))

    def decode_back(inputs):
        coarse, pixels = inputs
        decoded = to_bfloat(inverse_haar(coarse))
        pre = correlate(decoded, conv_kernel) + conv_bias
        act_grad = correlate(pixels.astype(jnp.float32).transpose(1, 2, 0), out_kernel)
        sigmoid_pre = jax.nn.sigmoid(pre)
        pre_grad = to_bfloat(act_grad * sigmoid_pre * (1.0 + pre * (1.0 - sigmoid_pre)))
        decoded_grad = correlate(pre_grad, back_kernel)
        return haar_analysis(decoded_grad).astype(jnp.bfloat16)

    return lax.map(decode_back, (features, pixel_grad))
```

```python
import jax
import jax.numpy as jnp
import numpy as np
from jax import lax
from jax.experimental import pallas as pl
from jax.experimental.pallas import tpu as pltpu
from jax.sharding import PartitionSpec as P

PIXEL_STD = (0.26862954, 0.26130258, 0.27577711)
BF16 = jnp.bfloat16
F32 = jnp.float32
VIEWS = 4
TILE_PIX = 68
SPAN = 128
PACK_ROWS = 24
PACK_STEP = 23
PACKED = 640
PITCH = 48
NT = (((1,), (1,)), ((), ()))
TN = (((0,), (0,)), ((), ()))
VMEM_LIMIT = 40 * 2**20


def iota(shape, axis):
    return lax.broadcasted_iota(jnp.int32, shape, axis)


def dot(a, b, dims=(((1,), (0,)), ((), ()))):
    return lax.dot_general(a, b, dims, preferred_element_type=F32)


def as_bf16(mask):
    return jnp.where(mask, 1.0, 0.0).astype(BF16)


def block_place(third, channel):
    start = (third * 3 + channel) * TILE_PIX
    return start // SPAN, start % SPAN


def prep_kernel(offsets, weight, line, wide, cols, rows):
    pair = jnp.concatenate([weight[...], weight[...]], axis=0)
    slot = iota((704, 588), 0)
    pick = as_bf16(((slot >> 4) * 14 + (slot & 15) == iota((704, 588), 1)) & ((slot & 15) < 14))
    spread = dot(pick, pair, NT).astype(BF16).reshape(44, 16, SPAN)
    half = iota((44, 16, SPAN), 2) >> 6
    nothing = jnp.zeros((44, 16, SPAN), BF16)
    for group in range(4):
        kept = jnp.where(half == group % 2, spread, nothing)
        wide[:, group, :, 0:SPAN] = kept if group < 2 else nothing
        wide[:, group, :, SPAN:] = kept if group >= 2 else nothing
    slot, lane = iota((256, 512), 0), iota((256, 512), 1)
    gap = (lane >> 7) * 64 - 2 + (lane & 127) - (slot >> 4) * 14 - (slot & 15)
    gap = jnp.where(((slot & 15) < 14) & ((lane & 127) < TILE_PIX), gap, -1000)
    for view in range(VIEWS):
        cols[view] = as_bf16(gap == offsets[view, 1])
    first = line[0:1]
    owner = line[1:2]
    for view in range(VIEWS):
        first = first + jnp.where(owner == view, offsets[view, 0], 0)
    step = iota((PACK_ROWS, 896), 0)
    for band in range(4):
        for third in range(3):
            y = step + (64 * band - 2 + PACK_STEP * third)
            start = (band * 3 + third) * PACK_ROWS
            hit = jnp.where((y == first) & (step < PACK_STEP), 1.0, 0.0)
            rows[start : start + PACK_ROWS, :] = hit


def placement_matrices(offsets, weight):
    index = np.arange(896)
    line = np.zeros((8, 896), np.int32)
    line[0] = 14 * (index % 16) + (index % 224) // 16
    line[1] = index // 224
    return pl.pallas_call(
        prep_kernel,
        out_shape=(
            jax.ShapeDtypeStruct((44, 4, 16, 256), BF16),
            jax.ShapeDtypeStruct((VIEWS, 256, 512), BF16),
            jax.ShapeDtypeStruct((288, 896), F32),
        ),
        in_specs=[
            pl.BlockSpec(memory_space=pltpu.SMEM),
            pl.BlockSpec(memory_space=pltpu.VMEM),
            pl.BlockSpec(memory_space=pltpu.VMEM),
        ],
        compiler_params=pltpu.CompilerParams(vmem_limit_bytes=VMEM_LIMIT),
        name="prep",
    )(offsets, weight, jnp.asarray(line))


def place_kernel(reward, wide, cols, rows, out, flat, left, strips, across, canvas):
    flat[...] = reward[...].astype(F32).reshape(512, SPAN)
    for view in range(VIEWS):
        for pair in range(8):
            top = (pair // 2) * 64 + view * 16
            side = (pair % 2) * SPAN
            values = flat[pl.ds(view * 8 + pair, 16, stride=32), :]
            left[top : top + 16, side : side + SPAN] = values.astype(BF16)
    low = iota((64, SPAN), 1) < 64
    for quad in range(11):
        part = dot(left[...], wide[4 * quad : 4 * quad + 4].reshape(256, 256), NT)
        for member in range(2):
            own = [part[64 * h : 64 * h + 64, member * SPAN : (member + 1) * SPAN] for h in range(4)]
            turned = [pltpu.roll(piece, 64, 1) for piece in own]
            for odd in range(2):
                start = (4 * quad + 2 * member + odd) * 16
                for side in range(2):
                    a, b = 2 * side, 2 * side + 1
                    if odd == 0:
                        joined = jnp.where(low, own[a], turned[b]).astype(BF16)
                    else:
                        joined = jnp.where(low, turned[a], own[b]).astype(BF16)
                    for view in range(VIEWS):
                        strips[view, start : start + 16, side * SPAN : (side + 1) * SPAN] = joined[
                            view * 16 : view * 16 + 16
                        ]
    for view in range(VIEWS):
        for channel in range(3):
            across[channel, view * 224 : (view + 1) * 224, :] = dot(
                strips[view, channel * 224 : (channel + 1) * 224, :], cols[view]
            ).astype(BF16)
    picks = rows[...].astype(BF16)
    for channel in range(3):
        canvas[channel] = dot(picks, across[channel])
    lane = iota((PACK_ROWS, SPAN), 1)
    for band in range(4):
        for column in range(4):
            tiles = [None] * 5
            for third in range(3):
                for channel in range(3):
                    tile, shift = block_place(third, channel)
                    start = (band * 3 + third) * PACK_ROWS
                    block = canvas[channel, start : start + PACK_ROWS, column * SPAN : (column + 1) * SPAN]
                    if shift:
                        block = pltpu.roll(block, shift, 1)
                    pieces = [(tile, block)]
                    if shift + TILE_PIX > SPAN:
                        pieces = [
                            (tile, jnp.where(lane >= shift, block, 0.0)),
                            (tile + 1, jnp.where(lane < shift, block, 0.0)),
                        ]
                    for index, piece in pieces:
                        tiles[index] = piece if tiles[index] is None else tiles[index] + piece
            for index in range(5):
                out[band * 4 + column, :, index * SPAN : (index + 1) * SPAN] = tiles[index].astype(BF16)


def place_partials(reward, wide, cols, rows):
    return pl.pallas_call(
        place_kernel,
        out_shape=jax.ShapeDtypeStruct((16, PACK_ROWS, PACKED), BF16),
        scratch_shapes=[
            pltpu.VMEM((512, SPAN), F32),
            pltpu.VMEM((256, 256), BF16),
            pltpu.VMEM((VIEWS, 704, 256), BF16),
            pltpu.VMEM((3, 896, 512), BF16),
            pltpu.VMEM((3, 288, 512), F32),
        ],
        compiler_params=pltpu.CompilerParams(vmem_limit_bytes=VMEM_LIMIT),
        name="place",
    )(reward, wide, cols, rows)


def inverse_haar(values):
    smooth, vertical, horizontal, diagonal = [values[:, k * 128 : (k + 1) * 128].astype(F32) for k in range(4)]
    upper_sum = smooth + vertical
    lower_sum = smooth - vertical
    upper_diff = horizontal + diagonal
    lower_diff = horizontal - diagonal
    return [
        0.5 * (upper_sum + upper_diff),
        0.5 * (upper_sum - upper_diff),
        0.5 * (lower_sum + lower_diff),
        0.5 * (lower_sum - lower_diff),
    ]


def gate_kernel(place, features, above, below, before, after, weight, bias, out, fine, near, far, taps):
    def put(line, values):
        for k, phase in enumerate(inverse_haar(values)):
            fine[line, 8:40, k * 128 : (k + 1) * 128] = phase

    put(0, above[0])
    put(33, below[0])

    @pl.loop(0, 32)
    def _(line):
        put(line + 1, features[line])

    for column, source in ((7, before), (40, after)):
        for k, phase in enumerate(inverse_haar(source[...])):
            for line in range(34):
                fine[line, column : column + 1, k * 128 : (k + 1) * 128] = phase[line : line + 1]

    @pl.loop(0, 34)
    def _(line):
        start = pl.multiple_of(line * PITCH, PITCH)
        near[pl.ds(start, PITCH), :] = fine[line, 7:55, :].astype(BF16)
        far[pl.ds(start, PITCH), :] = fine[line, 8:56, :].astype(BF16)

    nothing = jnp.zeros((128, 128), BF16)
    for a in range(3):
        for u in range(4):
            start = (a * 4 + u) * 128
            taps[start : start + 128, 0:128] = weight[a, u] if u < 3 else nothing
            taps[start : start + 128, 128:] = weight[a, u - 1] if u > 0 else nothing
    wide_bias = jnp.concatenate([bias[...], bias[...]], axis=1)
    column, lane = iota((PITCH, 256), 0), iota((PITCH, 256), 1)
    outside = ((place[1] == 0) & (column == 0) & (lane < 128)) | ((place[1] == 3) & (column == 32) & (lane >= 128))
    inside = jnp.where(outside, 0.0, 1.0)[None]
    count = 11 * PITCH

    @pl.loop(0, 3)
    def _(chunk):
        for phase in range(2):
            pieces = []
            for a in range(3):
                lines, parity = divmod(phase + a, 2)
                start = pl.multiple_of(chunk * count + lines * PITCH, PITCH)
                for source in (near, far):
                    pieces.append(source[pl.ds(start, count), parity * 256 : (parity + 1) * 256])
            pre = dot(jnp.concatenate(pieces, axis=1), taps[...]) + wide_bias
            sigmoid = 1.0 / (1.0 + jnp.exp(-pre))
            slope = sigmoid * (1.0 + pre * (1.0 - sigmoid))
            slope = (slope.reshape(11, PITCH, 256) * inside).reshape(count, 256)
            here = pl.multiple_of(chunk * count, PITCH)
            out[pl.ds(here, count), phase * 256 : (phase + 1) * 256] = slope.astype(BF16)

    empty = jnp.zeros((PITCH, 256), BF16)

    @pl.when(place[0] == 0)
    def _():
        out[0:PITCH, 0:256] = empty

    @pl.when(place[0] == 3)
    def _():
        out[32 * PITCH : 33 * PITCH, 256:512] = empty


def gates(place, features, above, below, before, after, weight, bias):
    specs = [pl.BlockSpec(memory_space=pltpu.VMEM)] * 7
    return pl.pallas_call(
        gate_kernel,
        out_shape=jax.ShapeDtypeStruct((33 * PITCH, 512), BF16),
        in_specs=[pl.BlockSpec(memory_space=pltpu.SMEM)] + specs,
        scratch_shapes=[
            pltpu.VMEM((34, 56, 512), F32),
            pltpu.VMEM((34 * PITCH, 512), BF16),
            pltpu.VMEM((34 * PITCH, 512), BF16),
            pltpu.VMEM((1536, 256), BF16),
        ],
        compiler_params=pltpu.CompilerParams(vmem_limit_bytes=VMEM_LIMIT),
        cost_estimate=pl.CostEstimate(flops=5 * 10**9, bytes_accessed=4 * 10**6, transcendentals=2 * 10**6),
        name="gate",
    )(place, features, above, below, before, after, weight, bias)


def finish_kernel(parts, gate, weight, out_taps, spread, lines, windows, out, pixels, stacked, near, far, taps):
    total = parts[0].astype(F32)
    for source in range(1, 16):
        total = total + parts[source].astype(F32)
    lane = iota((PACK_ROWS, SPAN), 1)
    pixels[...] = jnp.zeros_like(pixels)
    for channel in range(3):
        for third in range(3):
            tile, shift = block_place(third, channel)
            block = total[:, tile * SPAN : (tile + 1) * SPAN]
            if shift:
                block = pltpu.roll(block, SPAN - shift, 1)
            if shift + TILE_PIX > SPAN:
                rest = pltpu.roll(total[:, (tile + 1) * SPAN : (tile + 2) * SPAN], SPAN - shift, 1)
                block = jnp.where(lane < SPAN - shift, block, rest)
            start = channel * 80 + third * PACK_STEP
            pixels[start : start + PACK_ROWS, :] = block / PIXEL_STD[channel]
    rounded = pixels[...].astype(BF16)
    picked = None
    for third in range(3):
        moved = dot(rounded, spread[third]).astype(BF16)
        term = dot(lines[third], moved)
        picked = term if picked is None else picked + term
    picked = picked.astype(BF16)
    for line in range(11):
        for k in range(4):
            stacked[line, k * 16 : k * 16 + 16, :] = picked[line * 16 : line * 16 + 16, k * SPAN : (k + 1) * SPAN]
    kernel = jnp.concatenate([dot(windows[k], out_taps[...]).astype(BF16) for k in range(4)], axis=1)
    nothing = jnp.zeros((128, 128), BF16)
    for a in range(3):
        for u in range(4):
            start = (a * 4 + u) * 128
            for q in range(2):
                b = q + 2 - u
                block = weight[a, b] if 0 <= b <= 2 else nothing
                taps[q * 128 : (q + 1) * 128, start : start + 128] = block

    @pl.loop(0, 11)
    def _(line):
        act = dot(stacked[line], kernel, TN)
        for third in range(3):
            index = line * 3 + third
            scale = gate[pl.ds(pl.multiple_of(index * PITCH, PITCH), PITCH), :].astype(F32)
            grad = act[third * 40 : third * 40 + 40] * scale[0:40]
            start = pl.multiple_of(index * 32, 32)
            near[pl.ds(start, 32), :] = grad[0:32].astype(BF16)
            far[pl.ds(start, 32), :] = grad[1:33].astype(BF16)

    @pl.loop(0, 4)
    def _(chunk):
        found = []
        for p in range(2):
            pieces = []
            for a in range(3):
                step, parity = divmod(p + 2 - a, 2)
                start = pl.multiple_of(chunk * 256 + step * 32, 32)
                for source in (near, far):
                    pieces.append(source[pl.ds(start, 256), parity * 256 : (parity + 1) * 256])
            found.append(dot(jnp.concatenate(pieces, axis=1), taps[...], NT))
        plus, minus = found[0] + found[1], found[0] - found[1]
        bands = [
            plus[:, :128] + plus[:, 128:],
            minus[:, :128] + minus[:, 128:],
            plus[:, :128] - plus[:, 128:],
            minus[:, :128] - minus[:, 128:],
        ]
        for k, band in enumerate(bands):
            out[pl.ds(pl.multiple_of(chunk * 8, 8), 8), :, k * 128 : (k + 1) * 128] = (
                (0.5 * band).astype(BF16).reshape(8, 32, 128)
            )


def window_picks():
    spread = np.zeros((3, SPAN, 512), np.float32)
    lines = np.zeros((3, 176, 240), np.float32)
    windows = np.zeros((4, 64, 32), np.float32)
    for third in range(3):
        for wx in range(4):
            for j in range(33):
                spread[third, 2 * j + wx, wx * SPAN + third * 40 + j] = 1
        for line in range(11):
            for channel in range(3):
                for wy in range(4):
                    y = 2 * (3 * line + third) + wy
                    lines[third, line * 16 + channel * 4 + wy, channel * 80 + y] = 1
    for py in range(2):
        for px in range(2):
            for wx in range(4):
                for channel in range(3):
                    for wy in range(4):
                        a, b = py + 2 - wy, px + 2 - wx
                        if 0 <= a <= 2 and 0 <= b <= 2:
                            windows[py * 2 + px, wx * 16 + channel * 4 + wy, a * 9 + b * 3 + channel] = 1
    return [jnp.asarray(each, BF16) for each in (spread, lines, windows)]


def finish(parts, gate, weight, out_taps):
    return pl.pallas_call(
        finish_kernel,
        out_shape=jax.ShapeDtypeStruct((32, 32, 512), BF16),
        scratch_shapes=[
            pltpu.VMEM((240, SPAN), F32),
            pltpu.VMEM((11, 64, SPAN), BF16),
            pltpu.VMEM((33 * 32, 512), BF16),
            pltpu.VMEM((33 * 32, 512), BF16),
            pltpu.VMEM((256, 1536), BF16),
        ],
        compiler_params=pltpu.CompilerParams(vmem_limit_bytes=VMEM_LIMIT),
        name="finish",
    )(parts, gate, weight, out_taps, *window_picks())


def neighbours(first, last, axis):
    size = lax.axis_size(axis)
    up = [(i, i + 1) for i in range(size - 1)]
    down = [(i + 1, i) for i in range(size - 1)]
    return lax.ppermute(last, axis, up), lax.ppermute(first, axis, down)


def on_device(reward_grad, embed_weight, crop_offsets, features, conv_weight, conv_bias, out_weight):
    mine = lax.all_to_all(reward_grad.reshape(64, 8, SPAN), "tok", split_axis=0, concat_axis=0, tiled=True)
    wide, cols, rows = placement_matrices(crop_offsets, embed_weight)
    coarse = features[0]
    above, below = neighbours(coarse[:1], coarse[31:], "row")
    edges = [
        jnp.concatenate([above[:, k], coarse[:, k], below[:, k]], axis=0) for k in (0, 31)
    ]
    before, after = neighbours(edges[0], edges[1], "seq")
    place = jnp.stack([lax.axis_index("row"), lax.axis_index("seq")]).astype(jnp.int32)
    partials = place_partials(mine, wide, cols, rows)
    parts = lax.all_to_all(partials, ("row", "seq"), split_axis=0, concat_axis=0, tiled=True)
    gate = gates(place, coarse, above, below, before, after, conv_weight, conv_bias[None])
    out_taps = jnp.pad(out_weight.transpose(0, 1, 3, 2).reshape(27, 128), ((0, 5), (0, 0)))
    return finish(parts, gate, conv_weight, out_taps)[None]


def solution(mesh):
    placed = (
        P(None, "tok", ("row", "seq")),
        P(("row", "seq"), None),
        P("tok", None),
        P("tok", "row", "seq", None),
        P(),
        P(),
        P(),
    )
    return jax.shard_map(
        on_device,
        mesh=mesh,
        in_specs=placed,
        out_specs=P("tok", "row", "seq", None),
        check_vma=False,
    )
```

```python
import jax
import jax.numpy as jnp
import numpy as np
from jax import lax
from jax.experimental import pallas as pl
from jax.experimental.pallas import tpu as pltpu
from jax.sharding import Mesh
from jax.sharding import PartitionSpec as P

PIXEL_STD = (0.26862954, 0.26130258, 0.27577711)
BF16 = jnp.bfloat16
F32 = jnp.float32
VIEWS = 4
TILE_PIX = 68
SPAN = 128
HALF_TILE = 34
BAND = 80
PACKED = 112
PITCH = 48
NT = (((1,), (1,)), ((), ()))
TN = (((0,), (0,)), ((), ()))
VMEM_LIMIT = 16 * 2**20


def iota(shape, axis):
    return lax.broadcasted_iota(jnp.int32, shape, axis)


def dot(a, b, dims=(((1,), (0,)), ((), ()))):
    return lax.dot_general(a, b, dims, preferred_element_type=F32)


def as_bf16(mask):
    return jnp.where(mask, 1.0, 0.0).astype(BF16)


def pair_kernel(reward, out):
    for pair in range(32):
        out[pair] = jnp.concatenate([reward[2 * pair], reward[2 * pair + 1]], axis=1)


def view_pairs(reward):
    return pl.pallas_call(
        pair_kernel,
        out_shape=jax.ShapeDtypeStruct((32, 16, SPAN), BF16),
        compiler_params=pltpu.CompilerParams(vmem_limit_bytes=VMEM_LIMIT),
        name="pairs",
    )(reward)


def prep_kernel(offsets, weight, other_weight, line, wide, cols, rows):
    pair = jnp.concatenate([weight[...], other_weight[...]], axis=0)
    slot = iota((704, 588), 0)
    pick = as_bf16(((slot >> 4) * 14 + (slot & 15) == iota((704, 588), 1)) & ((slot & 15) < 14))
    spread = dot(pick, pair, NT).astype(BF16).reshape(44, 16, SPAN)
    nothing = jnp.zeros((44, 16, SPAN), BF16)
    for group in range(4):
        for k in range(4):
            wide[:, group, :, k * SPAN : (k + 1) * SPAN] = spread if k == group else nothing
    slot, lane = iota((256, 512), 0), iota((256, 512), 1)
    gap = (lane >> 7) * 64 - 2 + (lane & 127) - (slot >> 4) * 14 - (slot & 15)
    gap = jnp.where(((slot & 15) < 14) & ((lane & 127) < TILE_PIX), gap, -1000)
    for view in range(VIEWS):
        cols[view] = as_bf16(gap == offsets[1, view])
    first = line[0:1]
    owner = line[1:2]
    for view in range(VIEWS):
        first = first + jnp.where(owner == view, offsets[0, view], 0)
    step = iota((BAND, 896), 0)
    core = lax.axis_index("core")
    for high in range(2):
        y = step + (64 * (2 * high + core) - 2)
        hit = as_bf16((y == first) & (step < TILE_PIX))
        rows[high * BAND : (high + 1) * BAND, :] = hit


def placement_matrices(offsets, weight, other_weight):
    index = np.arange(896)
    line = np.zeros((8, 896), np.int32)
    line[0] = 14 * (index % 16) + (index % 224) // 16
    line[1] = index // 224
    return pl.pallas_call(
        prep_kernel,
        out_shape=(
            jax.ShapeDtypeStruct((44, 4, 16, 512), BF16),
            jax.ShapeDtypeStruct((VIEWS, 256, 512), BF16),
            jax.ShapeDtypeStruct((2 * BAND, 896), BF16),
        ),
        in_specs=[pl.BlockSpec(memory_space=pltpu.SMEM)] + [pl.BlockSpec(memory_space=pltpu.VMEM)] * 3,
        compiler_params=pltpu.CompilerParams(vmem_limit_bytes=VMEM_LIMIT),
        name="prep",
    )(offsets, weight, other_weight, jnp.asarray(line))


def place_kernel(reward, other, wide, cols, rows, out, flat, left, strips, across, canvas, packed):
    own, theirs = [each[...].astype(F32).reshape(512, SPAN) for each in (reward, other)]
    low = iota((512, SPAN), 1) < 64
    flat[0] = jnp.where(low, own, pltpu.roll(theirs, 64, 1))
    flat[1] = jnp.where(low, pltpu.roll(own, 64, 1), theirs)
    for view in range(VIEWS):
        for patch in range(16):
            top = (patch // 4) * 64 + view * 16
            side = (patch % 4) * SPAN
            values = flat[view % 2, pl.ds((view // 2) * 16 + patch, 16, stride=32), :]
            left[top : top + 16, side : side + SPAN] = values.astype(BF16)
    low = iota((64, SPAN), 1) < 64
    for quad in range(11):
        part = dot(left[...], wide[4 * quad : 4 * quad + 4].reshape(256, 512), NT)
        for member in range(2):
            own = [part[64 * h : 64 * h + 64, member * SPAN : (member + 1) * SPAN] for h in range(4)]
            turned = [pltpu.roll(piece, 64, 1) for piece in own]
            for odd in range(2):
                start = (4 * quad + 2 * member + odd) * 16
                for side in range(2):
                    a, b = 2 * side, 2 * side + 1
                    if odd == 0:
                        joined = jnp.where(low, own[a], turned[b]).astype(BF16)
                    else:
                        joined = jnp.where(low, turned[a], own[b]).astype(BF16)
                    for view in range(VIEWS):
                        strips[view, start : start + 16, side * SPAN : (side + 1) * SPAN] = joined[
                            view * 16 : view * 16 + 16
                        ]
    for view in range(VIEWS):
        for channel in range(3):
            across[channel, view * 224 : (view + 1) * 224, :] = dot(
                strips[view, channel * 224 : (channel + 1) * 224, :], cols[view]
            ).astype(BF16)
    for channel in range(3):
        canvas[channel] = dot(rows[...], across[channel])
    lane = iota((HALF_TILE, SPAN), 1)
    wide_lane = iota((BAND, SPAN), 1)
    for high in range(2):
        for column in range(4):
            side = slice(column * SPAN, (column + 1) * SPAN)
            top = high * BAND
            for channel in range(3):
                upper = canvas[channel, top : top + HALF_TILE, side]
                lower = pltpu.roll(canvas[channel, top + HALF_TILE : top + 2 * HALF_TILE, side], 64, 1)
                packed[channel * HALF_TILE : (channel + 1) * HALF_TILE, :] = jnp.where(lane < 64, upper, lower)
            last = [canvas[channel, top : top + BAND, side] for channel in range(3)]
            joined = jnp.where(wide_lane < 68, last[0], pltpu.roll(last[1], 4, 1))
            joined = jnp.where(wide_lane < 72, joined, pltpu.roll(last[2], 8, 1))
            rest = None
            for block in range(7):
                piece = pltpu.roll(joined[block * 10 : block * 10 + 10], (64 + block * 12) % SPAN, 1)
                rest = piece if block == 0 else jnp.where(wide_lane[:10] < block * 12, rest, piece)
            packed[3 * HALF_TILE :, :] = rest
            out[high * 4 + column] = packed[...].astype(BF16)


def place_partials(reward, other, wide, cols, rows):
    return pl.pallas_call(
        place_kernel,
        out_shape=jax.ShapeDtypeStruct((8, PACKED, SPAN), BF16),
        scratch_shapes=[
            pltpu.VMEM((2, 512, SPAN), F32),
            pltpu.VMEM((256, 512), BF16),
            pltpu.VMEM((VIEWS, 704, 256), BF16),
            pltpu.VMEM((3, 896, 512), BF16),
            pltpu.VMEM((3, 2 * BAND, 512), F32),
            pltpu.VMEM((PACKED, SPAN), F32),
        ],
        compiler_params=pltpu.CompilerParams(vmem_limit_bytes=VMEM_LIMIT),
        name="place",
    )(reward, other, wide, cols, rows)


def strip_kernel(features, partner_top, partner_bottom, far_bottom, far_top, first, last, spread):
    lower = lax.axis_index("core") == 1
    above = jnp.where(lower, partner_bottom[0].astype(F32), far_bottom[0].astype(F32))
    below = jnp.where(lower, far_top[0].astype(F32), partner_top[0].astype(F32))
    for out, side, row, corner in ((first, 0, 0, 0), (last, 16, 15, 31)):
        for k in range(4):
            lanes = slice(k * SPAN, (k + 1) * SPAN)
            spread[k] = features[:, side : side + 16, lanes].astype(F32).reshape(512, SPAN)
            edge = spread[k, pl.ds(row, 32, stride=16), :]
            ends = [above[corner : corner + 1, lanes], below[corner : corner + 1, lanes], jnp.zeros((14, SPAN), F32)]
            out[:, lanes] = jnp.concatenate([edge] + ends, axis=0).astype(BF16)


def strips_of(features, *halo):
    return pl.pallas_call(
        strip_kernel,
        out_shape=[jax.ShapeDtypeStruct((48, 512), BF16)] * 2,
        scratch_shapes=[pltpu.VMEM((4, 512, SPAN), F32)],
        compiler_params=pltpu.CompilerParams(vmem_limit_bytes=VMEM_LIMIT),
        name="strips",
    )(features, *halo)


def inverse_haar(values):
    smooth, vertical, horizontal, diagonal = [values[:, k * 128 : (k + 1) * 128].astype(F32) for k in range(4)]
    upper_sum = smooth + vertical
    lower_sum = smooth - vertical
    upper_diff = horizontal + diagonal
    lower_diff = horizontal - diagonal
    return [
        0.5 * (upper_sum + upper_diff),
        0.5 * (upper_sum - upper_diff),
        0.5 * (lower_sum + lower_diff),
        0.5 * (lower_sum - lower_diff),
    ]


def gate_kernel(
    features, partner_top, partner_bottom, far_bottom, far_top, before, after, weight, bias, out_weight, windows,
    out, back, kernel, fine, near, far, taps, small,
):
    high, core, column_tile = lax.axis_index("zhi"), lax.axis_index("core"), lax.axis_index("seq")
    lower = core == 1

    def put(line, values):
        for k, phase in enumerate(inverse_haar(values)):
            fine[line, 8:40, k * 128 : (k + 1) * 128] = phase

    put(0, jnp.where(lower, partner_bottom[0].astype(F32), far_bottom[0].astype(F32)))
    put(33, jnp.where(lower, far_top[0].astype(F32), partner_top[0].astype(F32)))

    @pl.loop(0, 32)
    def _(line):
        put(line + 1, features[line])

    for column, source in ((7, before), (40, after)):
        for k, phase in enumerate(inverse_haar(source[...])):
            for line in range(34):
                row = 32 if line == 0 else 33 if line == 33 else line - 1
                fine[line, column : column + 1, k * 128 : (k + 1) * 128] = phase[row : row + 1]

    @pl.loop(0, 34)
    def _(line):
        start = pl.multiple_of(line * PITCH, PITCH)
        near[pl.ds(start, PITCH), :] = fine[line, 7:55, :].astype(BF16)
        far[pl.ds(start, PITCH), :] = fine[line, 8:56, :].astype(BF16)

    nothing = jnp.zeros((128, 128), BF16)
    for a in range(3):
        for u in range(4):
            start = (a * 4 + u) * 128
            taps[start : start + 128, 0:128] = weight[a, u] if u < 3 else nothing
            taps[start : start + 128, 128:] = weight[a, u - 1] if u > 0 else nothing
    wide_bias = jnp.concatenate([bias[...], bias[...]], axis=1)
    column, lane = iota((PITCH, 256), 0), iota((PITCH, 256), 1)
    outside = ((column_tile == 0) & (column == 0) & (lane < 128)) | ((column_tile == 3) & (column == 32) & (lane >= 128))
    inside = jnp.where(outside, 0.0, 1.0)[None]
    count = 11 * PITCH

    @pl.loop(0, 3)
    def _(chunk):
        for phase in range(2):
            pieces = []
            for a in range(3):
                lines, parity = divmod(phase + a, 2)
                start = pl.multiple_of(chunk * count + lines * PITCH, PITCH)
                for source in (near, far):
                    pieces.append(source[pl.ds(start, count), parity * 256 : (parity + 1) * 256])
            pre = dot(jnp.concatenate(pieces, axis=1), taps[...]) + wide_bias
            sigmoid = 1.0 / (1.0 + jnp.exp(-pre))
            slope = sigmoid * (1.0 + pre * (1.0 - sigmoid))
            slope = (slope.reshape(11, PITCH, 256) * inside).reshape(count, 256)
            here = pl.multiple_of(chunk * count, PITCH)
            out[pl.ds(here, count), phase * 256 : (phase + 1) * 256] = slope.astype(BF16)

    empty = jnp.zeros((PITCH, 256), BF16)

    @pl.when((high == 0) & (core == 0))
    def _():
        out[0:PITCH, 0:256] = empty

    @pl.when((high == 1) & (core == 1))
    def _():
        out[32 * PITCH : 33 * PITCH, 256:512] = empty


    for a in range(3):
        for u in range(4):
            start = (a * 4 + u) * 128
            for q in range(2):
                b = q + 2 - u
                block = weight[a, b].astype(F32).T.astype(BF16) if 0 <= b <= 2 else nothing
                back[start : start + 128, q * 128 : (q + 1) * 128] = block
    small[...] = jnp.zeros_like(small)
    for k in range(9):
        small[3 * k : 3 * k + 3, :] = out_weight[k].astype(F32)
    for k in range(4):
        kernel[:, k * 128 : (k + 1) * 128] = dot(windows[k], small[...].astype(BF16)).astype(BF16)


def gates(features, halo, before, after, weight, bias, out_weight, windows):
    return pl.pallas_call(
        gate_kernel,
        out_shape=(
            jax.ShapeDtypeStruct((33 * PITCH, 512), BF16),
            jax.ShapeDtypeStruct((1536, 256), BF16),
            jax.ShapeDtypeStruct((64, 512), BF16),
        ),
        scratch_shapes=[
            pltpu.VMEM((34, 56, 512), F32),
            pltpu.VMEM((34 * PITCH, 512), BF16),
            pltpu.VMEM((34 * PITCH, 512), BF16),
            pltpu.VMEM((1536, 256), BF16),
            pltpu.VMEM((32, 128), F32),
        ],
        compiler_params=pltpu.CompilerParams(vmem_limit_bytes=VMEM_LIMIT),
        cost_estimate=pl.CostEstimate(flops=5 * 10**9, bytes_accessed=4 * 10**6, transcendentals=2 * 10**6),
        name="gate",
    )(features, *halo, before, after, weight, bias, out_weight, windows)


def finish_kernel(parts, gate, back, kernel, spread, lines, out, pixels, edges, total, stacked, near, far):
    sums = parts[0].astype(F32)
    for source in range(1, 8):
        sums = sums + parts[source].astype(F32)
    total[...] = sums
    pixels[...] = jnp.zeros_like(pixels)
    edges[...] = jnp.zeros_like(edges)
    for channel in range(3):
        top = channel * 80
        half = total[channel * HALF_TILE : (channel + 1) * HALF_TILE, :] / PIXEL_STD[channel]
        pixels[top : top + HALF_TILE, :] = half
        pixels[top + HALF_TILE : top + 2 * HALF_TILE, :] = pltpu.roll(half, 64, 1)
        rest = total[3 * HALF_TILE :, :] / PIXEL_STD[channel]
        for block in range(7):
            turn = (64 - block * 12 - channel * 4) % SPAN
            edges[top + block * 10 : top + block * 10 + 10, :] = pltpu.roll(rest, turn, 1)
    rounded = jnp.where(iota((240, SPAN), 1) < 64, pixels[...], edges[...]).astype(BF16)
    picked = None
    for third in range(3):
        moved = dot(rounded, spread[third]).astype(BF16)
        term = dot(lines[third], moved)
        picked = term if picked is None else picked + term
    picked = picked.astype(BF16)
    for line in range(11):
        for k in range(4):
            stacked[line, k * 16 : k * 16 + 16, :] = picked[line * 16 : line * 16 + 16, k * SPAN : (k + 1) * SPAN]

    @pl.loop(0, 11)
    def _(line):
        act = dot(stacked[line], kernel[...], TN)
        for third in range(3):
            index = line * 3 + third
            scale = gate[pl.ds(pl.multiple_of(index * PITCH, PITCH), PITCH), :].astype(F32)
            grad = act[third * 40 : third * 40 + 40] * scale[0:40]
            start = pl.multiple_of(index * 32, 32)
            near[pl.ds(start, 32), :] = grad[0:32].astype(BF16)
            far[pl.ds(start, 32), :] = grad[1:33].astype(BF16)

    @pl.loop(0, 4)
    def _(chunk):
        found = []
        for p in range(2):
            pieces = []
            for a in range(3):
                step, parity = divmod(p + 2 - a, 2)
                start = pl.multiple_of(chunk * 256 + step * 32, 32)
                for source in (near, far):
                    pieces.append(source[pl.ds(start, 256), parity * 256 : (parity + 1) * 256])
            found.append(dot(jnp.concatenate(pieces, axis=1), back[...]))
        plus, minus = found[0] + found[1], found[0] - found[1]
        bands = [
            plus[:, :128] + plus[:, 128:],
            minus[:, :128] + minus[:, 128:],
            plus[:, :128] - plus[:, 128:],
            minus[:, :128] - minus[:, 128:],
        ]
        for k, band in enumerate(bands):
            out[pl.ds(pl.multiple_of(chunk * 8, 8), 8), :, k * 128 : (k + 1) * 128] = (
                (0.5 * band).astype(BF16).reshape(8, 32, 128)
            )


def window_picks():
    spread = np.zeros((3, SPAN, 512), np.float32)
    lines = np.zeros((3, 176, 240), np.float32)
    windows = np.zeros((4, 64, 32), np.float32)
    for third in range(3):
        for wx in range(4):
            for j in range(33):
                spread[third, 2 * j + wx, wx * SPAN + third * 40 + j] = 1
        for line in range(11):
            for channel in range(3):
                for wy in range(4):
                    y = 2 * (3 * line + third) + wy
                    lines[third, line * 16 + channel * 4 + wy, channel * 80 + y] = 1
    for py in range(2):
        for px in range(2):
            for wx in range(4):
                for channel in range(3):
                    for wy in range(4):
                        a, b = py + 2 - wy, px + 2 - wx
                        if 0 <= a <= 2 and 0 <= b <= 2:
                            windows[py * 2 + px, wx * 16 + channel * 4 + wy, a * 9 + b * 3 + channel] = 1
    return [jnp.asarray(each, BF16) for each in (spread, lines, windows)]


def finish(parts, gate, back, kernel, spread, lines):
    return pl.pallas_call(
        finish_kernel,
        out_shape=jax.ShapeDtypeStruct((32, 32, 512), BF16),
        scratch_shapes=[
            pltpu.VMEM((240, SPAN), F32),
            pltpu.VMEM((240, SPAN), F32),
            pltpu.VMEM((PACKED, SPAN), F32),
            pltpu.VMEM((11, 64, SPAN), BF16),
            pltpu.VMEM((33 * 32, 512), BF16),
            pltpu.VMEM((33 * 32, 512), BF16),
        ],
        compiler_params=pltpu.CompilerParams(vmem_limit_bytes=VMEM_LIMIT),
        name="finish",
    )(parts, gate, back, kernel, spread, lines)


SWAP = [(0, 1), (1, 0)]
ROW = ("zhi", "core")


def on_device(reward_grad, embed_weight, crop_offsets, features, conv_weight, conv_bias, out_weight):
    mine = lax.all_to_all(view_pairs(reward_grad), "tok", split_axis=0, concat_axis=0, tiled=True)
    other_weight = lax.ppermute(embed_weight, "core", SWAP)
    coarse = features[0]
    partner_top = lax.ppermute(coarse[:1], "core", SWAP)
    partner_bottom = lax.ppermute(coarse[31:], "core", SWAP)
    far_bottom = lax.ppermute(partner_bottom, ROW, [(0, 2)])
    far_top = lax.ppermute(partner_top, ROW, [(3, 1)])
    halo = (partner_top, partner_bottom, far_bottom, far_top)
    wide, cols, rows = placement_matrices(crop_offsets.T, embed_weight, other_weight)
    other = lax.ppermute(mine, "core", SWAP)
    partials = place_partials(mine, other, wide, cols, rows)
    parts = lax.all_to_all(partials, ("zhi", "seq"), split_axis=0, concat_axis=0, tiled=True)
    first, last = strips_of(coarse, *halo)
    before = lax.ppermute(last, "seq", [(i, i + 1) for i in range(3)])
    after = lax.ppermute(first, "seq", [(i + 1, i) for i in range(3)])
    spread, lines, windows = window_picks()
    small = out_weight.transpose(0, 1, 3, 2).reshape(9, 3, 128)
    gate, back, kernel = gates(coarse, halo, before, after, conv_weight, conv_bias[None], small, windows)
    return finish(parts, gate, back, kernel, spread, lines)[None]


def solution(mesh):
    split = Mesh(mesh.devices.reshape(16, 2, 2, 4), ("tok", "zhi", "core", "seq"))
    placed = (
        P(None, "tok", ("zhi", "core", "seq")),
        P(("zhi", "core", "seq"), None),
        P("tok", None),
        P("tok", ROW, "seq", None),
        P(),
        P(),
        P(),
    )
    return jax.shard_map(
        on_device,
        mesh=split,
        in_specs=placed,
        out_specs=P("tok", ROW, "seq", None),
        check_vma=False,
    )
```

```python
import jax
import jax.numpy as jnp
from jax import lax
from jax.experimental import pallas as pl
from jax.experimental.pallas import tpu as pltpu
from jax.sharding import Mesh
from jax.sharding import PartitionSpec as P

PIXEL_STD = (0.26862954, 0.26130258, 0.27577711)
BF16 = jnp.bfloat16
F32 = jnp.float32
VIEWS = 4
TILE_PIX = 68
SPAN = 128
HALF_TILE = 34
BAND = 80
PACKED = 112
PITCH = 48
NT = (((1,), (1,)), ((), ()))
TN = (((0,), (0,)), ((), ()))
VMEM_LIMIT = 16 * 2**20
IN_HBM = pl.BlockSpec(memory_space=pltpu.HBM)
IN_VMEM = pl.BlockSpec(memory_space=pltpu.VMEM)


def iota(shape, axis):
    return lax.broadcasted_iota(jnp.int32, shape, axis)


def dot(a, b, dims=(((1,), (0,)), ((), ()))):
    return lax.dot_general(a, b, dims, preferred_element_type=F32)


def fetch(semaphores, pairs):
    copies = [pltpu.make_async_copy(src, dst, semaphores.at[k]) for k, (src, dst) in enumerate(pairs)]
    for copy in copies:
        copy.start()
    return copies


def as_bf16(mask):
    return jnp.where(mask, 1.0, 0.0).astype(BF16)


def pair_kernel(reward, out):
    for pair in range(32):
        out[pair] = jnp.concatenate([reward[2 * pair], reward[2 * pair + 1]], axis=1)


def view_pairs(reward):
    return pl.pallas_call(
        pair_kernel,
        out_shape=jax.ShapeDtypeStruct((32, 16, SPAN), BF16),
        compiler_params=pltpu.CompilerParams(vmem_limit_bytes=VMEM_LIMIT),
        name="pairs",
    )(reward)


def prep_kernel(offsets, weight, other_weight, wide, cols, rows):
    pair = jnp.concatenate([weight[...], other_weight[...]], axis=0)
    slot = iota((704, 588), 0)
    pick = as_bf16(((slot >> 4) * 14 + (slot & 15) == iota((704, 588), 1)) & ((slot & 15) < 14))
    spread = dot(pick, pair, NT).astype(BF16).reshape(44, 16, SPAN)
    nothing = jnp.zeros((44, 16, SPAN), BF16)
    for group in range(4):
        for k in range(4):
            wide[:, group, :, k * SPAN : (k + 1) * SPAN] = spread if k == group else nothing
    slot, lane = iota((256, 512), 0), iota((256, 512), 1)
    gap = (lane >> 7) * 64 - 2 + (lane & 127) - (slot >> 4) * 14 - (slot & 15)
    gap = jnp.where(((slot & 15) < 14) & ((lane & 127) < TILE_PIX), gap, -1000)
    for view in range(VIEWS):
        cols[view] = as_bf16(gap == offsets[1, view])
    step, index = iota((BAND, 896), 0), iota((1, 896), 1)
    local, corner = index, jnp.zeros((1, 896), jnp.int32) + offsets[0, 0]
    for view in range(1, VIEWS):
        local = jnp.where(index >= 224 * view, index - 224 * view, local)
        corner = jnp.where(index >= 224 * view, offsets[0, view], corner)
    first = corner + 14 * (local & 15) + (local >> 4)
    core = lax.axis_index("core")
    for high in range(2):
        y = step + (64 * (2 * high + core) - 2)
        hit = as_bf16((y == first) & (step < TILE_PIX))
        rows[high * BAND : (high + 1) * BAND, :] = hit


def placement_matrices(offsets, weight, other_weight):
    return pl.pallas_call(
        prep_kernel,
        out_shape=(
            jax.ShapeDtypeStruct((44, 4, 16, 512), BF16),
            jax.ShapeDtypeStruct((VIEWS, 256, 512), BF16),
            jax.ShapeDtypeStruct((2 * BAND, 896), BF16),
        ),
        in_specs=[pl.BlockSpec(memory_space=pltpu.SMEM), IN_VMEM, IN_VMEM],
        compiler_params=pltpu.CompilerParams(vmem_limit_bytes=VMEM_LIMIT),
        name="prep",
    )(offsets, weight, other_weight)


def place_kernel(reward, other, wide, cols, rows, out, flat, left, strips, across, canvas, packed):
    own, theirs = [each[...].astype(F32).reshape(512, SPAN) for each in (reward, other)]
    low = iota((512, SPAN), 1) < 64
    flat[0] = jnp.where(low, own, pltpu.roll(theirs, 64, 1))
    flat[1] = jnp.where(low, pltpu.roll(own, 64, 1), theirs)
    for view in range(VIEWS):
        for patch in range(16):
            top = (patch // 4) * 64 + view * 16
            side = (patch % 4) * SPAN
            values = flat[view % 2, pl.ds((view // 2) * 16 + patch, 16, stride=32), :]
            left[top : top + 16, side : side + SPAN] = values.astype(BF16)
    low = iota((64, SPAN), 1) < 64
    for quad in range(11):
        part = dot(left[...], wide[4 * quad : 4 * quad + 4].reshape(256, 512), NT)
        for member in range(2):
            own = [part[64 * h : 64 * h + 64, member * SPAN : (member + 1) * SPAN] for h in range(4)]
            turned = [pltpu.roll(piece, 64, 1) for piece in own]
            for odd in range(2):
                start = (4 * quad + 2 * member + odd) * 16
                for side in range(2):
                    a, b = 2 * side, 2 * side + 1
                    if odd == 0:
                        joined = jnp.where(low, own[a], turned[b]).astype(BF16)
                    else:
                        joined = jnp.where(low, turned[a], own[b]).astype(BF16)
                    for view in range(VIEWS):
                        strips[view, start : start + 16, side * SPAN : (side + 1) * SPAN] = joined[
                            view * 16 : view * 16 + 16
                        ]
    for view in range(VIEWS):
        for channel in range(3):
            across[channel, view * 224 : (view + 1) * 224, :] = dot(
                strips[view, channel * 224 : (channel + 1) * 224, :], cols[view]
            ).astype(BF16)
    for channel in range(3):
        canvas[channel] = dot(rows[...], across[channel])
    lane = iota((HALF_TILE, SPAN), 1)
    wide_lane = iota((BAND, SPAN), 1)
    for high in range(2):
        for column in range(4):
            side = slice(column * SPAN, (column + 1) * SPAN)
            top = high * BAND
            for channel in range(3):
                upper = canvas[channel, top : top + HALF_TILE, side]
                lower = pltpu.roll(canvas[channel, top + HALF_TILE : top + 2 * HALF_TILE, side], 64, 1)
                packed[channel * HALF_TILE : (channel + 1) * HALF_TILE, :] = jnp.where(lane < 64, upper, lower)
            last = [canvas[channel, top : top + BAND, side] for channel in range(3)]
            joined = jnp.where(wide_lane < 68, last[0], pltpu.roll(last[1], 4, 1))
            joined = jnp.where(wide_lane < 72, joined, pltpu.roll(last[2], 8, 1))
            rest = None
            for block in range(7):
                piece = pltpu.roll(joined[block * 10 : block * 10 + 10], (64 + block * 12) % SPAN, 1)
                rest = piece if block == 0 else jnp.where(wide_lane[:10] < block * 12, rest, piece)
            packed[3 * HALF_TILE :, :] = rest
            out[high * 4 + column] = packed[...].astype(BF16)


def place_partials(reward, other, wide, cols, rows):
    return pl.pallas_call(
        place_kernel,
        out_shape=jax.ShapeDtypeStruct((8, PACKED, SPAN), BF16),
        scratch_shapes=[
            pltpu.VMEM((2, 512, SPAN), F32),
            pltpu.VMEM((256, 512), BF16),
            pltpu.VMEM((VIEWS, 704, 256), BF16),
            pltpu.VMEM((3, 896, 512), BF16),
            pltpu.VMEM((3, 2 * BAND, 512), F32),
            pltpu.VMEM((PACKED, SPAN), F32),
        ],
        compiler_params=pltpu.CompilerParams(vmem_limit_bytes=VMEM_LIMIT),
        name="place",
    )(reward, other, wide, cols, rows)


def strip_kernel(features_hbm, *refs):
    halo_hbm, (first, last), (features, halo, spread, semaphores) = refs[:4], refs[4:6], refs[6:]
    pairs = [(features_hbm, features)] + [(each, halo.at[k]) for k, each in enumerate(halo_hbm)]
    for copy in fetch(semaphores, pairs):
        copy.wait()
    above, below = halo_rows(halo)
    for out, side, row, corner in ((first, 0, 0, 0), (last, 16, 15, 31)):
        for k in range(4):
            lanes = slice(k * SPAN, (k + 1) * SPAN)
            spread[k] = features[:, side : side + 16, lanes].astype(F32).reshape(512, SPAN)
            edge = spread[k, pl.ds(row, 32, stride=16), :]
            ends = [above[corner : corner + 1, lanes], below[corner : corner + 1, lanes], jnp.zeros((14, SPAN), F32)]
            out[:, lanes] = jnp.concatenate([edge] + ends, axis=0).astype(BF16)


def halo_rows(halo):
    lower = lax.axis_index("core") == 1
    partner_top, partner_bottom, far_bottom, far_top = [halo[k, 0].astype(F32) for k in range(4)]
    return jnp.where(lower, partner_bottom, far_bottom), jnp.where(lower, far_top, partner_top)


def strips_of(features, *halo):
    return pl.pallas_call(
        strip_kernel,
        out_shape=[jax.ShapeDtypeStruct((48, 512), BF16)] * 2,
        in_specs=[IN_HBM] * 5,
        scratch_shapes=[
            pltpu.VMEM((32, 32, 512), BF16),
            pltpu.VMEM((4, 1, 32, 512), BF16),
            pltpu.VMEM((4, 512, SPAN), F32),
            pltpu.SemaphoreType.DMA((5,)),
        ],
        compiler_params=pltpu.CompilerParams(vmem_limit_bytes=VMEM_LIMIT),
        name="strips",
    )(features, *halo)


def inverse_haar(values):
    smooth, vertical, horizontal, diagonal = [values[:, k * 128 : (k + 1) * 128].astype(F32) for k in range(4)]
    upper_sum = smooth + vertical
    lower_sum = smooth - vertical
    upper_diff = horizontal + diagonal
    lower_diff = horizontal - diagonal
    return [
        0.5 * (upper_sum + upper_diff),
        0.5 * (upper_sum - upper_diff),
        0.5 * (lower_sum + lower_diff),
        0.5 * (lower_sum - lower_diff),
    ]


def gate_kernel(
    features_hbm, weight_hbm, top_hbm, bottom_hbm, far_bottom_hbm, far_top_hbm, before_hbm, after_hbm, bias, out_weight,
    out, back, kernel, features, weight, halo, sides, fine, near, far, taps, small, semaphores,
):
    high, core, column_tile = lax.axis_index("zhi"), lax.axis_index("core"), lax.axis_index("seq")
    lines = [(each, halo.at[k]) for k, each in enumerate((top_hbm, bottom_hbm, far_bottom_hbm, far_top_hbm))]
    columns = [(before_hbm, sides.at[0]), (after_hbm, sides.at[1])]
    copies = fetch(semaphores, [(features_hbm, features), (weight_hbm, weight)] + lines + columns)
    copies[0].wait()

    def put(line, values):
        for k, phase in enumerate(inverse_haar(values)):
            fine[line, 8:40, k * 128 : (k + 1) * 128] = phase

    @pl.loop(0, 32)
    def _(line):
        put(line + 1, features[line])

    for copy in copies[1:]:
        copy.wait()
    above, below = halo_rows(halo)
    put(0, above)
    put(33, below)
    for column, source in ((7, sides[0]), (40, sides[1])):
        for k, phase in enumerate(inverse_haar(source)):
            for line in range(34):
                row = 32 if line == 0 else 33 if line == 33 else line - 1
                fine[line, column : column + 1, k * 128 : (k + 1) * 128] = phase[row : row + 1]

    @pl.loop(0, 34)
    def _(line):
        start = pl.multiple_of(line * PITCH, PITCH)
        near[pl.ds(start, PITCH), :] = fine[line, 7:55, :].astype(BF16)
        far[pl.ds(start, PITCH), :] = fine[line, 8:56, :].astype(BF16)

    nothing = jnp.zeros((128, 128), BF16)
    for a in range(3):
        for u in range(4):
            start = (a * 4 + u) * 128
            taps[start : start + 128, 0:128] = weight[a, u] if u < 3 else nothing
            taps[start : start + 128, 128:] = weight[a, u - 1] if u > 0 else nothing
    wide_bias = jnp.concatenate([bias[...], bias[...]], axis=1)
    column, lane = iota((PITCH, 256), 0), iota((PITCH, 256), 1)
    outside = ((column_tile == 0) & (column == 0) & (lane < 128)) | ((column_tile == 3) & (column == 32) & (lane >= 128))
    inside = jnp.where(outside, 0.0, 1.0)[None]
    count = 11 * PITCH

    @pl.loop(0, 3)
    def _(chunk):
        for phase in range(2):
            pieces = []
            for a in range(3):
                lines, parity = divmod(phase + a, 2)
                start = pl.multiple_of(chunk * count + lines * PITCH, PITCH)
                for source in (near, far):
                    pieces.append(source[pl.ds(start, count), parity * 256 : (parity + 1) * 256])
            pre = dot(jnp.concatenate(pieces, axis=1), taps[...]) + wide_bias
            sigmoid = 1.0 / (1.0 + jnp.exp(-pre))
            slope = sigmoid * (1.0 + pre * (1.0 - sigmoid))
            slope = (slope.reshape(11, PITCH, 256) * inside).reshape(count, 256)
            here = pl.multiple_of(chunk * count, PITCH)
            out[pl.ds(here, count), phase * 256 : (phase + 1) * 256] = slope.astype(BF16)

    empty = jnp.zeros((PITCH, 256), BF16)

    @pl.when((high == 0) & (core == 0))
    def _():
        out[0:PITCH, 0:256] = empty

    @pl.when((high == 1) & (core == 1))
    def _():
        out[32 * PITCH : 33 * PITCH, 256:512] = empty


    for a in range(3):
        for u in range(4):
            start = (a * 4 + u) * 128
            for q in range(2):
                b = q + 2 - u
                block = weight[a, b].astype(F32).T.astype(BF16) if 0 <= b <= 2 else nothing
                back[start : start + 128, q * 128 : (q + 1) * 128] = block
    slot = iota((64, 32), 0)
    small[...] = jnp.zeros_like(small)
    for k in range(9):
        small[3 * k : 3 * k + 3, :] = out_weight[k].astype(F32)
    for k in range(4):
        a, b = k // 2 + 2 - (slot & 3), k % 2 + 2 - (slot >> 4)
        channel = (slot >> 2) & 3
        valid = (a >= 0) & (a <= 2) & (b >= 0) & (b <= 2) & (channel < 3)
        window = as_bf16((iota((64, 32), 1) == a * 9 + b * 3 + channel) & valid)
        kernel[:, k * 128 : (k + 1) * 128] = dot(window, small[...].astype(BF16)).astype(BF16)


def gates(features, weight, halo, before, after, bias, out_weight):
    return pl.pallas_call(
        gate_kernel,
        out_shape=(
            jax.ShapeDtypeStruct((33 * PITCH, 512), BF16),
            jax.ShapeDtypeStruct((1536, 256), BF16),
            jax.ShapeDtypeStruct((64, 512), BF16),
        ),
        in_specs=[IN_HBM] * 8 + [IN_VMEM] * 2,
        scratch_shapes=[
            pltpu.VMEM((32, 32, 512), BF16),
            pltpu.VMEM((3, 3, 128, 128), BF16),
            pltpu.VMEM((4, 1, 32, 512), BF16),
            pltpu.VMEM((2, 48, 512), BF16),
            pltpu.VMEM((34, 56, 512), F32),
            pltpu.VMEM((34 * PITCH, 512), BF16),
            pltpu.VMEM((34 * PITCH, 512), BF16),
            pltpu.VMEM((1536, 256), BF16),
            pltpu.VMEM((32, 128), F32),
            pltpu.SemaphoreType.DMA((8,)),
        ],
        compiler_params=pltpu.CompilerParams(vmem_limit_bytes=VMEM_LIMIT),
        cost_estimate=pl.CostEstimate(flops=5 * 10**9, bytes_accessed=4 * 10**6, transcendentals=2 * 10**6),
        name="gate",
    )(features, weight, *halo, before, after, bias, out_weight)


def finish_kernel(
    parts, gate_hbm, back_hbm, kernel_hbm, out, gate, back, kernel, pixels, edges, total, stacked, near, far, semaphores
):
    copies = fetch(semaphores, [(kernel_hbm, kernel), (gate_hbm, gate), (back_hbm, back)])
    sums = parts[0].astype(F32)
    for source in range(1, 8):
        sums = sums + parts[source].astype(F32)
    total[...] = sums
    pixels[...] = jnp.zeros_like(pixels)
    edges[...] = jnp.zeros_like(edges)
    for channel in range(3):
        top = channel * 80
        half = total[channel * HALF_TILE : (channel + 1) * HALF_TILE, :] / PIXEL_STD[channel]
        pixels[top : top + HALF_TILE, :] = half
        pixels[top + HALF_TILE : top + 2 * HALF_TILE, :] = pltpu.roll(half, 64, 1)
        rest = total[3 * HALF_TILE :, :] / PIXEL_STD[channel]
        for block in range(7):
            turn = (64 - block * 12 - channel * 4) % SPAN
            edges[top + block * 10 : top + block * 10 + 10, :] = pltpu.roll(rest, turn, 1)
    rounded = jnp.where(iota((240, SPAN), 1) < 64, pixels[...], edges[...]).astype(BF16)
    picked = None
    x, lane = iota((SPAN, 512), 0), iota((SPAN, 512), 1)
    row, y = iota((176, 240), 0), iota((176, 240), 1)
    for third in range(3):
        j = (lane & 127) - 40 * third
        spread = as_bf16((x == 2 * j + (lane >> 7)) & (j >= 0) & (j < 33))
        channel = (row >> 2) & 3
        lines = as_bf16((y == channel * 80 + 2 * (3 * (row >> 4) + third) + (row & 3)) & (channel < 3))
        moved = dot(rounded, spread).astype(BF16)
        term = dot(lines, moved)
        picked = term if picked is None else picked + term
    picked = picked.astype(BF16)
    for line in range(11):
        for k in range(4):
            stacked[line, k * 16 : k * 16 + 16, :] = picked[line * 16 : line * 16 + 16, k * SPAN : (k + 1) * SPAN]
    copies[0].wait()
    copies[1].wait()

    @pl.loop(0, 11)
    def _(line):
        act = dot(stacked[line], kernel[...], TN)
        for third in range(3):
            index = line * 3 + third
            scale = gate[pl.ds(pl.multiple_of(index * PITCH, PITCH), PITCH), :].astype(F32)
            grad = act[third * 40 : third * 40 + 40] * scale[0:40]
            start = pl.multiple_of(index * 32, 32)
            near[pl.ds(start, 32), :] = grad[0:32].astype(BF16)
            far[pl.ds(start, 32), :] = grad[1:33].astype(BF16)

    copies[2].wait()

    @pl.loop(0, 4)
    def _(chunk):
        found = []
        for p in range(2):
            pieces = []
            for a in range(3):
                step, parity = divmod(p + 2 - a, 2)
                start = pl.multiple_of(chunk * 256 + step * 32, 32)
                for source in (near, far):
                    pieces.append(source[pl.ds(start, 256), parity * 256 : (parity + 1) * 256])
            found.append(dot(jnp.concatenate(pieces, axis=1), back[...]))
        plus, minus = found[0] + found[1], found[0] - found[1]
        bands = [
            plus[:, :128] + plus[:, 128:],
            minus[:, :128] + minus[:, 128:],
            plus[:, :128] - plus[:, 128:],
            minus[:, :128] - minus[:, 128:],
        ]
        for k, band in enumerate(bands):
            out[pl.ds(pl.multiple_of(chunk * 8, 8), 8), :, k * 128 : (k + 1) * 128] = (
                (0.5 * band).astype(BF16).reshape(8, 32, 128)
            )


def finish(parts, gate, back, kernel):
    return pl.pallas_call(
        finish_kernel,
        out_shape=jax.ShapeDtypeStruct((32, 32, 512), BF16),
        in_specs=[IN_VMEM] + [IN_HBM] * 3,
        scratch_shapes=[
            pltpu.VMEM((33 * PITCH, 512), BF16),
            pltpu.VMEM((1536, 256), BF16),
            pltpu.VMEM((64, 512), BF16),
            pltpu.VMEM((240, SPAN), F32),
            pltpu.VMEM((240, SPAN), F32),
            pltpu.VMEM((PACKED, SPAN), F32),
            pltpu.VMEM((11, 64, SPAN), BF16),
            pltpu.VMEM((33 * 32, 512), BF16),
            pltpu.VMEM((33 * 32, 512), BF16),
            pltpu.SemaphoreType.DMA((3,)),
        ],
        compiler_params=pltpu.CompilerParams(vmem_limit_bytes=VMEM_LIMIT),
        name="finish",
    )(parts, gate, back, kernel)


SWAP = [(0, 1), (1, 0)]
ROW = ("zhi", "core")


def on_device(reward_grad, embed_weight, crop_offsets, features, conv_weight, conv_bias, out_weight):
    mine = lax.all_to_all(view_pairs(reward_grad), "tok", split_axis=0, concat_axis=0, tiled=True)
    other_weight = lax.ppermute(embed_weight, "core", SWAP)
    coarse = features[0]
    partner_top = lax.ppermute(coarse[:1], "core", SWAP)
    partner_bottom = lax.ppermute(coarse[31:], "core", SWAP)
    matrices = placement_matrices(crop_offsets.T, embed_weight, other_weight)
    mine, matrices, partner_top, partner_bottom = lax.optimization_barrier(
        (mine, matrices, partner_top, partner_bottom)
    )
    far_bottom = lax.ppermute(partner_bottom, ROW, [(0, 2)])
    far_top = lax.ppermute(partner_top, ROW, [(3, 1)])
    halo = (partner_top, partner_bottom, far_bottom, far_top)
    partials = place_partials(mine, lax.ppermute(mine, "core", SWAP), *matrices)
    partials, coarse = lax.optimization_barrier((partials, coarse))
    parts = lax.all_to_all(partials, ("zhi", "seq"), split_axis=0, concat_axis=0, tiled=True)
    first, last = strips_of(coarse, *halo)
    before = lax.ppermute(last, "seq", [(i, i + 1) for i in range(3)])
    after = lax.ppermute(first, "seq", [(i + 1, i) for i in range(3)])
    small = out_weight.transpose(0, 1, 3, 2).reshape(9, 3, 128)
    gate, back, kernel = gates(coarse, conv_weight, halo, before, after, conv_bias[None], small)
    return finish(parts, gate, back, kernel)[None]


def solution(mesh):
    split = Mesh(mesh.devices.reshape(16, 2, 2, 4), ("tok", "zhi", "core", "seq"))
    placed = (
        P(None, "tok", ("zhi", "core", "seq")),
        P(("zhi", "core", "seq"), None),
        P("tok", None),
        P("tok", ROW, "seq", None),
        P(),
        P(),
        P(),
    )
    return jax.shard_map(
        on_device,
        mesh=split,
        in_specs=placed,
        out_specs=P("tok", ROW, "seq", None),
        check_vma=False,
    )
```

```python
import jax
import jax.numpy as jnp
from jax import lax
from jax.experimental import pallas as pl
from jax.experimental.pallas import tpu as pltpu
from jax.sharding import Mesh
from jax.sharding import PartitionSpec as P

PIXEL_STD = (0.26862954, 0.26130258, 0.27577711)
BF16 = jnp.bfloat16
F32 = jnp.float32
VIEWS = 4
TILE_PIX = 68
SPAN = 128
HALF_TILE = 34
BAND = 80
PACKED = 112
PITCH = 48
NT = (((1,), (1,)), ((), ()))
TN = (((0,), (0,)), ((), ()))
VMEM_LIMIT = 16 * 2**20
IN_HBM = pl.BlockSpec(memory_space=pltpu.HBM)
IN_VMEM = pl.BlockSpec(memory_space=pltpu.VMEM)


def iota(shape, axis):
    return lax.broadcasted_iota(jnp.int32, shape, axis)


def dot(a, b, dims=(((1,), (0,)), ((), ()))):
    return lax.dot_general(a, b, dims, preferred_element_type=F32)


def fetch(semaphores, pairs):
    copies = [pltpu.make_async_copy(src, dst, semaphores.at[k]) for k, (src, dst) in enumerate(pairs)]
    for copy in copies:
        copy.start()
    return copies


def as_bf16(mask):
    return jnp.where(mask, 1.0, 0.0).astype(BF16)


def pair_kernel(reward, out):
    for pair in range(32):
        out[pair] = jnp.concatenate([reward[2 * pair], reward[2 * pair + 1]], axis=1)


def view_pairs(reward):
    return pl.pallas_call(
        pair_kernel,
        out_shape=jax.ShapeDtypeStruct((32, 16, SPAN), BF16),
        compiler_params=pltpu.CompilerParams(vmem_limit_bytes=VMEM_LIMIT),
        name="pairs",
    )(reward)


def prep_kernel(offsets, weight, other_weight, wide, rows):
    pair = jnp.concatenate([weight[...], other_weight[...]], axis=0)
    slot = iota((704, 588), 0)
    pick = as_bf16(((slot >> 4) * 14 + (slot & 15) == iota((704, 588), 1)) & ((slot & 15) < 14))
    spread = dot(pick, pair, NT).astype(BF16).reshape(44, 16, SPAN)
    nothing = jnp.zeros((44, 16, SPAN), BF16)
    for group in range(4):
        for k in range(4):
            wide[:, group, :, k * SPAN : (k + 1) * SPAN] = spread if k == group else nothing
    step, index = iota((BAND, 896), 0), iota((1, 896), 1)
    local, corner = index, jnp.zeros((1, 896), jnp.int32) + offsets[0, 0]
    for view in range(1, VIEWS):
        local = jnp.where(index >= 224 * view, index - 224 * view, local)
        corner = jnp.where(index >= 224 * view, offsets[0, view], corner)
    first = corner + 14 * (local & 15) + (local >> 4)
    core = lax.axis_index("core")
    for high in range(2):
        y = step + (64 * (2 * high + core) - 2)
        hit = as_bf16((y == first) & (step < TILE_PIX))
        rows[high * BAND : (high + 1) * BAND, :] = hit


def placement_matrices(offsets, weight, other_weight):
    return pl.pallas_call(
        prep_kernel,
        out_shape=(
            jax.ShapeDtypeStruct((44, 4, 16, 512), BF16),
            jax.ShapeDtypeStruct((2 * BAND, 896), BF16),
        ),
        in_specs=[pl.BlockSpec(memory_space=pltpu.SMEM), IN_VMEM, IN_VMEM],
        compiler_params=pltpu.CompilerParams(vmem_limit_bytes=VMEM_LIMIT),
        name="prep",
    )(offsets, weight, other_weight)


def place_kernel(offsets, reward, other, wide, rows, out, flat, left, strips, across, canvas, packed):
    own, theirs = [each[...].astype(F32).reshape(512, SPAN) for each in (reward, other)]
    low = iota((512, SPAN), 1) < 64
    flat[0] = jnp.where(low, own, pltpu.roll(theirs, 64, 1))
    flat[1] = jnp.where(low, pltpu.roll(own, 64, 1), theirs)
    for view in range(VIEWS):
        for patch in range(16):
            top = (patch // 4) * 64 + view * 16
            side = (patch % 4) * SPAN
            values = flat[view % 2, pl.ds((view // 2) * 16 + patch, 16, stride=32), :]
            left[top : top + 16, side : side + SPAN] = values.astype(BF16)
    low = iota((64, SPAN), 1) < 64
    for quad in range(11):
        part = dot(left[...], wide[4 * quad : 4 * quad + 4].reshape(256, 512), NT)
        for member in range(2):
            own = [part[64 * h : 64 * h + 64, member * SPAN : (member + 1) * SPAN] for h in range(4)]
            turned = [pltpu.roll(piece, 64, 1) for piece in own]
            for odd in range(2):
                start = (4 * quad + 2 * member + odd) * 16
                for side in range(2):
                    a, b = 2 * side, 2 * side + 1
                    if odd == 0:
                        joined = jnp.where(low, own[a], turned[b]).astype(BF16)
                    else:
                        joined = jnp.where(low, turned[a], own[b]).astype(BF16)
                    for view in range(VIEWS):
                        strips[view, start : start + 16, side * SPAN : (side + 1) * SPAN] = joined[
                            view * 16 : view * 16 + 16
                        ]
    slot, lane = iota((256, 512), 0), iota((256, 512), 1)
    gap = (lane >> 7) * 64 - 2 + (lane & 127) - (slot >> 4) * 14 - (slot & 15)
    gap = jnp.where(((slot & 15) < 14) & ((lane & 127) < TILE_PIX), gap, -1000)
    for view in range(VIEWS):
        cols = as_bf16(gap == offsets[1, view])
        for channel in range(3):
            across[channel, view * 224 : (view + 1) * 224, :] = dot(
                strips[view, channel * 224 : (channel + 1) * 224, :], cols
            ).astype(BF16)
    for channel in range(3):
        canvas[channel] = dot(rows[...], across[channel])
    lane = iota((HALF_TILE, SPAN), 1)
    wide_lane = iota((BAND, SPAN), 1)
    for high in range(2):
        for column in range(4):
            side = slice(column * SPAN, (column + 1) * SPAN)
            top = high * BAND
            for channel in range(3):
                upper = canvas[channel, top : top + HALF_TILE, side]
                lower = pltpu.roll(canvas[channel, top + HALF_TILE : top + 2 * HALF_TILE, side], 64, 1)
                packed[channel * HALF_TILE : (channel + 1) * HALF_TILE, :] = jnp.where(lane < 64, upper, lower)
            last = [canvas[channel, top : top + BAND, side] for channel in range(3)]
            joined = jnp.where(wide_lane < 68, last[0], pltpu.roll(last[1], 4, 1))
            joined = jnp.where(wide_lane < 72, joined, pltpu.roll(last[2], 8, 1))
            rest = None
            for block in range(7):
                piece = pltpu.roll(joined[block * 10 : block * 10 + 10], (64 + block * 12) % SPAN, 1)
                rest = piece if block == 0 else jnp.where(wide_lane[:10] < block * 12, rest, piece)
            packed[3 * HALF_TILE :, :] = rest
            out[high * 4 + column] = packed[...].astype(BF16)


def place_partials(offsets, reward, other, wide, rows):
    return pl.pallas_call(
        place_kernel,
        out_shape=jax.ShapeDtypeStruct((8, PACKED, SPAN), BF16),
        in_specs=[pl.BlockSpec(memory_space=pltpu.SMEM)] + [IN_VMEM] * 4,
        scratch_shapes=[
            pltpu.VMEM((2, 512, SPAN), F32),
            pltpu.VMEM((256, 512), BF16),
            pltpu.VMEM((VIEWS, 704, 256), BF16),
            pltpu.VMEM((3, 896, 512), BF16),
            pltpu.VMEM((3, 2 * BAND, 512), F32),
            pltpu.VMEM((PACKED, SPAN), F32),
        ],
        compiler_params=pltpu.CompilerParams(vmem_limit_bytes=VMEM_LIMIT),
        name="place",
    )(offsets, reward, other, wide, rows)


def edge_kernel(features_hbm, partner_top, partner_bottom, out, features, spread, semaphores):
    high, core, column = lax.axis_index("zhi"), lax.axis_index("core"), lax.axis_index("seq")
    fetched = fetch(semaphores, [(features_hbm, features)])
    top, bottom = partner_top[0].astype(F32), partner_bottom[0].astype(F32)
    far = jnp.where(core == 0, bottom, top)
    out[(1 - high) * 4 + column, 0:32, :] = far.astype(BF16)
    fetched[0].wait()
    for step, side, row, corner in ((-1, 0, 0, 0), (1, 16, 15, 31)):
        there = jnp.clip(column + step, 0, 3)

        @pl.when(there != column)
        def _():
            for k in range(4):
                lanes = slice(k * SPAN, (k + 1) * SPAN)
                spread[k] = features[:, side : side + 16, lanes].astype(F32).reshape(512, SPAN)
                edge = spread[k, pl.ds(row, 32, stride=16), :]
                ends = [
                    bottom[corner : corner + 1, lanes],
                    top[corner : corner + 1, lanes],
                    jnp.zeros((6, SPAN), F32),
                ]
                out[high * 4 + there, :, lanes] = jnp.concatenate([edge] + ends, axis=0).astype(BF16)
            out[(1 - high) * 4 + there, 0:8, :] = jnp.broadcast_to(far[corner : corner + 1], (8, 512)).astype(BF16)


def edge_slots(features, partner_top, partner_bottom):
    return pl.pallas_call(
        edge_kernel,
        out_shape=jax.ShapeDtypeStruct((8, 40, 512), BF16),
        in_specs=[IN_HBM, IN_VMEM, IN_VMEM],
        scratch_shapes=[
            pltpu.VMEM((32, 32, 512), BF16),
            pltpu.VMEM((4, 512, SPAN), F32),
            pltpu.SemaphoreType.DMA((1,)),
        ],
        compiler_params=pltpu.CompilerParams(vmem_limit_bytes=VMEM_LIMIT),
        name="edges",
    )(features, partner_top, partner_bottom)


def inverse_haar(values):
    smooth, vertical, horizontal, diagonal = [values[:, k * 128 : (k + 1) * 128].astype(F32) for k in range(4)]
    upper_sum = smooth + vertical
    lower_sum = smooth - vertical
    upper_diff = horizontal + diagonal
    lower_diff = horizontal - diagonal
    return [
        0.5 * (upper_sum + upper_diff),
        0.5 * (upper_sum - upper_diff),
        0.5 * (lower_sum + lower_diff),
        0.5 * (lower_sum - lower_diff),
    ]


def gate_kernel(
    features_hbm, weight_hbm, top_hbm, bottom_hbm, slots_hbm, bias, out_weight,
    out, back, kernel, features, weight, rows, slots, fine, near, far, taps, small, semaphores,
):
    high, core, column_tile = lax.axis_index("zhi"), lax.axis_index("core"), lax.axis_index("seq")
    lines = [(top_hbm, rows.at[0]), (bottom_hbm, rows.at[1])]
    copies = fetch(semaphores, [(features_hbm, features), (weight_hbm, weight), (slots_hbm, slots)] + lines)
    copies[0].wait()

    def put(line, values):
        for k, phase in enumerate(inverse_haar(values)):
            fine[line, 8:40, k * 128 : (k + 1) * 128] = phase

    @pl.loop(0, 32)
    def _(line):
        put(line + 1, features[line])

    for copy in copies[1:]:
        copy.wait()
    other = (1 - high) * 4
    distant = slots[other + column_tile, 0:32, :].astype(F32)
    put(0, jnp.where(core == 1, rows[1, 0].astype(F32), jnp.where(high == 1, distant, 0.0)))
    put(33, jnp.where(core == 0, rows[0, 0].astype(F32), jnp.where(high == 0, distant, 0.0)))
    for column, step in ((7, -1), (40, 1)):
        there = jnp.clip(column_tile + step, 0, 3)
        side = slots[high * 4 + there].astype(F32)
        corner = slots[other + there, 0:8, :].astype(F32)[0:1]
        top = jnp.where(core == 1, side[32:33], jnp.where(high == 1, corner, 0.0))
        bottom = jnp.where(core == 0, side[33:34], jnp.where(high == 0, corner, 0.0))
        joined = jnp.concatenate([side[0:32], top, bottom, jnp.zeros((6, 512), F32)], axis=0)
        for k, phase in enumerate(inverse_haar(jnp.where(there == column_tile, 0.0, joined))):
            for line in range(34):
                row = 32 if line == 0 else 33 if line == 33 else line - 1
                fine[line, column : column + 1, k * 128 : (k + 1) * 128] = phase[row : row + 1]

    @pl.loop(0, 34)
    def _(line):
        start = pl.multiple_of(line * PITCH, PITCH)
        near[pl.ds(start, PITCH), :] = fine[line, 7:55, :].astype(BF16)
        far[pl.ds(start, PITCH), :] = fine[line, 8:56, :].astype(BF16)

    nothing = jnp.zeros((128, 128), BF16)
    for a in range(3):
        for u in range(4):
            start = (a * 4 + u) * 128
            taps[start : start + 128, 0:128] = weight[a, u] if u < 3 else nothing
            taps[start : start + 128, 128:] = weight[a, u - 1] if u > 0 else nothing
    wide_bias = jnp.concatenate([bias[...], bias[...]], axis=1)
    column, lane = iota((PITCH, 256), 0), iota((PITCH, 256), 1)
    outside = ((column_tile == 0) & (column == 0) & (lane < 128)) | ((column_tile == 3) & (column == 32) & (lane >= 128))
    inside = jnp.where(outside, 0.0, 1.0)[None]
    count = 11 * PITCH

    @pl.loop(0, 3)
    def _(chunk):
        for phase in range(2):
            pieces = []
            for a in range(3):
                lines, parity = divmod(phase + a, 2)
                start = pl.multiple_of(chunk * count + lines * PITCH, PITCH)
                for source in (near, far):
                    pieces.append(source[pl.ds(start, count), parity * 256 : (parity + 1) * 256])
            pre = dot(jnp.concatenate(pieces, axis=1), taps[...]) + wide_bias
            sigmoid = 1.0 / (1.0 + jnp.exp(-pre))
            slope = sigmoid * (1.0 + pre * (1.0 - sigmoid))
            slope = (slope.reshape(11, PITCH, 256) * inside).reshape(count, 256)
            here = pl.multiple_of(chunk * count, PITCH)
            out[pl.ds(here, count), phase * 256 : (phase + 1) * 256] = slope.astype(BF16)

    empty = jnp.zeros((PITCH, 256), BF16)

    @pl.when((high == 0) & (core == 0))
    def _():
        out[0:PITCH, 0:256] = empty

    @pl.when((high == 1) & (core == 1))
    def _():
        out[32 * PITCH : 33 * PITCH, 256:512] = empty


    for a in range(3):
        for u in range(4):
            start = (a * 4 + u) * 128
            for q in range(2):
                b = q + 2 - u
                block = weight[a, b].astype(F32).T.astype(BF16) if 0 <= b <= 2 else nothing
                back[start : start + 128, q * 128 : (q + 1) * 128] = block
    slot = iota((64, 32), 0)
    small[...] = jnp.zeros_like(small)
    for k in range(9):
        small[3 * k : 3 * k + 3, :] = out_weight[k].astype(F32)
    for k in range(4):
        a, b = k // 2 + 2 - (slot & 3), k % 2 + 2 - (slot >> 4)
        channel = (slot >> 2) & 3
        valid = (a >= 0) & (a <= 2) & (b >= 0) & (b <= 2) & (channel < 3)
        window = as_bf16((iota((64, 32), 1) == a * 9 + b * 3 + channel) & valid)
        kernel[:, k * 128 : (k + 1) * 128] = dot(window, small[...].astype(BF16)).astype(BF16)


def gates(features, weight, partner_top, partner_bottom, slots, bias, out_weight):
    return pl.pallas_call(
        gate_kernel,
        out_shape=(
            jax.ShapeDtypeStruct((33 * PITCH, 512), BF16),
            jax.ShapeDtypeStruct((1536, 256), BF16),
            jax.ShapeDtypeStruct((64, 512), BF16),
        ),
        in_specs=[IN_HBM] * 5 + [IN_VMEM] * 2,
        scratch_shapes=[
            pltpu.VMEM((32, 32, 512), BF16),
            pltpu.VMEM((3, 3, 128, 128), BF16),
            pltpu.VMEM((2, 1, 32, 512), BF16),
            pltpu.VMEM((8, 40, 512), BF16),
            pltpu.VMEM((34, 56, 512), F32),
            pltpu.VMEM((34 * PITCH, 512), BF16),
            pltpu.VMEM((34 * PITCH, 512), BF16),
            pltpu.VMEM((1536, 256), BF16),
            pltpu.VMEM((32, 128), F32),
            pltpu.SemaphoreType.DMA((5,)),
        ],
        compiler_params=pltpu.CompilerParams(vmem_limit_bytes=VMEM_LIMIT),
        cost_estimate=pl.CostEstimate(flops=5 * 10**9, bytes_accessed=4 * 10**6, transcendentals=2 * 10**6),
        name="gate",
    )(features, weight, partner_top, partner_bottom, slots, bias, out_weight)


def finish_kernel(
    parts, gate_hbm, back_hbm, kernel_hbm, out, gate, back, kernel, pixels, edges, total, stacked, near, far, semaphores
):
    copies = fetch(semaphores, [(kernel_hbm, kernel), (gate_hbm, gate), (back_hbm, back)])
    sums = parts[0].astype(F32)
    for source in range(1, 8):
        sums = sums + parts[source].astype(F32)
    total[...] = sums
    pixels[...] = jnp.zeros_like(pixels)
    edges[...] = jnp.zeros_like(edges)
    for channel in range(3):
        top = channel * 80
        half = total[channel * HALF_TILE : (channel + 1) * HALF_TILE, :] / PIXEL_STD[channel]
        pixels[top : top + HALF_TILE, :] = half
        pixels[top + HALF_TILE : top + 2 * HALF_TILE, :] = pltpu.roll(half, 64, 1)
        rest = total[3 * HALF_TILE :, :] / PIXEL_STD[channel]
        for block in range(7):
            turn = (64 - block * 12 - channel * 4) % SPAN
            edges[top + block * 10 : top + block * 10 + 10, :] = pltpu.roll(rest, turn, 1)
    rounded = jnp.where(iota((240, SPAN), 1) < 64, pixels[...], edges[...]).astype(BF16)
    picked = None
    x, lane = iota((SPAN, 512), 0), iota((SPAN, 512), 1)
    row, y = iota((176, 240), 0), iota((176, 240), 1)
    for third in range(3):
        j = (lane & 127) - 40 * third
        spread = as_bf16((x == 2 * j + (lane >> 7)) & (j >= 0) & (j < 33))
        channel = (row >> 2) & 3
        lines = as_bf16((y == channel * 80 + 2 * (3 * (row >> 4) + third) + (row & 3)) & (channel < 3))
        moved = dot(rounded, spread).astype(BF16)
        term = dot(lines, moved)
        picked = term if picked is None else picked + term
    picked = picked.astype(BF16)
    for line in range(11):
        for k in range(4):
            stacked[line, k * 16 : k * 16 + 16, :] = picked[line * 16 : line * 16 + 16, k * SPAN : (k + 1) * SPAN]
    copies[0].wait()
    copies[1].wait()

    @pl.loop(0, 11)
    def _(line):
        act = dot(stacked[line], kernel[...], TN)
        for third in range(3):
            index = line * 3 + third
            scale = gate[pl.ds(pl.multiple_of(index * PITCH, PITCH), PITCH), :].astype(F32)
            grad = act[third * 40 : third * 40 + 40] * scale[0:40]
            start = pl.multiple_of(index * 32, 32)
            near[pl.ds(start, 32), :] = grad[0:32].astype(BF16)
            far[pl.ds(start, 32), :] = grad[1:33].astype(BF16)

    copies[2].wait()

    @pl.loop(0, 4)
    def _(chunk):
        found = []
        for p in range(2):
            pieces = []
            for a in range(3):
                step, parity = divmod(p + 2 - a, 2)
                start = pl.multiple_of(chunk * 256 + step * 32, 32)
                for source in (near, far):
                    pieces.append(source[pl.ds(start, 256), parity * 256 : (parity + 1) * 256])
            found.append(dot(jnp.concatenate(pieces, axis=1), back[...]))
        plus, minus = found[0] + found[1], found[0] - found[1]
        bands = [
            plus[:, :128] + plus[:, 128:],
            minus[:, :128] + minus[:, 128:],
            plus[:, :128] - plus[:, 128:],
            minus[:, :128] - minus[:, 128:],
        ]
        for k, band in enumerate(bands):
            out[pl.ds(pl.multiple_of(chunk * 8, 8), 8), :, k * 128 : (k + 1) * 128] = (
                (0.5 * band).astype(BF16).reshape(8, 32, 128)
            )


def finish(parts, gate, back, kernel):
    return pl.pallas_call(
        finish_kernel,
        out_shape=jax.ShapeDtypeStruct((32, 32, 512), BF16),
        in_specs=[IN_VMEM] + [IN_HBM] * 3,
        scratch_shapes=[
            pltpu.VMEM((33 * PITCH, 512), BF16),
            pltpu.VMEM((1536, 256), BF16),
            pltpu.VMEM((64, 512), BF16),
            pltpu.VMEM((240, SPAN), F32),
            pltpu.VMEM((240, SPAN), F32),
            pltpu.VMEM((PACKED, SPAN), F32),
            pltpu.VMEM((11, 64, SPAN), BF16),
            pltpu.VMEM((33 * 32, 512), BF16),
            pltpu.VMEM((33 * 32, 512), BF16),
            pltpu.SemaphoreType.DMA((3,)),
        ],
        compiler_params=pltpu.CompilerParams(vmem_limit_bytes=VMEM_LIMIT),
        name="finish",
    )(parts, gate, back, kernel)


SWAP = [(0, 1), (1, 0)]
ROW = ("zhi", "core")


def on_device(reward_grad, embed_weight, crop_offsets, features, conv_weight, conv_bias, out_weight):
    mine = lax.all_to_all(view_pairs(reward_grad), "tok", split_axis=0, concat_axis=0, tiled=True)
    other_weight = lax.ppermute(embed_weight, "core", SWAP)
    coarse = features[0]
    partner_top = lax.ppermute(coarse[:1], "core", SWAP)
    partner_bottom = lax.ppermute(coarse[31:], "core", SWAP)
    offsets = crop_offsets.T
    matrices = placement_matrices(offsets, embed_weight, other_weight)
    slots = edge_slots(coarse, partner_top, partner_bottom)
    slots = lax.all_to_all(slots, ("zhi", "seq"), split_axis=0, concat_axis=0, tiled=True)
    mine, matrices = lax.optimization_barrier((mine, matrices))
    partials = place_partials(offsets, mine, lax.ppermute(mine, "core", SWAP), *matrices)
    parts = lax.all_to_all(partials, ("zhi", "seq"), split_axis=0, concat_axis=0, tiled=True)
    small = out_weight.transpose(0, 1, 3, 2).reshape(9, 3, 128)
    gate, back, kernel = gates(coarse, conv_weight, partner_top, partner_bottom, slots, conv_bias[None], small)
    return finish(parts, gate, back, kernel)[None]


def solution(mesh):
    split = Mesh(mesh.devices.reshape(16, 2, 2, 4), ("tok", "zhi", "core", "seq"))
    placed = (
        P(None, "tok", ("zhi", "core", "seq")),
        P(("zhi", "core", "seq"), None),
        P("tok", None),
        P("tok", ROW, "seq", None),
        P(),
        P(),
        P(),
    )
    return jax.shard_map(
        on_device,
        mesh=split,
        in_specs=placed,
        out_specs=P("tok", ROW, "seq", None),
        check_vma=False,
    )
```

```python
import jax
import jax.numpy as jnp
from jax import lax
from jax.experimental import pallas as pl
from jax.experimental.pallas import tpu as pltpu
from jax.sharding import Mesh
from jax.sharding import PartitionSpec as P

PIXEL_STD = (0.26862954, 0.26130258, 0.27577711)
BF16 = jnp.bfloat16
F32 = jnp.float32
VIEWS = 4
TILE_PIX = 68
SPAN = 128
HALF_TILE = 34
BAND = 80
PACKED = 112
HALO = 144
PITCH = 48
NT = (((1,), (1,)), ((), ()))
TN = (((0,), (0,)), ((), ()))
VMEM_LIMIT = 16 * 2**20
IN_HBM = pl.BlockSpec(memory_space=pltpu.HBM)
IN_VMEM = pl.BlockSpec(memory_space=pltpu.VMEM)


def iota(shape, axis):
    return lax.broadcasted_iota(jnp.int32, shape, axis)


def dot(a, b, dims=(((1,), (0,)), ((), ()))):
    return lax.dot_general(a, b, dims, preferred_element_type=F32)


def fetch(semaphores, pairs):
    copies = [pltpu.make_async_copy(src, dst, semaphores.at[k]) for k, (src, dst) in enumerate(pairs)]
    for copy in copies:
        copy.start()
    return copies


def as_bf16(mask):
    return jnp.where(mask, 1.0, 0.0).astype(BF16)


def pair_kernel(reward, out):
    for pair in range(32):
        out[pair] = jnp.concatenate([reward[2 * pair], reward[2 * pair + 1]], axis=1)


def view_pairs(reward):
    return pl.pallas_call(
        pair_kernel,
        out_shape=jax.ShapeDtypeStruct((32, 16, SPAN), BF16),
        compiler_params=pltpu.CompilerParams(vmem_limit_bytes=VMEM_LIMIT),
        name="pairs",
    )(reward)


def prep_kernel(weight, other_weight, wide):
    pair = jnp.concatenate([weight[...], other_weight[...]], axis=0)
    slot = iota((704, 588), 0)
    pick = as_bf16(((slot >> 4) * 14 + (slot & 15) == iota((704, 588), 1)) & ((slot & 15) < 14))
    spread = dot(pick, pair, NT).astype(BF16).reshape(44, 16, SPAN)
    nothing = jnp.zeros((44, 16, SPAN), BF16)
    for group in range(4):
        for k in range(4):
            wide[:, group, :, k * SPAN : (k + 1) * SPAN] = spread if k == group else nothing


def spread_weight(weight, other_weight):
    return pl.pallas_call(
        prep_kernel,
        out_shape=jax.ShapeDtypeStruct((44, 4, 16, 512), BF16),
        compiler_params=pltpu.CompilerParams(vmem_limit_bytes=VMEM_LIMIT),
        name="prep",
    )(weight, other_weight)


def place_kernel(offsets, reward, other, wide, halo, out, flat, left, strips, across, canvas, packed, rows):
    own, theirs = [each[...].astype(F32).reshape(512, SPAN) for each in (reward, other)]
    low = iota((512, SPAN), 1) < 64
    flat[0] = jnp.where(low, own, pltpu.roll(theirs, 64, 1))
    flat[1] = jnp.where(low, pltpu.roll(own, 64, 1), theirs)
    for view in range(VIEWS):
        for patch in range(16):
            top = (patch // 4) * 64 + view * 16
            side = (patch % 4) * SPAN
            values = flat[view % 2, pl.ds((view // 2) * 16 + patch, 16, stride=32), :]
            left[top : top + 16, side : side + SPAN] = values.astype(BF16)
    low = iota((64, SPAN), 1) < 64
    for quad in range(11):
        part = dot(left[...], wide[4 * quad : 4 * quad + 4].reshape(256, 512), NT)
        for member in range(2):
            own = [part[64 * h : 64 * h + 64, member * SPAN : (member + 1) * SPAN] for h in range(4)]
            turned = [pltpu.roll(piece, 64, 1) for piece in own]
            for odd in range(2):
                start = (4 * quad + 2 * member + odd) * 16
                for side in range(2):
                    a, b = 2 * side, 2 * side + 1
                    if odd == 0:
                        joined = jnp.where(low, own[a], turned[b]).astype(BF16)
                    else:
                        joined = jnp.where(low, turned[a], own[b]).astype(BF16)
                    for view in range(VIEWS):
                        strips[view, start : start + 16, side * SPAN : (side + 1) * SPAN] = joined[
                            view * 16 : view * 16 + 16
                        ]
    slot, lane = iota((256, 512), 0), iota((256, 512), 1)
    gap = (lane >> 7) * 64 - 2 + (lane & 127) - (slot >> 4) * 14 - (slot & 15)
    gap = jnp.where(((slot & 15) < 14) & ((lane & 127) < TILE_PIX), gap, -1000)
    for view in range(VIEWS):
        cols = as_bf16(gap == offsets[1, view])
        for channel in range(3):
            across[channel, view * 224 : (view + 1) * 224, :] = dot(
                strips[view, channel * 224 : (channel + 1) * 224, :], cols
            ).astype(BF16)
    step, index = iota((BAND, 896), 0), iota((1, 896), 1)
    local, corner = index, jnp.zeros((1, 896), jnp.int32) + offsets[0, 0]
    for view in range(1, VIEWS):
        local = jnp.where(index >= 224 * view, index - 224 * view, local)
        corner = jnp.where(index >= 224 * view, offsets[0, view], corner)
    first = corner + 14 * (local & 15) + (local >> 4)
    core = lax.axis_index("core")
    for high in range(2):
        y = step + (64 * (2 * high + core) - 2)
        hit = as_bf16((y == first) & (step < TILE_PIX))
        rows[high * BAND : (high + 1) * BAND, :] = hit
    for channel in range(3):
        canvas[channel] = dot(rows[...], across[channel])
    lane = iota((HALF_TILE, SPAN), 1)
    wide_lane = iota((BAND, SPAN), 1)
    for high in range(2):
        for column in range(4):
            side = slice(column * SPAN, (column + 1) * SPAN)
            top = high * BAND
            for channel in range(3):
                upper = canvas[channel, top : top + HALF_TILE, side]
                lower = pltpu.roll(canvas[channel, top + HALF_TILE : top + 2 * HALF_TILE, side], 64, 1)
                packed[channel * HALF_TILE : (channel + 1) * HALF_TILE, :] = jnp.where(lane < 64, upper, lower)
            last = [canvas[channel, top : top + BAND, side] for channel in range(3)]
            joined = jnp.where(wide_lane < 68, last[0], pltpu.roll(last[1], 4, 1))
            joined = jnp.where(wide_lane < 72, joined, pltpu.roll(last[2], 8, 1))
            rest = None
            for block in range(7):
                piece = pltpu.roll(joined[block * 10 : block * 10 + 10], (64 + block * 12) % SPAN, 1)
                rest = piece if block == 0 else jnp.where(wide_lane[:10] < block * 12, rest, piece)
            packed[3 * HALF_TILE :, :] = rest
            out[high * 4 + column, 0:PACKED, :] = packed[...].astype(BF16)
            out[high * 4 + column, PACKED:, :] = halo[high * 4 + column]


def place_partials(offsets, reward, other, wide, halo):
    return pl.pallas_call(
        place_kernel,
        out_shape=jax.ShapeDtypeStruct((8, PACKED + HALO, SPAN), BF16),
        in_specs=[pl.BlockSpec(memory_space=pltpu.SMEM)] + [IN_VMEM] * 4,
        scratch_shapes=[
            pltpu.VMEM((2, 512, SPAN), F32),
            pltpu.VMEM((256, 512), BF16),
            pltpu.VMEM((VIEWS, 704, 256), BF16),
            pltpu.VMEM((3, 896, 512), BF16),
            pltpu.VMEM((3, 2 * BAND, 512), F32),
            pltpu.VMEM((PACKED, SPAN), F32),
            pltpu.VMEM((2 * BAND, 896), BF16),
        ],
        compiler_params=pltpu.CompilerParams(vmem_limit_bytes=VMEM_LIMIT),
        name="place",
    )(offsets, reward, other, wide, halo)


def edge_kernel(features_hbm, partner_top, partner_bottom, out, own, features, spread, semaphores):
    high, core, column = lax.axis_index("zhi"), lax.axis_index("core"), lax.axis_index("seq")
    fetched = fetch(semaphores, [(features_hbm, features)])
    own[4] = partner_top[0]
    own[5] = partner_bottom[0]
    top, bottom = partner_top[0].astype(F32), partner_bottom[0].astype(F32)
    far = jnp.where(core == 0, bottom, top)
    nothing = jnp.zeros((8, SPAN), F32)

    def put(slot, values):
        for k in range(4):
            out[slot, 32 * k : 32 * k + 32, :] = values[:, k * SPAN : (k + 1) * SPAN].astype(BF16)

    def put_ends(slot, above, below):
        rows = [each[:, k * SPAN : (k + 1) * SPAN] for k in range(4) for each in (above, below)]
        out[slot, 128:144, :] = jnp.concatenate(rows + [nothing], axis=0).astype(BF16)

    put((1 - high) * 4 + column, far)
    fetched[0].wait()
    own[0] = features[0]
    own[1] = features[31]
    for index, (step, side, row, end) in enumerate(((-1, 0, 0, 0), (1, 16, 15, 31))):
        parts = []
        for k in range(4):
            lanes = slice(k * SPAN, (k + 1) * SPAN)
            spread[k] = features[:, side : side + 16, lanes].astype(F32).reshape(512, SPAN)
            parts.append(spread[k, pl.ds(row, 32, stride=16), :])
        edge = jnp.concatenate(parts, axis=1)
        own[2 + index] = edge.astype(BF16)
        there = jnp.clip(column + step, 0, 3)

        @pl.when(there != column)
        def _():
            put(high * 4 + there, edge)
            put_ends(high * 4 + there, bottom[end : end + 1], top[end : end + 1])
            put_ends((1 - high) * 4 + there, far[end : end + 1], far[end : end + 1])


def edge_slots(features, partner_top, partner_bottom):
    return pl.pallas_call(
        edge_kernel,
        out_shape=(jax.ShapeDtypeStruct((8, HALO, SPAN), BF16), jax.ShapeDtypeStruct((6, 32, 512), BF16)),
        in_specs=[IN_HBM, IN_VMEM, IN_VMEM],
        scratch_shapes=[
            pltpu.VMEM((32, 32, 512), BF16),
            pltpu.VMEM((4, 512, SPAN), F32),
            pltpu.SemaphoreType.DMA((1,)),
        ],
        compiler_params=pltpu.CompilerParams(vmem_limit_bytes=VMEM_LIMIT),
        name="edges",
    )(features, partner_top, partner_bottom)


def inverse_haar(values):
    smooth, vertical, horizontal, diagonal = [values[:, k * 128 : (k + 1) * 128].astype(F32) for k in range(4)]
    upper_sum = smooth + vertical
    lower_sum = smooth - vertical
    upper_diff = horizontal + diagonal
    lower_diff = horizontal - diagonal
    return [
        0.5 * (upper_sum + upper_diff),
        0.5 * (upper_sum - upper_diff),
        0.5 * (lower_sum + lower_diff),
        0.5 * (lower_sum - lower_diff),
    ]


def slope_of(pre):
    sigmoid = 0.5 + 0.5 * jnp.tanh(0.5 * pre)
    return sigmoid * (1.0 + pre * (1.0 - sigmoid))


def gate_kernel(
    features_hbm, weight_hbm, bias, out_weight,
    out, back, kernel, taps, features, weight, fine, near, far, small, semaphores,
):
    copies = fetch(semaphores, [(features_hbm, features), (weight_hbm, weight)])
    copies[0].wait()

    @pl.loop(0, 32, unroll=4)
    def _(line):
        for k, phase in enumerate(inverse_haar(features[line])):
            fine[line + 1, 8:40, k * 128 : (k + 1) * 128] = phase

    copies[1].wait()

    @pl.loop(0, 34, unroll=2)
    def _(line):
        start = pl.multiple_of(line * PITCH, PITCH)
        near[pl.ds(start, PITCH), :] = fine[line, 7:55, :].astype(BF16)
        far[pl.ds(start, PITCH), :] = fine[line, 8:56, :].astype(BF16)

    nothing = jnp.zeros((128, 128), BF16)
    for a in range(3):
        for u in range(4):
            start = (a * 4 + u) * 128
            taps[start : start + 128, 0:128] = weight[a, u] if u < 3 else nothing
            taps[start : start + 128, 128:] = weight[a, u - 1] if u > 0 else nothing
    wide_bias = jnp.concatenate([bias[...], bias[...]], axis=1)
    count = 11 * PITCH
    for chunk in range(3):
        for phase in range(2):
            pieces = []
            for a in range(3):
                lines, parity = divmod(phase + a, 2)
                start = chunk * count + lines * PITCH
                for source in (near, far):
                    pieces.append(source[start : start + count, parity * 256 : (parity + 1) * 256])
            slope = slope_of(dot(jnp.concatenate(pieces, axis=1), taps[...]) + wide_bias)
            here = chunk * count
            out[here : here + count, phase * 256 : (phase + 1) * 256] = slope.astype(BF16)
    for a in range(3):
        for u in range(4):
            start = (a * 4 + u) * 128
            for q in range(2):
                b = q + 2 - u
                block = weight[a, b].astype(F32).T.astype(BF16) if 0 <= b <= 2 else nothing
                back[start : start + 128, q * 128 : (q + 1) * 128] = block
    slot = iota((64, 32), 0)
    small[...] = jnp.zeros_like(small)
    for k in range(9):
        small[3 * k : 3 * k + 3, :] = out_weight[k].astype(F32)
    for k in range(4):
        a, b = k // 2 + 2 - (slot & 3), k % 2 + 2 - (slot >> 4)
        channel = (slot >> 2) & 3
        valid = (a >= 0) & (a <= 2) & (b >= 0) & (b <= 2) & (channel < 3)
        window = as_bf16((iota((64, 32), 1) == a * 9 + b * 3 + channel) & valid)
        kernel[:, k * 128 : (k + 1) * 128] = dot(window, small[...].astype(BF16)).astype(BF16)


def gates(features, weight, bias, out_weight):
    return pl.pallas_call(
        gate_kernel,
        out_shape=(
            jax.ShapeDtypeStruct((33 * PITCH, 512), BF16),
            jax.ShapeDtypeStruct((1536, 256), BF16),
            jax.ShapeDtypeStruct((64, 512), BF16),
            jax.ShapeDtypeStruct((1536, 256), BF16),
        ),
        in_specs=[IN_HBM] * 2 + [IN_VMEM] * 2,
        scratch_shapes=[
            pltpu.VMEM((32, 32, 512), BF16),
            pltpu.VMEM((3, 3, 128, 128), BF16),
            pltpu.VMEM((34, 56, 512), F32),
            pltpu.VMEM((34 * PITCH, 512), BF16),
            pltpu.VMEM((34 * PITCH, 512), BF16),
            pltpu.VMEM((32, 128), F32),
            pltpu.SemaphoreType.DMA((2,)),
        ],
        compiler_params=pltpu.CompilerParams(vmem_limit_bytes=VMEM_LIMIT),
        cost_estimate=pl.CostEstimate(flops=5 * 10**9, bytes_accessed=4 * 10**6, transcendentals=2 * 10**6),
        name="gate",
    )(features, weight, bias, out_weight)


def ring_gates(parts, own, bias, taps, strips):
    high, core, column = lax.axis_index("zhi"), lax.axis_index("core"), lax.axis_index("seq")
    other = (1 - high) * 4

    def halo(slot):
        return jnp.concatenate(
            [parts[slot, PACKED + 32 * k : PACKED + 32 * k + 32, :] for k in range(4)], axis=1
        ).astype(F32)

    def ends(slot):
        rows = parts[slot, PACKED + 128 :, :].astype(F32)
        return [jnp.concatenate([rows[2 * k + e : 2 * k + e + 1] for k in range(4)], axis=1) for e in range(2)]

    def only(condition, values):
        return jnp.where(condition, values, 0.0)

    lines = [own[k].astype(F32) for k in range(6)]
    distant = halo(other + column)
    above = jnp.where(core == 1, lines[5], only(high == 1, distant))
    below = jnp.where(core == 0, lines[4], only(high == 0, distant))
    sides, corners = [], []
    for step in (-1, 1):
        there = jnp.clip(column + step, 0, 3)
        inside = there != column
        sides.append(only(inside, halo(high * 4 + there)))
        near_ends, far_ends = ends(high * 4 + there), ends(other + there)
        corners.append(
            [
                only(inside, jnp.where(core == 1, near_ends[0], only(high == 1, far_ends[0]))),
                only(inside, jnp.where(core == 0, near_ends[1], only(high == 0, far_ends[1]))),
            ]
        )
    put = [
        (above, corners[0][0], corners[1][0]),
        (lines[0], sides[0][0:1], sides[1][0:1]),
        (lines[1], sides[0][31:32], sides[1][31:32]),
        (below, corners[0][1], corners[1][1]),
        (sides[0], corners[0][0], corners[0][1]),
        (lines[2], above[0:1], below[0:1]),
        (lines[3], above[31:32], below[31:32]),
        (sides[1], corners[1][0], corners[1][1]),
    ]
    for k, (middle, first, last) in enumerate(put):
        strips[k, 0:8, :] = jnp.zeros((8, 512), F32)
        strips[k, 40:56, :] = jnp.zeros((16, 512), F32)
        for at, values in ((8, middle), (7, first), (40, last)):
            for q, phase in enumerate(inverse_haar(values)):
                strips[k, at : at + values.shape[0], q * 128 : (q + 1) * 128] = phase
    shifted = [[strips[k, 7 + d : 55 + d, :].astype(BF16) for d in range(2)] for k in range(8)]
    wide_bias = jnp.concatenate([bias[...], bias[...]], axis=1)
    found = []
    for phase in range(2):
        stack = []
        for strip in range(4):
            pieces = []
            for a in range(3):
                step, parity = divmod(phase + a, 2)
                for turn in range(2):
                    if strip < 2:
                        source = shifted[2 * strip + step][turn]
                    else:
                        source = shifted[2 * strip + turn][step]
                    pieces.append(source[:, parity * 256 : (parity + 1) * 256])
            stack.append(jnp.concatenate(pieces, axis=1))
        found.append(slope_of(dot(jnp.concatenate(stack, axis=0), taps[...]) + wide_bias))
    rings = [
        jnp.concatenate([each[strip * PITCH : (strip + 1) * PITCH] for each in found], axis=1) for strip in range(4)
    ]
    at, lane = iota((PITCH, 512), 0), iota((PITCH, 512), 1)
    even, upper = (lane & 255) < 128, lane < 256
    left = (column == 0) & even
    right = (column == 3) & jnp.logical_not(even)
    beside = (left & (at == 0)) | (right & (at == 32))
    first_line = (high == 0) & (core == 0) & upper
    last_line = (high == 1) & (core == 1) & jnp.logical_not(upper)
    masks = [beside | first_line, beside | last_line, left, right]
    return [jnp.where(mask, 0.0, ring) for mask, ring in zip(masks, rings)]


def finish_kernel(
    parts, gate_hbm, back_hbm, kernel_hbm, taps_hbm, own_hbm, bias_hbm,
    out, gate, back, kernel, taps, own, bias, strips, columns, pixels, edges, total, stacked, near, far, semaphores,
):
    pairs = [(own_hbm, own), (bias_hbm, bias), (taps_hbm, taps), (kernel_hbm, kernel), (gate_hbm, gate), (back_hbm, back)]
    copies = fetch(semaphores, pairs)
    sums = parts[0, 0:PACKED, :].astype(F32)
    for source in range(1, 8):
        sums = sums + parts[source, 0:PACKED, :].astype(F32)
    total[...] = sums
    pixels[...] = jnp.zeros_like(pixels)
    edges[...] = jnp.zeros_like(edges)
    for channel in range(3):
        top = channel * 80
        half = total[channel * HALF_TILE : (channel + 1) * HALF_TILE, :] / PIXEL_STD[channel]
        pixels[top : top + HALF_TILE, :] = half
        pixels[top + HALF_TILE : top + 2 * HALF_TILE, :] = pltpu.roll(half, 64, 1)
        rest = total[3 * HALF_TILE :, :] / PIXEL_STD[channel]
        for block in range(7):
            turn = (64 - block * 12 - channel * 4) % SPAN
            edges[top + block * 10 : top + block * 10 + 10, :] = pltpu.roll(rest, turn, 1)
    rounded = jnp.where(iota((240, SPAN), 1) < 64, pixels[...], edges[...]).astype(BF16)
    picked = None
    x, lane = iota((SPAN, 512), 0), iota((SPAN, 512), 1)
    row, y = iota((176, 240), 0), iota((176, 240), 1)
    for third in range(3):
        j = (lane & 127) - 40 * third
        spread = as_bf16((x == 2 * j + (lane >> 7)) & (j >= 0) & (j < 33))
        channel = (row >> 2) & 3
        lines = as_bf16((y == channel * 80 + 2 * (3 * (row >> 4) + third) + (row & 3)) & (channel < 3))
        moved = dot(rounded, spread).astype(BF16)
        term = dot(lines, moved)
        picked = term if picked is None else picked + term
    picked = picked.astype(BF16)
    for line in range(11):
        for k in range(4):
            stacked[line, k * 16 : k * 16 + 16, :] = picked[line * 16 : line * 16 + 16, k * SPAN : (k + 1) * SPAN]
    for copy in copies[:4]:
        copy.wait()
    rings = ring_gates(parts, own, bias, taps, strips)
    columns[0] = rings[2]
    columns[1] = rings[3]
    copies[4].wait()
    at = iota((PITCH, 512), 0)
    for line in range(11):
        act = dot(stacked[line], kernel[...], TN)
        for third in range(3):
            index = line * 3 + third
            if index == 0:
                scale = rings[0]
            elif index == 32:
                scale = rings[1]
            else:
                scale = gate[index * PITCH : (index + 1) * PITCH, :].astype(F32)
                scale = jnp.where(at == 0, columns[0, index : index + 1, :], scale)
                scale = jnp.where(at == 32, columns[1, index : index + 1, :], scale)
            grad = act[third * 40 : third * 40 + 40] * scale[0:40]
            near[index * 32 : (index + 1) * 32, :] = grad[0:32].astype(BF16)
            far[index * 32 : (index + 1) * 32, :] = grad[1:33].astype(BF16)
    copies[5].wait()
    for chunk in range(4):
        stack = []
        for p in range(2):
            pieces = []
            for a in range(3):
                step, parity = divmod(p + 2 - a, 2)
                start = chunk * 256 + step * 32
                for source in (near, far):
                    pieces.append(source[start : start + 256, parity * 256 : (parity + 1) * 256])
            stack.append(jnp.concatenate(pieces, axis=1))
        found = dot(jnp.concatenate(stack, axis=0), back[...])
        plus, minus = found[:256] + found[256:], found[:256] - found[256:]
        bands = [
            plus[:, :128] + plus[:, 128:],
            minus[:, :128] + minus[:, 128:],
            plus[:, :128] - plus[:, 128:],
            minus[:, :128] - minus[:, 128:],
        ]
        for k, band in enumerate(bands):
            out[chunk * 8 : chunk * 8 + 8, :, k * 128 : (k + 1) * 128] = (0.5 * band).astype(BF16).reshape(8, 32, 128)


def finish(parts, gate, back, kernel, taps, own, bias):
    return pl.pallas_call(
        finish_kernel,
        out_shape=jax.ShapeDtypeStruct((32, 32, 512), BF16),
        in_specs=[IN_VMEM] + [IN_HBM] * 6,
        scratch_shapes=[
            pltpu.VMEM((33 * PITCH, 512), BF16),
            pltpu.VMEM((1536, 256), BF16),
            pltpu.VMEM((64, 512), BF16),
            pltpu.VMEM((1536, 256), BF16),
            pltpu.VMEM((6, 32, 512), BF16),
            pltpu.VMEM((1, 128), F32),
            pltpu.VMEM((8, 56, 512), F32),
            pltpu.VMEM((2, PITCH, 512), F32),
            pltpu.VMEM((240, SPAN), F32),
            pltpu.VMEM((240, SPAN), F32),
            pltpu.VMEM((PACKED, SPAN), F32),
            pltpu.VMEM((11, 64, SPAN), BF16),
            pltpu.VMEM((33 * 32, 512), BF16),
            pltpu.VMEM((33 * 32, 512), BF16),
            pltpu.SemaphoreType.DMA((6,)),
        ],
        compiler_params=pltpu.CompilerParams(vmem_limit_bytes=VMEM_LIMIT),
        name="finish",
    )(parts, gate, back, kernel, taps, own, bias)


SWAP = [(0, 1), (1, 0)]
ROW = ("zhi", "core")


def on_device(reward_grad, embed_weight, crop_offsets, features, conv_weight, conv_bias, out_weight):
    mine = lax.all_to_all(view_pairs(reward_grad), "tok", split_axis=0, concat_axis=0, tiled=True)
    other_weight = lax.ppermute(embed_weight, "core", SWAP)
    coarse = features[0]
    partner_top = lax.ppermute(coarse[:1], "core", SWAP)
    partner_bottom = lax.ppermute(coarse[31:], "core", SWAP)
    offsets = crop_offsets.T
    wide = spread_weight(embed_weight, other_weight)
    halo, own = edge_slots(coarse, partner_top, partner_bottom)
    mine, wide, halo = lax.optimization_barrier((mine, wide, halo))
    partials = place_partials(offsets, mine, lax.ppermute(mine, "core", SWAP), wide, halo)
    partials, coarse = lax.optimization_barrier((partials, coarse))
    parts = lax.all_to_all(partials, ("zhi", "seq"), split_axis=0, concat_axis=0, tiled=True)
    small = out_weight.transpose(0, 1, 3, 2).reshape(9, 3, 128)
    bias = conv_bias[None]
    gate, back, kernel, taps = gates(coarse, conv_weight, bias, small)
    return finish(parts, gate, back, kernel, taps, own, bias)[None]


def solution(mesh):
    split = Mesh(mesh.devices.reshape(16, 2, 2, 4), ("tok", "zhi", "core", "seq"))
    placed = (
        P(None, "tok", ("zhi", "core", "seq")),
        P(("zhi", "core", "seq"), None),
        P("tok", None),
        P("tok", ROW, "seq", None),
        P(),
        P(),
        P(),
    )
    return jax.shard_map(
        on_device,
        mesh=split,
        in_specs=placed,
        out_specs=P("tok", ROW, "seq", None),
        check_vma=False,
    )
```

```python
import jax
import jax.numpy as jnp
from jax import lax
from jax.experimental import pallas as pl
from jax.experimental.pallas import tpu as pltpu
from jax.sharding import Mesh
from jax.sharding import PartitionSpec as P

PIXEL_STD = (0.26862954, 0.26130258, 0.27577711)
BF16 = jnp.bfloat16
F32 = jnp.float32
VIEWS = 4
TILE_PIX = 68
SPAN = 128
HALF_TILE = 34
BAND = 80
PACKED = 112
HALO = 144
PITCH = 48
NT = (((1,), (1,)), ((), ()))
TN = (((0,), (0,)), ((), ()))
VMEM_LIMIT = 16 * 2**20
IN_HBM = pl.BlockSpec(memory_space=pltpu.HBM)
IN_VMEM = pl.BlockSpec(memory_space=pltpu.VMEM)


def iota(shape, axis):
    return lax.broadcasted_iota(jnp.int32, shape, axis)


def dot(a, b, dims=(((1,), (0,)), ((), ()))):
    return lax.dot_general(a, b, dims, preferred_element_type=F32)


def fetch(semaphores, pairs):
    copies = [pltpu.make_async_copy(src, dst, semaphores.at[k]) for k, (src, dst) in enumerate(pairs)]
    for copy in copies:
        copy.start()
    return copies


def as_bf16(mask):
    return jnp.where(mask, 1.0, 0.0).astype(BF16)


def pair_kernel(reward, out):
    for pair in range(32):
        out[pair] = jnp.concatenate([reward[2 * pair], reward[2 * pair + 1]], axis=1)


def view_pairs(reward):
    return pl.pallas_call(
        pair_kernel,
        out_shape=jax.ShapeDtypeStruct((32, 16, SPAN), BF16),
        compiler_params=pltpu.CompilerParams(vmem_limit_bytes=VMEM_LIMIT),
        name="pairs",
    )(reward)


def prep_kernel(weight, other_weight, wide):
    pair = jnp.concatenate([weight[...], other_weight[...]], axis=0)
    slot = iota((704, 588), 0)
    pick = as_bf16(((slot >> 4) * 14 + (slot & 15) == iota((704, 588), 1)) & ((slot & 15) < 14))
    spread = dot(pick, pair, NT).astype(BF16).reshape(44, 16, SPAN)
    nothing = jnp.zeros((44, 16, SPAN), BF16)
    for group in range(4):
        for k in range(4):
            wide[:, group, :, k * SPAN : (k + 1) * SPAN] = spread if k == group else nothing


def spread_weight(weight, other_weight):
    return pl.pallas_call(
        prep_kernel,
        out_shape=jax.ShapeDtypeStruct((44, 4, 16, 512), BF16),
        compiler_params=pltpu.CompilerParams(vmem_limit_bytes=VMEM_LIMIT),
        name="prep",
    )(weight, other_weight)


def place_kernel(offsets, reward, other, wide, halo, out, flat, left, strips, across, canvas, packed, rows):
    own, theirs = [each[...].astype(F32).reshape(512, SPAN) for each in (reward, other)]
    low = iota((512, SPAN), 1) < 64
    flat[0] = jnp.where(low, own, pltpu.roll(theirs, 64, 1))
    flat[1] = jnp.where(low, pltpu.roll(own, 64, 1), theirs)
    for view in range(VIEWS):
        for patch in range(16):
            top = (patch // 4) * 64 + view * 16
            side = (patch % 4) * SPAN
            values = flat[view % 2, pl.ds((view // 2) * 16 + patch, 16, stride=32), :]
            left[top : top + 16, side : side + SPAN] = values.astype(BF16)
    low = iota((64, SPAN), 1) < 64
    for quad in range(11):
        part = dot(left[...], wide[4 * quad : 4 * quad + 4].reshape(256, 512), NT)
        for member in range(2):
            own = [part[64 * h : 64 * h + 64, member * SPAN : (member + 1) * SPAN] for h in range(4)]
            turned = [pltpu.roll(piece, 64, 1) for piece in own]
            for odd in range(2):
                start = (4 * quad + 2 * member + odd) * 16
                for side in range(2):
                    a, b = 2 * side, 2 * side + 1
                    if odd == 0:
                        joined = jnp.where(low, own[a], turned[b]).astype(BF16)
                    else:
                        joined = jnp.where(low, turned[a], own[b]).astype(BF16)
                    for view in range(VIEWS):
                        strips[view, start : start + 16, side * SPAN : (side + 1) * SPAN] = joined[
                            view * 16 : view * 16 + 16
                        ]
    slot, lane = iota((256, 512), 0), iota((256, 512), 1)
    gap = (lane >> 7) * 64 - 2 + (lane & 127) - (slot >> 4) * 14 - (slot & 15)
    gap = jnp.where(((slot & 15) < 14) & ((lane & 127) < TILE_PIX), gap, -1000)
    for view in range(VIEWS):
        cols = as_bf16(gap == offsets[1, view])
        for channel in range(3):
            across[channel, view * 224 : (view + 1) * 224, :] = dot(
                strips[view, channel * 224 : (channel + 1) * 224, :], cols
            ).astype(BF16)
    step, index = iota((BAND, 896), 0), iota((1, 896), 1)
    local, corner = index, jnp.zeros((1, 896), jnp.int32) + offsets[0, 0]
    for view in range(1, VIEWS):
        local = jnp.where(index >= 224 * view, index - 224 * view, local)
        corner = jnp.where(index >= 224 * view, offsets[0, view], corner)
    first = corner + 14 * (local & 15) + (local >> 4)
    core = lax.axis_index("core")
    for high in range(2):
        y = step + (64 * (2 * high + core) - 2)
        hit = as_bf16((y == first) & (step < TILE_PIX))
        rows[high * BAND : (high + 1) * BAND, :] = hit
    for channel in range(3):
        canvas[channel] = dot(rows[...], across[channel])
    lane = iota((HALF_TILE, SPAN), 1)
    wide_lane = iota((BAND, SPAN), 1)
    for high in range(2):
        for column in range(4):
            side = slice(column * SPAN, (column + 1) * SPAN)
            top = high * BAND
            for channel in range(3):
                upper = canvas[channel, top : top + HALF_TILE, side]
                lower = pltpu.roll(canvas[channel, top + HALF_TILE : top + 2 * HALF_TILE, side], 64, 1)
                packed[channel * HALF_TILE : (channel + 1) * HALF_TILE, :] = jnp.where(lane < 64, upper, lower)
            last = [canvas[channel, top : top + BAND, side] for channel in range(3)]
            joined = jnp.where(wide_lane < 68, last[0], pltpu.roll(last[1], 4, 1))
            joined = jnp.where(wide_lane < 72, joined, pltpu.roll(last[2], 8, 1))
            rest = None
            for block in range(7):
                piece = pltpu.roll(joined[block * 10 : block * 10 + 10], (64 + block * 12) % SPAN, 1)
                rest = piece if block == 0 else jnp.where(wide_lane[:10] < block * 12, rest, piece)
            packed[3 * HALF_TILE :, :] = rest
            out[high * 4 + column, 0:PACKED, :] = packed[...].astype(BF16)
            out[high * 4 + column, PACKED:, :] = halo[high * 4 + column]


def place_partials(offsets, reward, other, wide, halo):
    return pl.pallas_call(
        place_kernel,
        out_shape=jax.ShapeDtypeStruct((8, PACKED + HALO, SPAN), BF16),
        in_specs=[pl.BlockSpec(memory_space=pltpu.SMEM)] + [IN_VMEM] * 4,
        scratch_shapes=[
            pltpu.VMEM((2, 512, SPAN), F32),
            pltpu.VMEM((256, 512), BF16),
            pltpu.VMEM((VIEWS, 704, 256), BF16),
            pltpu.VMEM((3, 896, 512), BF16),
            pltpu.VMEM((3, 2 * BAND, 512), F32),
            pltpu.VMEM((PACKED, SPAN), F32),
            pltpu.VMEM((2 * BAND, 896), BF16),
        ],
        compiler_params=pltpu.CompilerParams(vmem_limit_bytes=VMEM_LIMIT),
        name="place",
    )(offsets, reward, other, wide, halo)


def edge_kernel(features_hbm, partner_top, partner_bottom, out, own, features, spread, semaphores):
    high, core, column = lax.axis_index("zhi"), lax.axis_index("core"), lax.axis_index("seq")
    fetched = fetch(semaphores, [(features_hbm, features)])
    own[4] = partner_top[0]
    own[5] = partner_bottom[0]
    top, bottom = partner_top[0].astype(F32), partner_bottom[0].astype(F32)
    far = jnp.where(core == 0, bottom, top)
    nothing = jnp.zeros((8, SPAN), F32)

    def put(slot, values):
        for k in range(4):
            out[slot, 32 * k : 32 * k + 32, :] = values[:, k * SPAN : (k + 1) * SPAN].astype(BF16)

    def put_ends(slot, above, below):
        rows = [each[:, k * SPAN : (k + 1) * SPAN] for k in range(4) for each in (above, below)]
        out[slot, 128:144, :] = jnp.concatenate(rows + [nothing], axis=0).astype(BF16)

    put((1 - high) * 4 + column, far)
    fetched[0].wait()
    own[0] = features[0]
    own[1] = features[31]
    for index, (step, side, row, end) in enumerate(((-1, 0, 0, 0), (1, 16, 15, 31))):
        parts = []
        for k in range(4):
            lanes = slice(k * SPAN, (k + 1) * SPAN)
            spread[k] = features[:, side : side + 16, lanes].astype(F32).reshape(512, SPAN)
            parts.append(spread[k, pl.ds(row, 32, stride=16), :])
        edge = jnp.concatenate(parts, axis=1)
        own[2 + index] = edge.astype(BF16)
        there = jnp.clip(column + step, 0, 3)

        @pl.when(there != column)
        def _():
            put(high * 4 + there, edge)
            put_ends(high * 4 + there, bottom[end : end + 1], top[end : end + 1])
            put_ends((1 - high) * 4 + there, far[end : end + 1], far[end : end + 1])


def edge_slots(features, partner_top, partner_bottom):
    return pl.pallas_call(
        edge_kernel,
        out_shape=(jax.ShapeDtypeStruct((8, HALO, SPAN), BF16), jax.ShapeDtypeStruct((6, 32, 512), BF16)),
        in_specs=[IN_HBM, IN_VMEM, IN_VMEM],
        scratch_shapes=[
            pltpu.VMEM((32, 32, 512), BF16),
            pltpu.VMEM((4, 512, SPAN), F32),
            pltpu.SemaphoreType.DMA((1,)),
        ],
        compiler_params=pltpu.CompilerParams(vmem_limit_bytes=VMEM_LIMIT),
        name="edges",
    )(features, partner_top, partner_bottom)


def inverse_haar(values):
    smooth, vertical, horizontal, diagonal = [values[:, k * 128 : (k + 1) * 128].astype(F32) for k in range(4)]
    upper_sum = smooth + vertical
    lower_sum = smooth - vertical
    upper_diff = horizontal + diagonal
    lower_diff = horizontal - diagonal
    return [
        0.5 * (upper_sum + upper_diff),
        0.5 * (upper_sum - upper_diff),
        0.5 * (lower_sum + lower_diff),
        0.5 * (lower_sum - lower_diff),
    ]


def slope_of(pre):
    sigmoid = 0.5 + 0.5 * jnp.tanh(0.5 * pre)
    return sigmoid * (1.0 + pre * (1.0 - sigmoid))


def gate_kernel(
    features_hbm, weight_hbm, bias, out_weight,
    out, back, kernel, taps, features, weight, fine, near, far, small, semaphores,
):
    copies = fetch(semaphores, [(features_hbm, features), (weight_hbm, weight)])
    copies[0].wait()

    @pl.loop(0, 32, unroll=4)
    def _(line):
        for k, phase in enumerate(inverse_haar(features[line])):
            fine[line + 1, 8:40, k * 128 : (k + 1) * 128] = phase

    copies[1].wait()

    @pl.loop(0, 34, unroll=2)
    def _(line):
        start = pl.multiple_of(line * PITCH, PITCH)
        near[pl.ds(start, PITCH), :] = fine[line, 7:55, :].astype(BF16)
        far[pl.ds(start, PITCH), :] = fine[line, 8:56, :].astype(BF16)

    nothing = jnp.zeros((128, 128), BF16)
    for a in range(3):
        for u in range(4):
            start = (a * 4 + u) * 128
            taps[start : start + 128, 0:128] = weight[a, u] if u < 3 else nothing
            taps[start : start + 128, 128:] = weight[a, u - 1] if u > 0 else nothing
    wide_bias = jnp.concatenate([bias[...], bias[...]], axis=1)
    count = 11 * PITCH
    for chunk in range(3):
        for phase in range(2):
            pieces = []
            for a in range(3):
                lines, parity = divmod(phase + a, 2)
                start = chunk * count + lines * PITCH
                for source in (near, far):
                    pieces.append(source[start : start + count, parity * 256 : (parity + 1) * 256])
            slope = slope_of(dot(jnp.concatenate(pieces, axis=1), taps[...]) + wide_bias)
            here = chunk * count
            out[here : here + count, phase * 256 : (phase + 1) * 256] = slope.astype(BF16)
    for a in range(3):
        for u in range(4):
            start = (a * 4 + u) * 128
            for q in range(2):
                b = q + 2 - u
                block = weight[a, b].astype(F32).T.astype(BF16) if 0 <= b <= 2 else nothing
                back[start : start + 128, q * 128 : (q + 1) * 128] = block
    slot = iota((64, 32), 0)
    small[...] = jnp.zeros_like(small)
    for k in range(9):
        small[3 * k : 3 * k + 3, :] = out_weight[k].astype(F32)
    for k in range(4):
        a, b = k // 2 + 2 - (slot & 3), k % 2 + 2 - (slot >> 4)
        channel = (slot >> 2) & 3
        valid = (a >= 0) & (a <= 2) & (b >= 0) & (b <= 2) & (channel < 3)
        window = as_bf16((iota((64, 32), 1) == a * 9 + b * 3 + channel) & valid)
        kernel[:, k * 128 : (k + 1) * 128] = dot(window, small[...].astype(BF16)).astype(BF16)


def gates(features, weight, bias, out_weight):
    return pl.pallas_call(
        gate_kernel,
        out_shape=(
            jax.ShapeDtypeStruct((33 * PITCH, 512), BF16),
            jax.ShapeDtypeStruct((1536, 256), BF16),
            jax.ShapeDtypeStruct((64, 512), BF16),
            jax.ShapeDtypeStruct((1536, 256), BF16),
        ),
        in_specs=[IN_HBM] * 2 + [IN_VMEM] * 2,
        scratch_shapes=[
            pltpu.VMEM((32, 32, 512), BF16),
            pltpu.VMEM((3, 3, 128, 128), BF16),
            pltpu.VMEM((34, 56, 512), F32),
            pltpu.VMEM((34 * PITCH, 512), BF16),
            pltpu.VMEM((34 * PITCH, 512), BF16),
            pltpu.VMEM((32, 128), F32),
            pltpu.SemaphoreType.DMA((2,)),
        ],
        compiler_params=pltpu.CompilerParams(vmem_limit_bytes=VMEM_LIMIT),
        cost_estimate=pl.CostEstimate(flops=5 * 10**9, bytes_accessed=4 * 10**6, transcendentals=2 * 10**6),
        name="gate",
    )(features, weight, bias, out_weight)


def ring_gates(parts, own, bias, taps, strips):
    high, core, column = lax.axis_index("zhi"), lax.axis_index("core"), lax.axis_index("seq")
    other = (1 - high) * 4

    def halo(slot):
        return jnp.concatenate(
            [parts[slot, PACKED + 32 * k : PACKED + 32 * k + 32, :] for k in range(4)], axis=1
        ).astype(F32)

    def ends(slot):
        rows = parts[slot, PACKED + 128 :, :].astype(F32)
        return [jnp.concatenate([rows[2 * k + e : 2 * k + e + 1] for k in range(4)], axis=1) for e in range(2)]

    def only(condition, values):
        return jnp.where(condition, values, 0.0)

    lines = [own[k].astype(F32) for k in range(6)]
    distant = halo(other + column)
    above = jnp.where(core == 1, lines[5], only(high == 1, distant))
    below = jnp.where(core == 0, lines[4], only(high == 0, distant))
    sides, corners = [], []
    for step in (-1, 1):
        there = jnp.clip(column + step, 0, 3)
        inside = there != column
        sides.append(only(inside, halo(high * 4 + there)))
        near_ends, far_ends = ends(high * 4 + there), ends(other + there)
        corners.append(
            [
                only(inside, jnp.where(core == 1, near_ends[0], only(high == 1, far_ends[0]))),
                only(inside, jnp.where(core == 0, near_ends[1], only(high == 0, far_ends[1]))),
            ]
        )
    put = [
        (above, corners[0][0], corners[1][0]),
        (lines[0], sides[0][0:1], sides[1][0:1]),
        (lines[1], sides[0][31:32], sides[1][31:32]),
        (below, corners[0][1], corners[1][1]),
        (sides[0], corners[0][0], corners[0][1]),
        (lines[2], above[0:1], below[0:1]),
        (lines[3], above[31:32], below[31:32]),
        (sides[1], corners[1][0], corners[1][1]),
    ]
    for k, (middle, first, last) in enumerate(put):
        strips[k, 0:8, :] = jnp.zeros((8, 512), F32)
        strips[k, 40:56, :] = jnp.zeros((16, 512), F32)
        for at, values in ((8, middle), (7, first), (40, last)):
            for q, phase in enumerate(inverse_haar(values)):
                strips[k, at : at + values.shape[0], q * 128 : (q + 1) * 128] = phase
    shifted = [[strips[k, 7 + d : 55 + d, :].astype(BF16) for d in range(2)] for k in range(8)]
    wide_bias = jnp.concatenate([bias[...], bias[...]], axis=1)
    found = []
    for phase in range(2):
        stack = []
        for strip in range(4):
            pieces = []
            for a in range(3):
                step, parity = divmod(phase + a, 2)
                for turn in range(2):
                    if strip < 2:
                        source = shifted[2 * strip + step][turn]
                    else:
                        source = shifted[2 * strip + turn][step]
                    pieces.append(source[:, parity * 256 : (parity + 1) * 256])
            stack.append(jnp.concatenate(pieces, axis=1))
        found.append(slope_of(dot(jnp.concatenate(stack, axis=0), taps[...]) + wide_bias))
    rings = [
        jnp.concatenate([each[strip * PITCH : (strip + 1) * PITCH] for each in found], axis=1) for strip in range(4)
    ]
    at, lane = iota((PITCH, 512), 0), iota((PITCH, 512), 1)
    even, upper = (lane & 255) < 128, lane < 256
    left = (column == 0) & even
    right = (column == 3) & jnp.logical_not(even)
    beside = (left & (at == 0)) | (right & (at == 32))
    first_line = (high == 0) & (core == 0) & upper
    last_line = (high == 1) & (core == 1) & jnp.logical_not(upper)
    masks = [beside | first_line, beside | last_line, left, right]
    return [jnp.where(mask, 0.0, ring) for mask, ring in zip(masks, rings)]


def finish_kernel(
    parts, gate_hbm, back_hbm, kernel_hbm, taps_hbm, own_hbm, bias_hbm,
    out, gate, back, kernel, taps, own, bias, strips, columns, pixels, edges, total, stacked, near, far, semaphores,
):
    pairs = [(own_hbm, own), (bias_hbm, bias), (taps_hbm, taps), (kernel_hbm, kernel), (gate_hbm, gate), (back_hbm, back)]
    copies = fetch(semaphores, pairs)
    sums = parts[0, 0:PACKED, :].astype(F32)
    for source in range(1, 8):
        sums = sums + parts[source, 0:PACKED, :].astype(F32)
    total[...] = sums
    pixels[...] = jnp.zeros_like(pixels)
    edges[...] = jnp.zeros_like(edges)
    for channel in range(3):
        top = channel * 80
        half = total[channel * HALF_TILE : (channel + 1) * HALF_TILE, :] / PIXEL_STD[channel]
        pixels[top : top + HALF_TILE, :] = half
        pixels[top + HALF_TILE : top + 2 * HALF_TILE, :] = pltpu.roll(half, 64, 1)
        rest = total[3 * HALF_TILE :, :] / PIXEL_STD[channel]
        for block in range(7):
            turn = (64 - block * 12 - channel * 4) % SPAN
            edges[top + block * 10 : top + block * 10 + 10, :] = pltpu.roll(rest, turn, 1)
    rounded = jnp.where(iota((240, SPAN), 1) < 64, pixels[...], edges[...]).astype(BF16)
    picked = None
    x, lane = iota((SPAN, 512), 0), iota((SPAN, 512), 1)
    row, y = iota((176, 240), 0), iota((176, 240), 1)
    for third in range(3):
        j = (lane & 127) - 40 * third
        spread = as_bf16((x == 2 * j + (lane >> 7)) & (j >= 0) & (j < 33))
        channel = (row >> 2) & 3
        lines = as_bf16((y == channel * 80 + 2 * (3 * (row >> 4) + third) + (row & 3)) & (channel < 3))
        moved = dot(rounded, spread).astype(BF16)
        term = dot(lines, moved)
        picked = term if picked is None else picked + term
    picked = picked.astype(BF16)
    for line in range(11):
        for k in range(4):
            stacked[line, k * 16 : k * 16 + 16, :] = picked[line * 16 : line * 16 + 16, k * SPAN : (k + 1) * SPAN]
    for copy in copies[:4]:
        copy.wait()
    rings = ring_gates(parts, own, bias, taps, strips)
    columns[0] = rings[2]
    columns[1] = rings[3]
    copies[4].wait()
    at = iota((PITCH, 512), 0)
    for line in range(11):
        act = dot(stacked[line], kernel[...], TN)
        for third in range(3):
            index = line * 3 + third
            if index == 0:
                scale = rings[0]
            elif index == 32:
                scale = rings[1]
            else:
                scale = gate[index * PITCH : (index + 1) * PITCH, :].astype(F32)
                scale = jnp.where(at == 0, columns[0, index : index + 1, :], scale)
                scale = jnp.where(at == 32, columns[1, index : index + 1, :], scale)
            grad = act[third * 40 : third * 40 + 40] * scale[0:40]
            near[index * 32 : (index + 1) * 32, :] = grad[0:32].astype(BF16)
            far[index * 32 : (index + 1) * 32, :] = grad[1:33].astype(BF16)
    copies[5].wait()
    for chunk in range(4):
        stack = []
        for p in range(2):
            pieces = []
            for a in range(3):
                step, parity = divmod(p + 2 - a, 2)
                start = chunk * 256 + step * 32
                for source in (near, far):
                    pieces.append(source[start : start + 256, parity * 256 : (parity + 1) * 256])
            stack.append(jnp.concatenate(pieces, axis=1))
        found = dot(jnp.concatenate(stack, axis=0), back[...])
        plus, minus = found[:256] + found[256:], found[:256] - found[256:]
        bands = [
            plus[:, :128] + plus[:, 128:],
            minus[:, :128] + minus[:, 128:],
            plus[:, :128] - plus[:, 128:],
            minus[:, :128] - minus[:, 128:],
        ]
        for k, band in enumerate(bands):
            out[chunk * 8 : chunk * 8 + 8, :, k * 128 : (k + 1) * 128] = (0.5 * band).astype(BF16).reshape(8, 32, 128)


def finish(parts, gate, back, kernel, taps, own, bias):
    return pl.pallas_call(
        finish_kernel,
        out_shape=jax.ShapeDtypeStruct((32, 32, 512), BF16),
        in_specs=[IN_VMEM] + [IN_HBM] * 6,
        scratch_shapes=[
            pltpu.VMEM((33 * PITCH, 512), BF16),
            pltpu.VMEM((1536, 256), BF16),
            pltpu.VMEM((64, 512), BF16),
            pltpu.VMEM((1536, 256), BF16),
            pltpu.VMEM((6, 32, 512), BF16),
            pltpu.VMEM((1, 128), F32),
            pltpu.VMEM((8, 56, 512), F32),
            pltpu.VMEM((2, PITCH, 512), F32),
            pltpu.VMEM((240, SPAN), F32),
            pltpu.VMEM((240, SPAN), F32),
            pltpu.VMEM((PACKED, SPAN), F32),
            pltpu.VMEM((11, 64, SPAN), BF16),
            pltpu.VMEM((33 * 32, 512), BF16),
            pltpu.VMEM((33 * 32, 512), BF16),
            pltpu.SemaphoreType.DMA((6,)),
        ],
        compiler_params=pltpu.CompilerParams(vmem_limit_bytes=VMEM_LIMIT),
        name="finish",
    )(parts, gate, back, kernel, taps, own, bias)


SWAP = [(0, 1), (1, 0)]
ROW = ("zhi", "core")


def on_device(reward_grad, embed_weight, crop_offsets, features, conv_weight, conv_bias, out_weight):
    mine = lax.all_to_all(view_pairs(reward_grad), "tok", split_axis=0, concat_axis=0, tiled=True)
    other_weight = lax.ppermute(embed_weight, "core", SWAP)
    coarse = features[0]
    partner_top = lax.ppermute(coarse[:1], "core", SWAP)
    partner_bottom = lax.ppermute(coarse[31:], "core", SWAP)
    offsets = crop_offsets.T
    wide = spread_weight(embed_weight, other_weight)
    halo, own = edge_slots(coarse, partner_top, partner_bottom)
    mine, wide, halo = lax.optimization_barrier((mine, wide, halo))
    partials = place_partials(offsets, mine, lax.ppermute(mine, "core", SWAP), wide, halo)
    small = out_weight.transpose(0, 1, 3, 2).reshape(9, 3, 128)
    bias = conv_bias[None]
    gate = gates(coarse, conv_weight, bias, small)
    partials, gate, own = lax.optimization_barrier((partials, gate, own))
    parts = lax.all_to_all(partials, ("zhi", "seq"), split_axis=0, concat_axis=0, tiled=True)
    return finish(parts, *gate, own, bias)[None]


def solution(mesh):
    split = Mesh(mesh.devices.reshape(16, 2, 2, 4), ("tok", "zhi", "core", "seq"))
    placed = (
        P(None, "tok", ("zhi", "core", "seq")),
        P(("zhi", "core", "seq"), None),
        P("tok", None),
        P("tok", ROW, "seq", None),
        P(),
        P(),
        P(),
    )
    return jax.shard_map(
        on_device,
        mesh=split,
        in_specs=placed,
        out_specs=P("tok", ROW, "seq", None),
        check_vma=False,
    )
```

```python
import jax
import jax.numpy as jnp
from jax import lax
from jax.experimental import pallas as pl
from jax.experimental.pallas import tpu as pltpu
from jax.sharding import Mesh
from jax.sharding import PartitionSpec as P

PIXEL_STD = (0.26862954, 0.26130258, 0.27577711)
BF16 = jnp.bfloat16
F32 = jnp.float32
VIEWS = 4
TILE_PIX = 68
SPAN = 128
HALF_TILE = 34
BAND = 80
PACKED = 112
CORNERS = 16
PITCH = 48
NT = (((1,), (1,)), ((), ()))
TN = (((0,), (0,)), ((), ()))
VMEM_LIMIT = 16 * 2**20
WHOLE_VMEM = 60 * 2**20
IN_HBM = pl.BlockSpec(memory_space=pltpu.HBM)
IN_VMEM = pl.BlockSpec(memory_space=pltpu.VMEM)


def iota(shape, axis):
    return lax.broadcasted_iota(jnp.int32, shape, axis)


def dot(a, b, dims=(((1,), (0,)), ((), ()))):
    return lax.dot_general(a, b, dims, preferred_element_type=F32)


def fetch(semaphores, pairs):
    copies = [pltpu.make_async_copy(src, dst, semaphores.at[k]) for k, (src, dst) in enumerate(pairs)]
    for copy in copies:
        copy.start()
    return copies


def as_bf16(mask):
    return jnp.where(mask, 1.0, 0.0).astype(BF16)


def pair_kernel(reward, out):
    for pair in range(32):
        out[pair] = jnp.concatenate([reward[2 * pair], reward[2 * pair + 1]], axis=1)


def view_pairs(reward):
    return pl.pallas_call(
        pair_kernel,
        out_shape=jax.ShapeDtypeStruct((32, 16, SPAN), BF16),
        compiler_params=pltpu.CompilerParams(vmem_limit_bytes=VMEM_LIMIT),
        name="pairs",
    )(reward)


def place_kernel(offsets, reward, other, spread, ends, out, flat, left, strips, across, canvas, packed, rows):
    own, theirs = [each[...].astype(F32).reshape(512, SPAN) for each in (reward, other)]
    low = iota((512, SPAN), 1) < 64
    flat[0] = jnp.where(low, own, pltpu.roll(theirs, 64, 1))
    flat[1] = jnp.where(low, pltpu.roll(own, 64, 1), theirs)
    for view in range(VIEWS):
        for patch in range(16):
            top = (patch // 4) * 64 + view * 16
            side = (patch % 4) * SPAN
            values = flat[view % 2, pl.ds((view // 2) * 16 + patch, 16, stride=32), :]
            left[top : top + 16, side : side + SPAN] = values.astype(BF16)
    low = iota((64, SPAN), 1) < 64
    own_group = ((iota((256, 512), 0) >> 4) & 3) == (iota((256, 512), 1) >> 7)
    for quad in range(11):
        blocks = [jnp.concatenate([spread[4 * quad + k]] * 4, axis=0) for k in range(4)]
        weights = jnp.concatenate([jnp.concatenate(blocks, axis=0)] * 4, axis=1)
        part = dot(left[...], jnp.where(own_group, weights, jnp.zeros((256, 512), BF16)), NT)
        for member in range(2):
            own = [part[64 * h : 64 * h + 64, member * SPAN : (member + 1) * SPAN] for h in range(4)]
            turned = [pltpu.roll(piece, 64, 1) for piece in own]
            for odd in range(2):
                start = (4 * quad + 2 * member + odd) * 16
                for side in range(2):
                    a, b = 2 * side, 2 * side + 1
                    if odd == 0:
                        joined = jnp.where(low, own[a], turned[b]).astype(BF16)
                    else:
                        joined = jnp.where(low, turned[a], own[b]).astype(BF16)
                    for view in range(VIEWS):
                        strips[view, start : start + 16, side * SPAN : (side + 1) * SPAN] = joined[
                            view * 16 : view * 16 + 16
                        ]
    slot, lane = iota((256, 512), 0), iota((256, 512), 1)
    gap = (lane >> 7) * 64 - 2 + (lane & 127) - (slot >> 4) * 14 - (slot & 15)
    gap = jnp.where(((slot & 15) < 14) & ((lane & 127) < TILE_PIX), gap, -1000)
    for view in range(VIEWS):
        cols = as_bf16(gap == offsets[1, view])
        for channel in range(3):
            across[channel, view * 224 : (view + 1) * 224, :] = dot(
                strips[view, channel * 224 : (channel + 1) * 224, :], cols
            ).astype(BF16)
    step, index = iota((BAND, 896), 0), iota((1, 896), 1)
    local, corner = index, jnp.zeros((1, 896), jnp.int32) + offsets[0, 0]
    for view in range(1, VIEWS):
        local = jnp.where(index >= 224 * view, index - 224 * view, local)
        corner = jnp.where(index >= 224 * view, offsets[0, view], corner)
    first = corner + 14 * (local & 15) + (local >> 4)
    core = lax.axis_index("core")
    for high in range(2):
        y = step + (64 * (2 * high + core) - 2)
        hit = as_bf16((y == first) & (step < TILE_PIX))
        rows[high * BAND : (high + 1) * BAND, :] = hit
    for channel in range(3):
        canvas[channel] = dot(rows[...], across[channel])
    lane = iota((HALF_TILE, SPAN), 1)
    wide_lane = iota((BAND, SPAN), 1)
    for high in range(2):
        for column in range(4):
            side = slice(column * SPAN, (column + 1) * SPAN)
            top = high * BAND
            for channel in range(3):
                upper = canvas[channel, top : top + HALF_TILE, side]
                lower = pltpu.roll(canvas[channel, top + HALF_TILE : top + 2 * HALF_TILE, side], 64, 1)
                packed[channel * HALF_TILE : (channel + 1) * HALF_TILE, :] = jnp.where(lane < 64, upper, lower)
            last = [canvas[channel, top : top + BAND, side] for channel in range(3)]
            joined = jnp.where(wide_lane < 68, last[0], pltpu.roll(last[1], 4, 1))
            joined = jnp.where(wide_lane < 72, joined, pltpu.roll(last[2], 8, 1))
            rest = None
            for block in range(7):
                piece = pltpu.roll(joined[block * 10 : block * 10 + 10], (64 + block * 12) % SPAN, 1)
                rest = piece if block == 0 else jnp.where(wide_lane[:10] < block * 12, rest, piece)
            packed[3 * HALF_TILE :, :] = rest
            out[high * 4 + column, 0:PACKED, :] = packed[...].astype(BF16)
            out[high * 4 + column, PACKED:, :] = ends[high * 4 + column]


def place_partials(offsets, reward, other, spread, ends):
    return pl.pallas_call(
        place_kernel,
        out_shape=jax.ShapeDtypeStruct((8, PACKED + CORNERS, SPAN), BF16),
        in_specs=[pl.BlockSpec(memory_space=pltpu.SMEM)] + [IN_VMEM] * 4,
        scratch_shapes=[
            pltpu.VMEM((2, 512, SPAN), F32),
            pltpu.VMEM((256, 512), BF16),
            pltpu.VMEM((VIEWS, 704, 256), BF16),
            pltpu.VMEM((3, 896, 512), BF16),
            pltpu.VMEM((3, 2 * BAND, 512), F32),
            pltpu.VMEM((PACKED, SPAN), F32),
            pltpu.VMEM((2 * BAND, 896), BF16),
        ],
        compiler_params=pltpu.CompilerParams(vmem_limit_bytes=VMEM_LIMIT),
        name="place",
    )(offsets, reward, other, spread, ends)


def edge_kernel(
    features_hbm, weight_hbm, other_hbm, top_hbm, bottom_hbm,
    spread, own, out, features, weights, halves, semaphores,
):
    high, core, column = lax.axis_index("zhi"), lax.axis_index("core"), lax.axis_index("seq")
    pairs = [(weight_hbm, weights.at[0]), (other_hbm, weights.at[1])]
    pairs += [(top_hbm, own.at[4:5]), (bottom_hbm, own.at[5:6]), (features_hbm, features)]
    copies = fetch(semaphores, pairs)
    copies[0].wait()
    copies[1].wait()
    slot = iota((704, 588), 0)
    pick = as_bf16(((slot >> 4) * 14 + (slot & 15) == iota((704, 588), 1)) & ((slot & 15) < 14))
    both = jnp.concatenate([weights[0], weights[1]], axis=0)
    spread[...] = dot(pick, both, NT).astype(BF16).reshape(44, 16, SPAN)
    for copy in copies[2:]:
        copy.wait()
    top, bottom = own[4].astype(F32), own[5].astype(F32)
    far = jnp.where(core == 0, bottom, top)
    nothing = jnp.zeros((8, SPAN), F32)

    def put_ends(slot, above, below):
        rows = [each[:, k * SPAN : (k + 1) * SPAN] for k in range(4) for each in (above, below)]
        out[slot] = jnp.concatenate(rows + [nothing], axis=0).astype(BF16)

    out[...] = jnp.zeros_like(out)
    own[0] = features[0]
    own[1] = features[31]
    for index, (step, side, row, end) in enumerate(((-1, 0, 0, 0), (1, 16, 15, 31))):
        parts = []
        for k in range(4):
            lanes = slice(k * SPAN, (k + 1) * SPAN)
            halves[k] = features[:, side : side + 16, lanes].astype(F32).reshape(512, SPAN)
            parts.append(halves[k, pl.ds(row, 32, stride=16), :])
        own[2 + index] = jnp.concatenate(parts, axis=1).astype(BF16)
        there = jnp.clip(column + step, 0, 3)

        @pl.when(there != column)
        def _():
            put_ends(high * 4 + there, bottom[end : end + 1], top[end : end + 1])
            put_ends((1 - high) * 4 + there, far[end : end + 1], far[end : end + 1])


def edges_of(features, weight, other_weight, partner_top, partner_bottom):
    return pl.pallas_call(
        edge_kernel,
        out_shape=(
            jax.ShapeDtypeStruct((44, 16, SPAN), BF16),
            jax.ShapeDtypeStruct((6, 32, 512), BF16),
            jax.ShapeDtypeStruct((8, CORNERS, SPAN), BF16),
        ),
        in_specs=[IN_HBM] * 5,
        scratch_shapes=[
            pltpu.VMEM((32, 32, 512), BF16),
            pltpu.VMEM((2, 64, 588), BF16),
            pltpu.VMEM((4, 512, SPAN), F32),
            pltpu.SemaphoreType.DMA((5,)),
        ],
        compiler_params=pltpu.CompilerParams(vmem_limit_bytes=48 * 2**20),
        name="edges",
    )(features, weight, other_weight, partner_top, partner_bottom)


def inverse_haar(values):
    smooth, vertical, horizontal, diagonal = [values[:, k * 128 : (k + 1) * 128].astype(F32) for k in range(4)]
    upper_sum = smooth + vertical
    lower_sum = smooth - vertical
    upper_diff = horizontal + diagonal
    lower_diff = horizontal - diagonal
    return [
        0.5 * (upper_sum + upper_diff),
        0.5 * (upper_sum - upper_diff),
        0.5 * (lower_sum + lower_diff),
        0.5 * (lower_sum - lower_diff),
    ]


def slope_of(pre):
    sigmoid = 0.5 + 0.5 * jnp.tanh(0.5 * pre)
    return sigmoid * (1.0 + pre * (1.0 - sigmoid))


def gate_kernel(
    features_hbm, weight_hbm, bias, out_weight,
    out, back, kernel, taps, features, weight, fine, near, far, small, semaphores,
):
    copies = fetch(semaphores, [(features_hbm, features), (weight_hbm, weight)])
    copies[0].wait()

    @pl.loop(0, 32, unroll=4)
    def _(line):
        for k, phase in enumerate(inverse_haar(features[line])):
            fine[line + 1, 8:40, k * 128 : (k + 1) * 128] = phase

    copies[1].wait()

    @pl.loop(0, 34, unroll=2)
    def _(line):
        start = pl.multiple_of(line * PITCH, PITCH)
        near[pl.ds(start, PITCH), :] = fine[line, 7:55, :].astype(BF16)
        far[pl.ds(start, PITCH), :] = fine[line, 8:56, :].astype(BF16)

    nothing = jnp.zeros((128, 128), BF16)
    for a in range(3):
        for u in range(4):
            start = (a * 4 + u) * 128
            taps[start : start + 128, 0:128] = weight[a, u] if u < 3 else nothing
            taps[start : start + 128, 128:] = weight[a, u - 1] if u > 0 else nothing
    wide_bias = jnp.concatenate([bias[...], bias[...]], axis=1)
    count = 11 * PITCH
    for chunk in range(3):
        for phase in range(2):
            pieces = []
            for a in range(3):
                lines, parity = divmod(phase + a, 2)
                start = chunk * count + lines * PITCH
                for source in (near, far):
                    pieces.append(source[start : start + count, parity * 256 : (parity + 1) * 256])
            slope = slope_of(dot(jnp.concatenate(pieces, axis=1), taps[...]) + wide_bias)
            here = chunk * count
            out[here : here + count, phase * 256 : (phase + 1) * 256] = slope.astype(BF16)
    for a in range(3):
        for u in range(4):
            start = (a * 4 + u) * 128
            for q in range(2):
                b = q + 2 - u
                block = weight[a, b].astype(F32).T.astype(BF16) if 0 <= b <= 2 else nothing
                back[start : start + 128, q * 128 : (q + 1) * 128] = block
    slot = iota((64, 32), 0)
    small[...] = jnp.zeros_like(small)
    for k in range(9):
        small[3 * k : 3 * k + 3, :] = out_weight[k].astype(F32)
    for k in range(4):
        a, b = k // 2 + 2 - (slot & 3), k % 2 + 2 - (slot >> 4)
        channel = (slot >> 2) & 3
        valid = (a >= 0) & (a <= 2) & (b >= 0) & (b <= 2) & (channel < 3)
        window = as_bf16((iota((64, 32), 1) == a * 9 + b * 3 + channel) & valid)
        kernel[:, k * 128 : (k + 1) * 128] = dot(window, small[...].astype(BF16)).astype(BF16)


def gates(features, weight, bias, out_weight):
    return pl.pallas_call(
        gate_kernel,
        out_shape=(
            jax.ShapeDtypeStruct((33 * PITCH, 512), BF16),
            jax.ShapeDtypeStruct((1536, 256), BF16),
            jax.ShapeDtypeStruct((64, 512), BF16),
            jax.ShapeDtypeStruct((1536, 256), BF16),
        ),
        in_specs=[IN_HBM] * 2 + [IN_VMEM] * 2,
        scratch_shapes=[
            pltpu.VMEM((32, 32, 512), BF16),
            pltpu.VMEM((3, 3, 128, 128), BF16),
            pltpu.VMEM((34, 56, 512), F32),
            pltpu.VMEM((34 * PITCH, 512), BF16),
            pltpu.VMEM((34 * PITCH, 512), BF16),
            pltpu.VMEM((32, 128), F32),
            pltpu.SemaphoreType.DMA((2,)),
        ],
        compiler_params=pltpu.CompilerParams(vmem_limit_bytes=WHOLE_VMEM),
        cost_estimate=pl.CostEstimate(flops=5 * 10**9, bytes_accessed=4 * 10**6, transcendentals=2 * 10**6),
        name="gate",
    )(features, weight, bias, out_weight)


def ring_gates(parts, own, far, sides, bias, taps, strips):
    high, core, column = lax.axis_index("zhi"), lax.axis_index("core"), lax.axis_index("seq")
    other = (1 - high) * 4

    def ends(slot):
        rows = parts[slot, PACKED:, :].astype(F32)
        return [jnp.concatenate([rows[2 * k + e : 2 * k + e + 1] for k in range(4)], axis=1) for e in range(2)]

    def only(condition, values):
        return jnp.where(condition, values, 0.0)

    lines = [own[k].astype(F32) for k in range(6)]
    above = jnp.where(core == 1, lines[5], far[0].astype(F32))
    below = jnp.where(core == 0, lines[4], far[1].astype(F32))
    sides = [sides[k].astype(F32) for k in range(2)]
    corners = []
    for step in (-1, 1):
        there = jnp.clip(column + step, 0, 3)
        inside = there != column
        near_ends, far_ends = ends(high * 4 + there), ends(other + there)
        corners.append(
            [
                only(inside, jnp.where(core == 1, near_ends[0], only(high == 1, far_ends[0]))),
                only(inside, jnp.where(core == 0, near_ends[1], only(high == 0, far_ends[1]))),
            ]
        )
    put = [
        (above, corners[0][0], corners[1][0]),
        (lines[0], sides[0][0:1], sides[1][0:1]),
        (lines[1], sides[0][31:32], sides[1][31:32]),
        (below, corners[0][1], corners[1][1]),
        (sides[0], corners[0][0], corners[0][1]),
        (lines[2], above[0:1], below[0:1]),
        (lines[3], above[31:32], below[31:32]),
        (sides[1], corners[1][0], corners[1][1]),
    ]
    for k, (middle, first, last) in enumerate(put):
        strips[k, 0:8, :] = jnp.zeros((8, 512), F32)
        strips[k, 40:56, :] = jnp.zeros((16, 512), F32)
        for at, values in ((8, middle), (7, first), (40, last)):
            for q, phase in enumerate(inverse_haar(values)):
                strips[k, at : at + values.shape[0], q * 128 : (q + 1) * 128] = phase
    shifted = [[strips[k, 7 + d : 55 + d, :].astype(BF16) for d in range(2)] for k in range(8)]
    wide_bias = jnp.concatenate([bias[...], bias[...]], axis=1)
    found = []
    for phase in range(2):
        stack = []
        for strip in range(4):
            pieces = []
            for a in range(3):
                step, parity = divmod(phase + a, 2)
                for turn in range(2):
                    if strip < 2:
                        source = shifted[2 * strip + step][turn]
                    else:
                        source = shifted[2 * strip + turn][step]
                    pieces.append(source[:, parity * 256 : (parity + 1) * 256])
            stack.append(jnp.concatenate(pieces, axis=1))
        found.append(slope_of(dot(jnp.concatenate(stack, axis=0), taps[...]) + wide_bias))
    rings = [
        jnp.concatenate([each[strip * PITCH : (strip + 1) * PITCH] for each in found], axis=1) for strip in range(4)
    ]
    at, lane = iota((PITCH, 512), 0), iota((PITCH, 512), 1)
    even, upper = (lane & 255) < 128, lane < 256
    left = (column == 0) & even
    right = (column == 3) & jnp.logical_not(even)
    beside = (left & (at == 0)) | (right & (at == 32))
    first_line = (high == 0) & (core == 0) & upper
    last_line = (high == 1) & (core == 1) & jnp.logical_not(upper)
    masks = [beside | first_line, beside | last_line, left, right]
    return [jnp.where(mask, 0.0, ring) for mask, ring in zip(masks, rings)]


def finish_kernel(
    parts, gate_hbm, back_hbm, kernel_hbm, taps_hbm, own_hbm, above_hbm, below_hbm, before_hbm, after_hbm, bias_hbm,
    out, gate, back, kernel, taps, own, far_rows, sides, bias, strips, columns, pixels, edges, total, stacked, near, far, semaphores,
):
    pairs = [(own_hbm, own), (bias_hbm, bias), (above_hbm, far_rows.at[0:1]), (below_hbm, far_rows.at[1:2])]
    pairs += [(before_hbm, sides.at[0]), (after_hbm, sides.at[1]), (taps_hbm, taps), (kernel_hbm, kernel)]
    pairs += [(gate_hbm, gate), (back_hbm, back)]
    copies = fetch(semaphores, pairs)
    sums = parts[0, 0:PACKED, :].astype(F32)
    for source in range(1, 8):
        sums = sums + parts[source, 0:PACKED, :].astype(F32)
    total[...] = sums
    pixels[...] = jnp.zeros_like(pixels)
    edges[...] = jnp.zeros_like(edges)
    for channel in range(3):
        top = channel * 80
        half = total[channel * HALF_TILE : (channel + 1) * HALF_TILE, :] / PIXEL_STD[channel]
        pixels[top : top + HALF_TILE, :] = half
        pixels[top + HALF_TILE : top + 2 * HALF_TILE, :] = pltpu.roll(half, 64, 1)
        rest = total[3 * HALF_TILE :, :] / PIXEL_STD[channel]
        for block in range(7):
            turn = (64 - block * 12 - channel * 4) % SPAN
            edges[top + block * 10 : top + block * 10 + 10, :] = pltpu.roll(rest, turn, 1)
    rounded = jnp.where(iota((240, SPAN), 1) < 64, pixels[...], edges[...]).astype(BF16)
    picked = None
    x, lane = iota((SPAN, 512), 0), iota((SPAN, 512), 1)
    row, y = iota((176, 240), 0), iota((176, 240), 1)
    for third in range(3):
        j = (lane & 127) - 40 * third
        spread = as_bf16((x == 2 * j + (lane >> 7)) & (j >= 0) & (j < 33))
        channel = (row >> 2) & 3
        lines = as_bf16((y == channel * 80 + 2 * (3 * (row >> 4) + third) + (row & 3)) & (channel < 3))
        moved = dot(rounded, spread).astype(BF16)
        term = dot(lines, moved)
        picked = term if picked is None else picked + term
    picked = picked.astype(BF16)
    for line in range(11):
        for k in range(4):
            stacked[line, k * 16 : k * 16 + 16, :] = picked[line * 16 : line * 16 + 16, k * SPAN : (k + 1) * SPAN]
    for copy in copies[:8]:
        copy.wait()
    rings = ring_gates(parts, own, far_rows, sides, bias, taps, strips)
    columns[0] = rings[2]
    columns[1] = rings[3]
    copies[8].wait()
    at = iota((PITCH, 512), 0)
    for line in range(11):
        act = dot(stacked[line], kernel[...], TN)
        for third in range(3):
            index = line * 3 + third
            if index == 0:
                scale = rings[0]
            elif index == 32:
                scale = rings[1]
            else:
                scale = gate[index * PITCH : (index + 1) * PITCH, :].astype(F32)
                scale = jnp.where(at == 0, columns[0, index : index + 1, :], scale)
                scale = jnp.where(at == 32, columns[1, index : index + 1, :], scale)
            grad = act[third * 40 : third * 40 + 40] * scale[0:40]
            near[index * 32 : (index + 1) * 32, :] = grad[0:32].astype(BF16)
            far[index * 32 : (index + 1) * 32, :] = grad[1:33].astype(BF16)
    copies[9].wait()
    for chunk in range(4):
        stack = []
        for p in range(2):
            pieces = []
            for a in range(3):
                step, parity = divmod(p + 2 - a, 2)
                start = chunk * 256 + step * 32
                for source in (near, far):
                    pieces.append(source[start : start + 256, parity * 256 : (parity + 1) * 256])
            stack.append(jnp.concatenate(pieces, axis=1))
        found = dot(jnp.concatenate(stack, axis=0), back[...])
        plus, minus = found[:256] + found[256:], found[:256] - found[256:]
        bands = [
            plus[:, :128] + plus[:, 128:],
            minus[:, :128] + minus[:, 128:],
            plus[:, :128] - plus[:, 128:],
            minus[:, :128] - minus[:, 128:],
        ]
        for k, band in enumerate(bands):
            out[chunk * 8 : chunk * 8 + 8, :, k * 128 : (k + 1) * 128] = (0.5 * band).astype(BF16).reshape(8, 32, 128)


def finish(parts, gate, back, kernel, taps, *rest):
    return pl.pallas_call(
        finish_kernel,
        out_shape=jax.ShapeDtypeStruct((32, 32, 512), BF16),
        in_specs=[IN_VMEM] + [IN_HBM] * 10,
        scratch_shapes=[
            pltpu.VMEM((33 * PITCH, 512), BF16),
            pltpu.VMEM((1536, 256), BF16),
            pltpu.VMEM((64, 512), BF16),
            pltpu.VMEM((1536, 256), BF16),
            pltpu.VMEM((6, 32, 512), BF16),
            pltpu.VMEM((2, 32, 512), BF16),
            pltpu.VMEM((2, 32, 512), BF16),
            pltpu.VMEM((1, 128), F32),
            pltpu.VMEM((8, 56, 512), F32),
            pltpu.VMEM((2, PITCH, 512), F32),
            pltpu.VMEM((240, SPAN), F32),
            pltpu.VMEM((240, SPAN), F32),
            pltpu.VMEM((PACKED, SPAN), F32),
            pltpu.VMEM((11, 64, SPAN), BF16),
            pltpu.VMEM((33 * 32, 512), BF16),
            pltpu.VMEM((33 * 32, 512), BF16),
            pltpu.SemaphoreType.DMA((10,)),
        ],
        compiler_params=pltpu.CompilerParams(vmem_limit_bytes=WHOLE_VMEM),
        name="finish",
    )(parts, gate, back, kernel, taps, *rest)


SWAP = [(0, 1), (1, 0)]
ROW = ("zhi", "core")


def on_device(reward_grad, embed_weight, crop_offsets, features, conv_weight, conv_bias, out_weight):
    mine = lax.all_to_all(view_pairs(reward_grad), "tok", split_axis=0, concat_axis=0, tiled=True)
    other_weight = lax.ppermute(embed_weight, "core", SWAP)
    coarse = features[0]
    partner_top = lax.ppermute(coarse[:1], "core", SWAP)
    partner_bottom = lax.ppermute(coarse[31:], "core", SWAP)
    far_bottom = lax.ppermute(partner_bottom, ROW, [(0, 2)])
    far_top = lax.ppermute(partner_top, ROW, [(3, 1)])
    spread, own, ends = edges_of(coarse, embed_weight, other_weight, partner_top, partner_bottom)
    mine, spread, ends, own, far_bottom, far_top = lax.optimization_barrier(
        (mine, spread, ends, own, far_bottom, far_top)
    )
    partials = place_partials(crop_offsets.T, mine, lax.ppermute(mine, "core", SWAP), spread, ends)
    partials, coarse, own = lax.optimization_barrier((partials, coarse, own))
    parts = lax.all_to_all(partials, ("zhi", "seq"), split_axis=0, concat_axis=0, tiled=True)
    before = lax.ppermute(own[3], "seq", [(i, i + 1) for i in range(3)])
    after = lax.ppermute(own[2], "seq", [(i + 1, i) for i in range(3)])
    small = out_weight.transpose(0, 1, 3, 2).reshape(9, 3, 128)
    bias = conv_bias[None]
    gate = gates(coarse, conv_weight, bias, small)
    return finish(parts, *gate, own, far_bottom, far_top, before, after, bias)[None]


def solution(mesh):
    split = Mesh(mesh.devices.reshape(16, 2, 2, 4), ("tok", "zhi", "core", "seq"))
    placed = (
        P(None, "tok", ("zhi", "core", "seq")),
        P(("zhi", "core", "seq"), None),
        P("tok", None),
        P("tok", ROW, "seq", None),
        P(),
        P(),
        P(),
    )
    return jax.shard_map(
        on_device,
        mesh=split,
        in_specs=placed,
        out_specs=P("tok", ROW, "seq", None),
        check_vma=False,
    )
```

```python
import jax
import jax.numpy as jnp
from jax import lax
from jax.experimental import pallas as pl
from jax.experimental.pallas import tpu as pltpu
from jax.sharding import Mesh
from jax.sharding import PartitionSpec as P

PIXEL_STD = (0.26862954, 0.26130258, 0.27577711)
BF16 = jnp.bfloat16
F32 = jnp.float32
VIEWS = 4
TILE_PIX = 68
SPAN = 128
HALF_TILE = 34
BAND = 80
PACKED = 112
FAR = 64
CORNERS = 16
PITCH = 48
NT = (((1,), (1,)), ((), ()))
TN = (((0,), (0,)), ((), ()))
VMEM_LIMIT = 16 * 2**20
WHOLE_VMEM = 60 * 2**20
IN_HBM = pl.BlockSpec(memory_space=pltpu.HBM)
IN_VMEM = pl.BlockSpec(memory_space=pltpu.VMEM)


def iota(shape, axis):
    return lax.broadcasted_iota(jnp.int32, shape, axis)


def dot(a, b, dims=(((1,), (0,)), ((), ()))):
    return lax.dot_general(a, b, dims, preferred_element_type=F32)


def fetch(semaphores, pairs):
    copies = [pltpu.make_async_copy(src, dst, semaphores.at[k]) for k, (src, dst) in enumerate(pairs)]
    for copy in copies:
        copy.start()
    return copies


def as_bf16(mask):
    return jnp.where(mask, 1.0, 0.0).astype(BF16)


def pair_kernel(reward, out):
    for pair in range(32):
        out[pair] = jnp.concatenate([reward[2 * pair], reward[2 * pair + 1]], axis=1)


def view_pairs(reward):
    return pl.pallas_call(
        pair_kernel,
        out_shape=jax.ShapeDtypeStruct((32, 16, SPAN), BF16),
        compiler_params=pltpu.CompilerParams(vmem_limit_bytes=VMEM_LIMIT),
        name="pairs",
    )(reward)


def place_kernel(offsets, reward, other, spread, ends, out, flat, left, strips, across, canvas, packed, rows):
    own, theirs = [each[...].astype(F32).reshape(512, SPAN) for each in (reward, other)]
    low = iota((512, SPAN), 1) < 64
    flat[0] = jnp.where(low, own, pltpu.roll(theirs, 64, 1))
    flat[1] = jnp.where(low, pltpu.roll(own, 64, 1), theirs)
    for view in range(VIEWS):
        for patch in range(16):
            top = (patch // 4) * 64 + view * 16
            side = (patch % 4) * SPAN
            values = flat[view % 2, pl.ds((view // 2) * 16 + patch, 16, stride=32), :]
            left[top : top + 16, side : side + SPAN] = values.astype(BF16)
    low = iota((64, SPAN), 1) < 64
    own_group = ((iota((256, 512), 0) >> 4) & 3) == (iota((256, 512), 1) >> 7)
    for quad in range(11):
        blocks = [jnp.concatenate([spread[4 * quad + k]] * 4, axis=0) for k in range(4)]
        weights = jnp.concatenate([jnp.concatenate(blocks, axis=0)] * 4, axis=1)
        part = dot(left[...], jnp.where(own_group, weights, jnp.zeros((256, 512), BF16)), NT)
        for member in range(2):
            own = [part[64 * h : 64 * h + 64, member * SPAN : (member + 1) * SPAN] for h in range(4)]
            turned = [pltpu.roll(piece, 64, 1) for piece in own]
            for odd in range(2):
                start = (4 * quad + 2 * member + odd) * 16
                for side in range(2):
                    a, b = 2 * side, 2 * side + 1
                    if odd == 0:
                        joined = jnp.where(low, own[a], turned[b]).astype(BF16)
                    else:
                        joined = jnp.where(low, turned[a], own[b]).astype(BF16)
                    for view in range(VIEWS):
                        strips[view, start : start + 16, side * SPAN : (side + 1) * SPAN] = joined[
                            view * 16 : view * 16 + 16
                        ]
    slot, lane = iota((256, 512), 0), iota((256, 512), 1)
    gap = (lane >> 7) * 64 - 2 + (lane & 127) - (slot >> 4) * 14 - (slot & 15)
    gap = jnp.where(((slot & 15) < 14) & ((lane & 127) < TILE_PIX), gap, -1000)
    for view in range(VIEWS):
        cols = as_bf16(gap == offsets[1, view])
        for channel in range(3):
            across[channel, view * 224 : (view + 1) * 224, :] = dot(
                strips[view, channel * 224 : (channel + 1) * 224, :], cols
            ).astype(BF16)
    step, index = iota((BAND, 896), 0), iota((1, 896), 1)
    local, corner = index, jnp.zeros((1, 896), jnp.int32) + offsets[0, 0]
    for view in range(1, VIEWS):
        local = jnp.where(index >= 224 * view, index - 224 * view, local)
        corner = jnp.where(index >= 224 * view, offsets[0, view], corner)
    first = corner + 14 * (local & 15) + (local >> 4)
    core = lax.axis_index("core")
    for high in range(2):
        y = step + (64 * (2 * high + core) - 2)
        hit = as_bf16((y == first) & (step < TILE_PIX))
        rows[high * BAND : (high + 1) * BAND, :] = hit
    for channel in range(3):
        canvas[channel] = dot(rows[...], across[channel])
    lane = iota((HALF_TILE, SPAN), 1)
    wide_lane = iota((BAND, SPAN), 1)
    for high in range(2):
        for column in range(4):
            side = slice(column * SPAN, (column + 1) * SPAN)
            top = high * BAND
            for channel in range(3):
                upper = canvas[channel, top : top + HALF_TILE, side]
                lower = pltpu.roll(canvas[channel, top + HALF_TILE : top + 2 * HALF_TILE, side], 64, 1)
                packed[channel * HALF_TILE : (channel + 1) * HALF_TILE, :] = jnp.where(lane < 64, upper, lower)
            last = [canvas[channel, top : top + BAND, side] for channel in range(3)]
            joined = jnp.where(wide_lane < 68, last[0], pltpu.roll(last[1], 4, 1))
            joined = jnp.where(wide_lane < 72, joined, pltpu.roll(last[2], 8, 1))
            rest = None
            for block in range(7):
                piece = pltpu.roll(joined[block * 10 : block * 10 + 10], (64 + block * 12) % SPAN, 1)
                rest = piece if block == 0 else jnp.where(wide_lane[:10] < block * 12, rest, piece)
            packed[3 * HALF_TILE :, :] = rest
            out[high * 4 + column, 0:PACKED, :] = packed[...].astype(BF16)
            out[high * 4 + column, PACKED:, :] = ends[high * 4 + column]


def place_partials(offsets, reward, other, spread, ends):
    return pl.pallas_call(
        place_kernel,
        out_shape=jax.ShapeDtypeStruct((8, PACKED + FAR + CORNERS, SPAN), BF16),
        in_specs=[pl.BlockSpec(memory_space=pltpu.SMEM)] + [IN_VMEM] * 4,
        scratch_shapes=[
            pltpu.VMEM((2, 512, SPAN), F32),
            pltpu.VMEM((256, 512), BF16),
            pltpu.VMEM((VIEWS, 704, 256), BF16),
            pltpu.VMEM((3, 896, 512), BF16),
            pltpu.VMEM((3, 2 * BAND, 512), F32),
            pltpu.VMEM((PACKED, SPAN), F32),
            pltpu.VMEM((2 * BAND, 896), BF16),
        ],
        compiler_params=pltpu.CompilerParams(vmem_limit_bytes=VMEM_LIMIT),
        name="place",
    )(offsets, reward, other, spread, ends)


def edge_kernel(
    features_hbm, weight_hbm, other_hbm, top_hbm, bottom_hbm,
    spread, own, out, features, weights, halves, semaphores,
):
    high, core, column = lax.axis_index("zhi"), lax.axis_index("core"), lax.axis_index("seq")
    pairs = [(weight_hbm, weights.at[0]), (other_hbm, weights.at[1])]
    pairs += [(top_hbm, own.at[4:5]), (bottom_hbm, own.at[5:6]), (features_hbm, features)]
    copies = fetch(semaphores, pairs)
    copies[0].wait()
    copies[1].wait()
    slot = iota((704, 588), 0)
    pick = as_bf16(((slot >> 4) * 14 + (slot & 15) == iota((704, 588), 1)) & ((slot & 15) < 14))
    both = jnp.concatenate([weights[0], weights[1]], axis=0)
    spread[...] = dot(pick, both, NT).astype(BF16).reshape(44, 16, SPAN)
    for copy in copies[2:]:
        copy.wait()
    top, bottom = own[4].astype(F32), own[5].astype(F32)
    far = jnp.where(core == 0, bottom, top)
    nothing = jnp.zeros((8, SPAN), F32)

    def put_ends(slot, above, below):
        rows = [each[:, k * SPAN : (k + 1) * SPAN] for k in range(4) for each in (above, below)]
        out[slot, FAR:, :] = jnp.concatenate(rows + [nothing], axis=0).astype(BF16)

    out[...] = jnp.zeros_like(out)
    own[0] = features[0]
    own[1] = features[31]
    across = jnp.where(
        high == 0,
        jnp.where(core == 0, bottom, own[1].astype(F32)),
        jnp.where(core == 1, top, own[0].astype(F32)),
    )
    half = jnp.where(core == high, across[0:16], across[16:32]).astype(BF16)
    for k in range(4):
        out[(1 - high) * 4 + column, 16 * k : 16 * k + 16, :] = half[:, k * SPAN : (k + 1) * SPAN]
    for index, (step, side, row, end) in enumerate(((-1, 0, 0, 0), (1, 16, 15, 31))):
        parts = []
        for k in range(4):
            lanes = slice(k * SPAN, (k + 1) * SPAN)
            halves[k] = features[:, side : side + 16, lanes].astype(F32).reshape(512, SPAN)
            parts.append(halves[k, pl.ds(row, 32, stride=16), :])
        own[2 + index] = jnp.concatenate(parts, axis=1).astype(BF16)
        there = jnp.clip(column + step, 0, 3)

        @pl.when(there != column)
        def _():
            put_ends(high * 4 + there, bottom[end : end + 1], top[end : end + 1])
            put_ends((1 - high) * 4 + there, far[end : end + 1], far[end : end + 1])


def edges_of(features, weight, other_weight, partner_top, partner_bottom):
    return pl.pallas_call(
        edge_kernel,
        out_shape=(
            jax.ShapeDtypeStruct((44, 16, SPAN), BF16),
            jax.ShapeDtypeStruct((6, 32, 512), BF16),
            jax.ShapeDtypeStruct((8, FAR + CORNERS, SPAN), BF16),
        ),
        in_specs=[IN_HBM] * 5,
        scratch_shapes=[
            pltpu.VMEM((32, 32, 512), BF16),
            pltpu.VMEM((2, 64, 588), BF16),
            pltpu.VMEM((4, 512, SPAN), F32),
            pltpu.SemaphoreType.DMA((5,)),
        ],
        compiler_params=pltpu.CompilerParams(vmem_limit_bytes=48 * 2**20),
        name="edges",
    )(features, weight, other_weight, partner_top, partner_bottom)


def inverse_haar(values):
    smooth, vertical, horizontal, diagonal = [values[:, k * 128 : (k + 1) * 128].astype(F32) for k in range(4)]
    upper_sum = smooth + vertical
    lower_sum = smooth - vertical
    upper_diff = horizontal + diagonal
    lower_diff = horizontal - diagonal
    return [
        0.5 * (upper_sum + upper_diff),
        0.5 * (upper_sum - upper_diff),
        0.5 * (lower_sum + lower_diff),
        0.5 * (lower_sum - lower_diff),
    ]


def slope_of(pre):
    sigmoid = 0.5 + 0.5 * jnp.tanh(0.5 * pre)
    return sigmoid * (1.0 + pre * (1.0 - sigmoid))


def gate_kernel(
    features_hbm, weight_hbm, bias, out_weight,
    out, back, kernel, taps, features, weight, fine, near, far, small, semaphores,
):
    copies = fetch(semaphores, [(features_hbm, features), (weight_hbm, weight)])
    copies[0].wait()

    @pl.loop(0, 32, unroll=4)
    def _(line):
        for k, phase in enumerate(inverse_haar(features[line])):
            fine[line + 1, 8:40, k * 128 : (k + 1) * 128] = phase

    copies[1].wait()

    @pl.loop(0, 34, unroll=2)
    def _(line):
        start = pl.multiple_of(line * PITCH, PITCH)
        near[pl.ds(start, PITCH), :] = fine[line, 7:55, :].astype(BF16)
        far[pl.ds(start, PITCH), :] = fine[line, 8:56, :].astype(BF16)

    nothing = jnp.zeros((128, 128), BF16)
    for a in range(3):
        for u in range(4):
            start = (a * 4 + u) * 128
            taps[start : start + 128, 0:128] = weight[a, u] if u < 3 else nothing
            taps[start : start + 128, 128:] = weight[a, u - 1] if u > 0 else nothing
    wide_bias = jnp.concatenate([bias[...], bias[...]], axis=1)
    count = 11 * PITCH
    for chunk in range(3):
        for phase in range(2):
            pieces = []
            for a in range(3):
                lines, parity = divmod(phase + a, 2)
                start = chunk * count + lines * PITCH
                for source in (near, far):
                    pieces.append(source[start : start + count, parity * 256 : (parity + 1) * 256])
            slope = slope_of(dot(jnp.concatenate(pieces, axis=1), taps[...]) + wide_bias)
            here = chunk * count
            out[here : here + count, phase * 256 : (phase + 1) * 256] = slope.astype(BF16)
    for a in range(3):
        for u in range(4):
            start = (a * 4 + u) * 128
            for q in range(2):
                b = q + 2 - u
                block = weight[a, b].astype(F32).T.astype(BF16) if 0 <= b <= 2 else nothing
                back[start : start + 128, q * 128 : (q + 1) * 128] = block
    slot = iota((64, 32), 0)
    small[...] = jnp.zeros_like(small)
    for k in range(9):
        small[3 * k : 3 * k + 3, :] = out_weight[k].astype(F32)
    for k in range(4):
        a, b = k // 2 + 2 - (slot & 3), k % 2 + 2 - (slot >> 4)
        channel = (slot >> 2) & 3
        valid = (a >= 0) & (a <= 2) & (b >= 0) & (b <= 2) & (channel < 3)
        window = as_bf16((iota((64, 32), 1) == a * 9 + b * 3 + channel) & valid)
        kernel[:, k * 128 : (k + 1) * 128] = dot(window, small[...].astype(BF16)).astype(BF16)


def gates(features, weight, bias, out_weight):
    return pl.pallas_call(
        gate_kernel,
        out_shape=(
            jax.ShapeDtypeStruct((33 * PITCH, 512), BF16),
            jax.ShapeDtypeStruct((1536, 256), BF16),
            jax.ShapeDtypeStruct((64, 512), BF16),
            jax.ShapeDtypeStruct((1536, 256), BF16),
        ),
        in_specs=[IN_HBM] * 2 + [IN_VMEM] * 2,
        scratch_shapes=[
            pltpu.VMEM((32, 32, 512), BF16),
            pltpu.VMEM((3, 3, 128, 128), BF16),
            pltpu.VMEM((34, 56, 512), F32),
            pltpu.VMEM((34 * PITCH, 512), BF16),
            pltpu.VMEM((34 * PITCH, 512), BF16),
            pltpu.VMEM((32, 128), F32),
            pltpu.SemaphoreType.DMA((2,)),
        ],
        compiler_params=pltpu.CompilerParams(vmem_limit_bytes=WHOLE_VMEM),
        cost_estimate=pl.CostEstimate(flops=5 * 10**9, bytes_accessed=4 * 10**6, transcendentals=2 * 10**6),
        name="gate",
    )(features, weight, bias, out_weight)


def ring_gates(parts, own, handed, sides, bias, taps, strips):
    high, core, column = lax.axis_index("zhi"), lax.axis_index("core"), lax.axis_index("seq")
    other = (1 - high) * 4

    def ends(slot):
        rows = parts[slot, PACKED + FAR :, :].astype(F32)
        return [jnp.concatenate([rows[2 * k + e : 2 * k + e + 1] for k in range(4)], axis=1) for e in range(2)]

    def only(condition, values):
        return jnp.where(condition, values, 0.0)

    lines = [own[k].astype(F32) for k in range(6)]
    halves = []
    for k in range(4):
        first = parts[other + column, PACKED + 16 * k : PACKED + 16 * k + 16, :].astype(F32)
        halves.append(jnp.concatenate([first, handed[0, 16 * k : 16 * k + 16, :].astype(F32)], axis=0))
    distant = jnp.concatenate(halves, axis=1)
    above = jnp.where(core == 1, lines[5], only(high == 1, distant))
    below = jnp.where(core == 0, lines[4], only(high == 0, distant))
    sides = [sides[k].astype(F32) for k in range(2)]
    corners = []
    for step in (-1, 1):
        there = jnp.clip(column + step, 0, 3)
        inside = there != column
        near_ends, far_ends = ends(high * 4 + there), ends(other + there)
        corners.append(
            [
                only(inside, jnp.where(core == 1, near_ends[0], only(high == 1, far_ends[0]))),
                only(inside, jnp.where(core == 0, near_ends[1], only(high == 0, far_ends[1]))),
            ]
        )
    put = [
        (above, corners[0][0], corners[1][0]),
        (lines[0], sides[0][0:1], sides[1][0:1]),
        (lines[1], sides[0][31:32], sides[1][31:32]),
        (below, corners[0][1], corners[1][1]),
        (sides[0], corners[0][0], corners[0][1]),
        (lines[2], above[0:1], below[0:1]),
        (lines[3], above[31:32], below[31:32]),
        (sides[1], corners[1][0], corners[1][1]),
    ]
    for k, (middle, first, last) in enumerate(put):
        strips[k, 0:8, :] = jnp.zeros((8, 512), F32)
        strips[k, 40:56, :] = jnp.zeros((16, 512), F32)
        for at, values in ((8, middle), (7, first), (40, last)):
            for q, phase in enumerate(inverse_haar(values)):
                strips[k, at : at + values.shape[0], q * 128 : (q + 1) * 128] = phase
    shifted = [[strips[k, 7 + d : 55 + d, :].astype(BF16) for d in range(2)] for k in range(8)]
    wide_bias = jnp.concatenate([bias[...], bias[...]], axis=1)
    found = []
    for phase in range(2):
        stack = []
        for strip in range(4):
            pieces = []
            for a in range(3):
                step, parity = divmod(phase + a, 2)
                for turn in range(2):
                    if strip < 2:
                        source = shifted[2 * strip + step][turn]
                    else:
                        source = shifted[2 * strip + turn][step]
                    pieces.append(source[:, parity * 256 : (parity + 1) * 256])
            stack.append(jnp.concatenate(pieces, axis=1))
        found.append(slope_of(dot(jnp.concatenate(stack, axis=0), taps[...]) + wide_bias))
    rings = [
        jnp.concatenate([each[strip * PITCH : (strip + 1) * PITCH] for each in found], axis=1) for strip in range(4)
    ]
    at, lane = iota((PITCH, 512), 0), iota((PITCH, 512), 1)
    even, upper = (lane & 255) < 128, lane < 256
    left = (column == 0) & even
    right = (column == 3) & jnp.logical_not(even)
    beside = (left & (at == 0)) | (right & (at == 32))
    first_line = (high == 0) & (core == 0) & upper
    last_line = (high == 1) & (core == 1) & jnp.logical_not(upper)
    masks = [beside | first_line, beside | last_line, left, right]
    return [jnp.where(mask, 0.0, ring) for mask, ring in zip(masks, rings)]


def finish_kernel(
    parts, gate_hbm, back_hbm, kernel_hbm, taps_hbm, own_hbm, handed_hbm, before_hbm, after_hbm, bias_hbm,
    out, gate, back, kernel, taps, own, handed, sides, bias, strips, columns, pixels, edges, total, stacked, near, far, semaphores,
):
    pairs = [(own_hbm, own), (bias_hbm, bias), (handed_hbm, handed)]
    pairs += [(before_hbm, sides.at[0]), (after_hbm, sides.at[1]), (taps_hbm, taps), (kernel_hbm, kernel)]
    pairs += [(gate_hbm, gate), (back_hbm, back)]
    copies = fetch(semaphores, pairs)
    sums = parts[0, 0:PACKED, :].astype(F32)
    for source in range(1, 8):
        sums = sums + parts[source, 0:PACKED, :].astype(F32)
    total[...] = sums
    pixels[...] = jnp.zeros_like(pixels)
    edges[...] = jnp.zeros_like(edges)
    for channel in range(3):
        top = channel * 80
        half = total[channel * HALF_TILE : (channel + 1) * HALF_TILE, :] / PIXEL_STD[channel]
        pixels[top : top + HALF_TILE, :] = half
        pixels[top + HALF_TILE : top + 2 * HALF_TILE, :] = pltpu.roll(half, 64, 1)
        rest = total[3 * HALF_TILE :, :] / PIXEL_STD[channel]
        for block in range(7):
            turn = (64 - block * 12 - channel * 4) % SPAN
            edges[top + block * 10 : top + block * 10 + 10, :] = pltpu.roll(rest, turn, 1)
    rounded = jnp.where(iota((240, SPAN), 1) < 64, pixels[...], edges[...]).astype(BF16)
    picked = None
    x, lane = iota((SPAN, 512), 0), iota((SPAN, 512), 1)
    row, y = iota((176, 240), 0), iota((176, 240), 1)
    for third in range(3):
        j = (lane & 127) - 40 * third
        spread = as_bf16((x == 2 * j + (lane >> 7)) & (j >= 0) & (j < 33))
        channel = (row >> 2) & 3
        lines = as_bf16((y == channel * 80 + 2 * (3 * (row >> 4) + third) + (row & 3)) & (channel < 3))
        moved = dot(rounded, spread).astype(BF16)
        term = dot(lines, moved)
        picked = term if picked is None else picked + term
    picked = picked.astype(BF16)
    for line in range(11):
        for k in range(4):
            stacked[line, k * 16 : k * 16 + 16, :] = picked[line * 16 : line * 16 + 16, k * SPAN : (k + 1) * SPAN]
    for copy in copies[:7]:
        copy.wait()
    rings = ring_gates(parts, own, handed, sides, bias, taps, strips)
    columns[0] = rings[2]
    columns[1] = rings[3]
    copies[7].wait()
    at = iota((PITCH, 512), 0)
    for line in range(11):
        act = dot(stacked[line], kernel[...], TN)
        for third in range(3):
            index = line * 3 + third
            if index == 0:
                scale = rings[0]
            elif index == 32:
                scale = rings[1]
            else:
                scale = gate[index * PITCH : (index + 1) * PITCH, :].astype(F32)
                scale = jnp.where(at == 0, columns[0, index : index + 1, :], scale)
                scale = jnp.where(at == 32, columns[1, index : index + 1, :], scale)
            grad = act[third * 40 : third * 40 + 40] * scale[0:40]
            near[index * 32 : (index + 1) * 32, :] = grad[0:32].astype(BF16)
            far[index * 32 : (index + 1) * 32, :] = grad[1:33].astype(BF16)
    copies[8].wait()
    for chunk in range(4):
        stack = []
        for p in range(2):
            pieces = []
            for a in range(3):
                step, parity = divmod(p + 2 - a, 2)
                start = chunk * 256 + step * 32
                for source in (near, far):
                    pieces.append(source[start : start + 256, parity * 256 : (parity + 1) * 256])
            stack.append(jnp.concatenate(pieces, axis=1))
        found = dot(jnp.concatenate(stack, axis=0), back[...])
        plus, minus = found[:256] + found[256:], found[:256] - found[256:]
        bands = [
            plus[:, :128] + plus[:, 128:],
            minus[:, :128] + minus[:, 128:],
            plus[:, :128] - plus[:, 128:],
            minus[:, :128] - minus[:, 128:],
        ]
        for k, band in enumerate(bands):
            out[chunk * 8 : chunk * 8 + 8, :, k * 128 : (k + 1) * 128] = (0.5 * band).astype(BF16).reshape(8, 32, 128)


def finish(parts, gate, back, kernel, taps, *rest):
    return pl.pallas_call(
        finish_kernel,
        out_shape=jax.ShapeDtypeStruct((32, 32, 512), BF16),
        in_specs=[IN_VMEM] + [IN_HBM] * 9,
        scratch_shapes=[
            pltpu.VMEM((33 * PITCH, 512), BF16),
            pltpu.VMEM((1536, 256), BF16),
            pltpu.VMEM((64, 512), BF16),
            pltpu.VMEM((1536, 256), BF16),
            pltpu.VMEM((6, 32, 512), BF16),
            pltpu.VMEM((1, FAR, SPAN), BF16),
            pltpu.VMEM((2, 32, 512), BF16),
            pltpu.VMEM((1, 128), F32),
            pltpu.VMEM((8, 56, 512), F32),
            pltpu.VMEM((2, PITCH, 512), F32),
            pltpu.VMEM((240, SPAN), F32),
            pltpu.VMEM((240, SPAN), F32),
            pltpu.VMEM((PACKED, SPAN), F32),
            pltpu.VMEM((11, 64, SPAN), BF16),
            pltpu.VMEM((33 * 32, 512), BF16),
            pltpu.VMEM((33 * 32, 512), BF16),
            pltpu.SemaphoreType.DMA((9,)),
        ],
        compiler_params=pltpu.CompilerParams(vmem_limit_bytes=WHOLE_VMEM),
        name="finish",
    )(parts, gate, back, kernel, taps, *rest)


SWAP = [(0, 1), (1, 0)]
ROW = ("zhi", "core")


def on_device(reward_grad, embed_weight, crop_offsets, features, conv_weight, conv_bias, out_weight):
    mine = lax.all_to_all(view_pairs(reward_grad), "tok", split_axis=0, concat_axis=0, tiled=True)
    other_weight = lax.ppermute(embed_weight, "core", SWAP)
    coarse = features[0]
    partner_top = lax.ppermute(coarse[:1], "core", SWAP)
    partner_bottom = lax.ppermute(coarse[31:], "core", SWAP)
    spread, own, ends = edges_of(coarse, embed_weight, other_weight, partner_top, partner_bottom)
    mine, spread, ends, own = lax.optimization_barrier((mine, spread, ends, own))
    partials = place_partials(crop_offsets.T, mine, lax.ppermute(mine, "core", SWAP), spread, ends)
    partials, coarse, own = lax.optimization_barrier((partials, coarse, own))
    parts = lax.all_to_all(partials, ("zhi", "seq"), split_axis=0, concat_axis=0, tiled=True)
    before = lax.ppermute(own[3], "seq", [(i, i + 1) for i in range(3)])
    after = lax.ppermute(own[2], "seq", [(i + 1, i) for i in range(3)])
    small = out_weight.transpose(0, 1, 3, 2).reshape(9, 3, 128)
    bias = conv_bias[None]
    gate = gates(coarse, conv_weight, bias, small)
    parts, gate, before, after = lax.optimization_barrier((parts, gate, before, after))
    slot = (1 - lax.axis_index("zhi")) * 4 + lax.axis_index("seq")
    handed = lax.ppermute(lax.dynamic_slice(parts, (slot, PACKED, 0), (1, FAR, SPAN)), "core", SWAP)
    return finish(parts, *gate, own, handed, before, after, bias)[None]


def solution(mesh):
    split = Mesh(mesh.devices.reshape(16, 2, 2, 4), ("tok", "zhi", "core", "seq"))
    placed = (
        P(None, "tok", ("zhi", "core", "seq")),
        P(("zhi", "core", "seq"), None),
        P("tok", None),
        P("tok", ROW, "seq", None),
        P(),
        P(),
        P(),
    )
    return jax.shard_map(
        on_device,
        mesh=split,
        in_specs=placed,
        out_specs=P("tok", ROW, "seq", None),
        check_vma=False,
    )
```

```python
import jax
import jax.numpy as jnp
from jax import lax
from jax.experimental import pallas as pl
from jax.experimental.pallas import tpu as pltpu
from jax.sharding import Mesh
from jax.sharding import PartitionSpec as P

PIXEL_STD = (0.26862954, 0.26130258, 0.27577711)
BF16 = jnp.bfloat16
F32 = jnp.float32
VIEWS = 4
TILE_PIX = 68
SPAN = 128
HALF_TILE = 34
BAND = 80
PACKED = 112
FAR = 64
CORNERS = 16
PITCH = 48
NT = (((1,), (1,)), ((), ()))
TN = (((0,), (0,)), ((), ()))
VMEM_LIMIT = 16 * 2**20
WHOLE_VMEM = 60 * 2**20
IN_HBM = pl.BlockSpec(memory_space=pltpu.HBM)
IN_VMEM = pl.BlockSpec(memory_space=pltpu.VMEM)


def iota(shape, axis):
    return lax.broadcasted_iota(jnp.int32, shape, axis)


def dot(a, b, dims=(((1,), (0,)), ((), ()))):
    return lax.dot_general(a, b, dims, preferred_element_type=F32)


def fetch(semaphores, pairs):
    copies = [pltpu.make_async_copy(src, dst, semaphores.at[k]) for k, (src, dst) in enumerate(pairs)]
    for copy in copies:
        copy.start()
    return copies


def as_bf16(mask):
    return jnp.where(mask, 1.0, 0.0).astype(BF16)


def pair_kernel(reward, out):
    for pair in range(32):
        out[pair] = jnp.concatenate([reward[2 * pair], reward[2 * pair + 1]], axis=1)


def view_pairs(reward):
    return pl.pallas_call(
        pair_kernel,
        out_shape=jax.ShapeDtypeStruct((32, 16, SPAN), BF16),
        compiler_params=pltpu.CompilerParams(vmem_limit_bytes=VMEM_LIMIT),
        name="pairs",
    )(reward)


def place_kernel(offsets, reward, other, spread, ends, out, flat, left, strips, across, canvas, packed, rows):
    own, theirs = [each[...].astype(F32).reshape(512, SPAN) for each in (reward, other)]
    low = iota((512, SPAN), 1) < 64
    flat[0] = jnp.where(low, own, pltpu.roll(theirs, 64, 1))
    flat[1] = jnp.where(low, pltpu.roll(own, 64, 1), theirs)
    for view in range(VIEWS):
        for patch in range(16):
            top = (patch // 4) * 64 + view * 16
            side = (patch % 4) * SPAN
            values = flat[view % 2, pl.ds((view // 2) * 16 + patch, 16, stride=32), :]
            left[top : top + 16, side : side + SPAN] = values.astype(BF16)
    low = iota((64, SPAN), 1) < 64
    own_group = ((iota((256, 512), 0) >> 4) & 3) == (iota((256, 512), 1) >> 7)
    for quad in range(11):
        blocks = [jnp.concatenate([spread[4 * quad + k]] * 4, axis=0) for k in range(4)]
        weights = jnp.concatenate([jnp.concatenate(blocks, axis=0)] * 4, axis=1)
        part = dot(left[...], jnp.where(own_group, weights, jnp.zeros((256, 512), BF16)), NT)
        for member in range(2):
            own = [part[64 * h : 64 * h + 64, member * SPAN : (member + 1) * SPAN] for h in range(4)]
            turned = [pltpu.roll(piece, 64, 1) for piece in own]
            for odd in range(2):
                start = (4 * quad + 2 * member + odd) * 16
                for side in range(2):
                    a, b = 2 * side, 2 * side + 1
                    if odd == 0:
                        joined = jnp.where(low, own[a], turned[b]).astype(BF16)
                    else:
                        joined = jnp.where(low, turned[a], own[b]).astype(BF16)
                    for view in range(VIEWS):
                        strips[view, start : start + 16, side * SPAN : (side + 1) * SPAN] = joined[
                            view * 16 : view * 16 + 16
                        ]
    slot, lane = iota((256, 512), 0), iota((256, 512), 1)
    gap = (lane >> 7) * 64 - 2 + (lane & 127) - (slot >> 4) * 14 - (slot & 15)
    gap = jnp.where(((slot & 15) < 14) & ((lane & 127) < TILE_PIX), gap, -1000)
    for view in range(VIEWS):
        cols = as_bf16(gap == offsets[1, view])
        for channel in range(3):
            across[channel, view * 224 : (view + 1) * 224, :] = dot(
                strips[view, channel * 224 : (channel + 1) * 224, :], cols
            ).astype(BF16)
    step, index = iota((BAND, 896), 0), iota((1, 896), 1)
    local, corner = index, jnp.zeros((1, 896), jnp.int32) + offsets[0, 0]
    for view in range(1, VIEWS):
        local = jnp.where(index >= 224 * view, index - 224 * view, local)
        corner = jnp.where(index >= 224 * view, offsets[0, view], corner)
    first = corner + 14 * (local & 15) + (local >> 4)
    core = lax.axis_index("core")
    for high in range(2):
        y = step + (64 * (2 * high + core) - 2)
        hit = as_bf16((y == first) & (step < TILE_PIX))
        rows[high * BAND : (high + 1) * BAND, :] = hit
    for channel in range(3):
        canvas[channel] = dot(rows[...], across[channel])
    lane = iota((HALF_TILE, SPAN), 1)
    wide_lane = iota((BAND, SPAN), 1)
    for high in range(2):
        for column in range(4):
            side = slice(column * SPAN, (column + 1) * SPAN)
            top = high * BAND
            for channel in range(3):
                upper = canvas[channel, top : top + HALF_TILE, side]
                lower = pltpu.roll(canvas[channel, top + HALF_TILE : top + 2 * HALF_TILE, side], 64, 1)
                packed[channel * HALF_TILE : (channel + 1) * HALF_TILE, :] = jnp.where(lane < 64, upper, lower)
            last = [canvas[channel, top : top + BAND, side] for channel in range(3)]
            joined = jnp.where(wide_lane < 68, last[0], pltpu.roll(last[1], 4, 1))
            joined = jnp.where(wide_lane < 72, joined, pltpu.roll(last[2], 8, 1))
            rest = None
            for block in range(7):
                piece = pltpu.roll(joined[block * 10 : block * 10 + 10], (64 + block * 12) % SPAN, 1)
                rest = piece if block == 0 else jnp.where(wide_lane[:10] < block * 12, rest, piece)
            packed[3 * HALF_TILE :, :] = rest
            out[high * 4 + column, 0:PACKED, :] = packed[...].astype(BF16)
            out[high * 4 + column, PACKED:, :] = ends[high * 4 + column]


def place_partials(offsets, reward, other, spread, ends):
    return pl.pallas_call(
        place_kernel,
        out_shape=jax.ShapeDtypeStruct((8, PACKED + FAR + CORNERS, SPAN), BF16),
        in_specs=[pl.BlockSpec(memory_space=pltpu.SMEM)] + [IN_VMEM] * 4,
        scratch_shapes=[
            pltpu.VMEM((2, 512, SPAN), F32),
            pltpu.VMEM((256, 512), BF16),
            pltpu.VMEM((VIEWS, 704, 256), BF16),
            pltpu.VMEM((3, 896, 512), BF16),
            pltpu.VMEM((3, 2 * BAND, 512), F32),
            pltpu.VMEM((PACKED, SPAN), F32),
            pltpu.VMEM((2 * BAND, 896), BF16),
        ],
        compiler_params=pltpu.CompilerParams(vmem_limit_bytes=VMEM_LIMIT),
        name="place",
    )(offsets, reward, other, spread, ends)


def edge_kernel(
    features_hbm, weight_hbm, other_hbm, top_hbm, bottom_hbm,
    spread, own, out, features, weights, halves, semaphores,
):
    high, core, column = lax.axis_index("zhi"), lax.axis_index("core"), lax.axis_index("seq")
    pairs = [(weight_hbm, weights.at[0]), (other_hbm, weights.at[1])]
    pairs += [(top_hbm, own.at[4:5]), (bottom_hbm, own.at[5:6]), (features_hbm, features)]
    copies = fetch(semaphores, pairs)
    copies[0].wait()
    copies[1].wait()
    slot = iota((704, 588), 0)
    pick = as_bf16(((slot >> 4) * 14 + (slot & 15) == iota((704, 588), 1)) & ((slot & 15) < 14))
    both = jnp.concatenate([weights[0], weights[1]], axis=0)
    spread[...] = dot(pick, both, NT).astype(BF16).reshape(44, 16, SPAN)
    for copy in copies[2:]:
        copy.wait()
    top, bottom = own[4].astype(F32), own[5].astype(F32)
    far = jnp.where(core == 0, bottom, top)
    nothing = jnp.zeros((8, SPAN), F32)

    def put_ends(slot, above, below):
        rows = [each[:, k * SPAN : (k + 1) * SPAN] for k in range(4) for each in (above, below)]
        out[slot, FAR:, :] = jnp.concatenate(rows + [nothing], axis=0).astype(BF16)

    out[...] = jnp.zeros_like(out)
    own[0] = features[0]
    own[1] = features[31]
    across = jnp.where(
        high == 0,
        jnp.where(core == 0, bottom, own[1].astype(F32)),
        jnp.where(core == 1, top, own[0].astype(F32)),
    )
    half = jnp.where(core == high, across[0:16], across[16:32]).astype(BF16)
    for k in range(4):
        out[(1 - high) * 4 + column, 16 * k : 16 * k + 16, :] = half[:, k * SPAN : (k + 1) * SPAN]
    for index, (step, side, row, end) in enumerate(((-1, 0, 0, 0), (1, 16, 15, 31))):
        parts = []
        for k in range(4):
            lanes = slice(k * SPAN, (k + 1) * SPAN)
            halves[k] = features[:, side : side + 16, lanes].astype(F32).reshape(512, SPAN)
            parts.append(halves[k, pl.ds(row, 32, stride=16), :])
        own[2 + index] = jnp.concatenate(parts, axis=1).astype(BF16)
        there = jnp.clip(column + step, 0, 3)

        @pl.when(there != column)
        def _():
            put_ends(high * 4 + there, bottom[end : end + 1], top[end : end + 1])
            put_ends((1 - high) * 4 + there, far[end : end + 1], far[end : end + 1])


def edges_of(features, weight, other_weight, partner_top, partner_bottom):
    return pl.pallas_call(
        edge_kernel,
        out_shape=(
            jax.ShapeDtypeStruct((44, 16, SPAN), BF16),
            jax.ShapeDtypeStruct((6, 32, 512), BF16),
            jax.ShapeDtypeStruct((8, FAR + CORNERS, SPAN), BF16),
        ),
        in_specs=[IN_HBM] * 5,
        scratch_shapes=[
            pltpu.VMEM((32, 32, 512), BF16),
            pltpu.VMEM((2, 64, 588), BF16),
            pltpu.VMEM((4, 512, SPAN), F32),
            pltpu.SemaphoreType.DMA((5,)),
        ],
        compiler_params=pltpu.CompilerParams(vmem_limit_bytes=48 * 2**20),
        name="edges",
    )(features, weight, other_weight, partner_top, partner_bottom)


def inverse_haar(values):
    smooth, vertical, horizontal, diagonal = [values[:, k * 128 : (k + 1) * 128].astype(F32) for k in range(4)]
    upper_sum = smooth + vertical
    lower_sum = smooth - vertical
    upper_diff = horizontal + diagonal
    lower_diff = horizontal - diagonal
    return [
        0.5 * (upper_sum + upper_diff),
        0.5 * (upper_sum - upper_diff),
        0.5 * (lower_sum + lower_diff),
        0.5 * (lower_sum - lower_diff),
    ]


def slope_of(pre):
    sigmoid = 0.5 + 0.5 * jnp.tanh(0.5 * pre)
    return sigmoid * (1.0 + pre * (1.0 - sigmoid))


def gate_kernel(
    features_hbm, weight_hbm, bias, out_weight,
    out, back, kernel, taps, features, weight, fine, near, far, small, semaphores,
):
    copies = fetch(semaphores, [(features_hbm, features), (weight_hbm, weight)])
    copies[0].wait()

    @pl.loop(0, 32, unroll=4)
    def _(line):
        for k, phase in enumerate(inverse_haar(features[line])):
            fine[line + 1, 8:40, k * 128 : (k + 1) * 128] = phase

    copies[1].wait()

    @pl.loop(0, 34, unroll=2)
    def _(line):
        start = pl.multiple_of(line * PITCH, PITCH)
        near[pl.ds(start, PITCH), :] = fine[line, 7:55, :].astype(BF16)
        far[pl.ds(start, PITCH), :] = fine[line, 8:56, :].astype(BF16)

    nothing = jnp.zeros((128, 128), BF16)
    for a in range(3):
        for u in range(4):
            start = (a * 4 + u) * 128
            taps[start : start + 128, 0:128] = weight[a, u] if u < 3 else nothing
            taps[start : start + 128, 128:] = weight[a, u - 1] if u > 0 else nothing
    wide_bias = jnp.concatenate([bias[...], bias[...]], axis=1)
    count = 11 * PITCH
    for chunk in range(3):
        for phase in range(2):
            pieces = []
            for a in range(3):
                lines, parity = divmod(phase + a, 2)
                start = chunk * count + lines * PITCH
                for source in (near, far):
                    pieces.append(source[start : start + count, parity * 256 : (parity + 1) * 256])
            slope = slope_of(dot(jnp.concatenate(pieces, axis=1), taps[...]) + wide_bias)
            here = chunk * count
            out[here : here + count, phase * 256 : (phase + 1) * 256] = slope.astype(BF16)
    for a in range(3):
        for u in range(4):
            start = (a * 4 + u) * 128
            for q in range(2):
                b = q + 2 - u
                block = weight[a, b].astype(F32).T.astype(BF16) if 0 <= b <= 2 else nothing
                back[start : start + 128, q * 128 : (q + 1) * 128] = block
    slot = iota((64, 32), 0)
    small[...] = jnp.zeros_like(small)
    for k in range(9):
        small[3 * k : 3 * k + 3, :] = out_weight[k].astype(F32)
    for k in range(4):
        a, b = k // 2 + 2 - (slot & 3), k % 2 + 2 - (slot >> 4)
        channel = (slot >> 2) & 3
        valid = (a >= 0) & (a <= 2) & (b >= 0) & (b <= 2) & (channel < 3)
        window = as_bf16((iota((64, 32), 1) == a * 9 + b * 3 + channel) & valid)
        kernel[:, k * 128 : (k + 1) * 128] = dot(window, small[...].astype(BF16)).astype(BF16)


def gates(features, weight, bias, out_weight):
    return pl.pallas_call(
        gate_kernel,
        out_shape=(
            jax.ShapeDtypeStruct((33 * PITCH, 512), BF16),
            jax.ShapeDtypeStruct((1536, 256), BF16),
            jax.ShapeDtypeStruct((64, 512), BF16),
            jax.ShapeDtypeStruct((1536, 256), BF16),
        ),
        in_specs=[IN_HBM] * 2 + [IN_VMEM] * 2,
        scratch_shapes=[
            pltpu.VMEM((32, 32, 512), BF16),
            pltpu.VMEM((3, 3, 128, 128), BF16),
            pltpu.VMEM((34, 56, 512), F32),
            pltpu.VMEM((34 * PITCH, 512), BF16),
            pltpu.VMEM((34 * PITCH, 512), BF16),
            pltpu.VMEM((32, 128), F32),
            pltpu.SemaphoreType.DMA((2,)),
        ],
        compiler_params=pltpu.CompilerParams(vmem_limit_bytes=WHOLE_VMEM),
        cost_estimate=pl.CostEstimate(flops=5 * 10**9, bytes_accessed=4 * 10**6, transcendentals=2 * 10**6),
        name="gate",
    )(features, weight, bias, out_weight)


def ring_gates(parts, own, handed, sides, bias, taps, strips):
    high, core, column = lax.axis_index("zhi"), lax.axis_index("core"), lax.axis_index("seq")
    other = (1 - high) * 4

    def ends(slot):
        rows = parts[slot, FAR:, :].astype(F32)
        return [jnp.concatenate([rows[2 * k + e : 2 * k + e + 1] for k in range(4)], axis=1) for e in range(2)]

    def only(condition, values):
        return jnp.where(condition, values, 0.0)

    lines = [own[k].astype(F32) for k in range(6)]
    halves = []
    for k in range(4):
        first = parts[other + column, 16 * k : 16 * k + 16, :].astype(F32)
        halves.append(jnp.concatenate([first, handed[0, 16 * k : 16 * k + 16, :].astype(F32)], axis=0))
    distant = jnp.concatenate(halves, axis=1)
    above = jnp.where(core == 1, lines[5], only(high == 1, distant))
    below = jnp.where(core == 0, lines[4], only(high == 0, distant))
    sides = [sides[k].astype(F32) for k in range(2)]
    corners = []
    for step in (-1, 1):
        there = jnp.clip(column + step, 0, 3)
        inside = there != column
        near_ends, far_ends = ends(high * 4 + there), ends(other + there)
        corners.append(
            [
                only(inside, jnp.where(core == 1, near_ends[0], only(high == 1, far_ends[0]))),
                only(inside, jnp.where(core == 0, near_ends[1], only(high == 0, far_ends[1]))),
            ]
        )
    put = [
        (above, corners[0][0], corners[1][0]),
        (lines[0], sides[0][0:1], sides[1][0:1]),
        (lines[1], sides[0][31:32], sides[1][31:32]),
        (below, corners[0][1], corners[1][1]),
        (sides[0], corners[0][0], corners[0][1]),
        (lines[2], above[0:1], below[0:1]),
        (lines[3], above[31:32], below[31:32]),
        (sides[1], corners[1][0], corners[1][1]),
    ]
    for k, (middle, first, last) in enumerate(put):
        strips[k, 0:8, :] = jnp.zeros((8, 512), F32)
        strips[k, 40:56, :] = jnp.zeros((16, 512), F32)
        for at, values in ((8, middle), (7, first), (40, last)):
            for q, phase in enumerate(inverse_haar(values)):
                strips[k, at : at + values.shape[0], q * 128 : (q + 1) * 128] = phase
    shifted = [[strips[k, 7 + d : 55 + d, :].astype(BF16) for d in range(2)] for k in range(8)]
    wide_bias = jnp.concatenate([bias[...], bias[...]], axis=1)
    found = []
    for phase in range(2):
        stack = []
        for strip in range(4):
            pieces = []
            for a in range(3):
                step, parity = divmod(phase + a, 2)
                for turn in range(2):
                    if strip < 2:
                        source = shifted[2 * strip + step][turn]
                    else:
                        source = shifted[2 * strip + turn][step]
                    pieces.append(source[:, parity * 256 : (parity + 1) * 256])
            stack.append(jnp.concatenate(pieces, axis=1))
        found.append(slope_of(dot(jnp.concatenate(stack, axis=0), taps[...]) + wide_bias))
    rings = [
        jnp.concatenate([each[strip * PITCH : (strip + 1) * PITCH] for each in found], axis=1) for strip in range(4)
    ]
    at, lane = iota((PITCH, 512), 0), iota((PITCH, 512), 1)
    even, upper = (lane & 255) < 128, lane < 256
    left = (column == 0) & even
    right = (column == 3) & jnp.logical_not(even)
    beside = (left & (at == 0)) | (right & (at == 32))
    first_line = (high == 0) & (core == 0) & upper
    last_line = (high == 1) & (core == 1) & jnp.logical_not(upper)
    masks = [beside | first_line, beside | last_line, left, right]
    return [jnp.where(mask, 0.0, ring) for mask, ring in zip(masks, rings)]


def pixel_kernel(parts, stacked, pixels, edges, total):
    sums = parts[0, 0:PACKED, :].astype(F32)
    for source in range(1, 8):
        sums = sums + parts[source, 0:PACKED, :].astype(F32)
    total[...] = sums
    pixels[...] = jnp.zeros_like(pixels)
    edges[...] = jnp.zeros_like(edges)
    for channel in range(3):
        top = channel * 80
        half = total[channel * HALF_TILE : (channel + 1) * HALF_TILE, :] / PIXEL_STD[channel]
        pixels[top : top + HALF_TILE, :] = half
        pixels[top + HALF_TILE : top + 2 * HALF_TILE, :] = pltpu.roll(half, 64, 1)
        rest = total[3 * HALF_TILE :, :] / PIXEL_STD[channel]
        for block in range(7):
            turn = (64 - block * 12 - channel * 4) % SPAN
            edges[top + block * 10 : top + block * 10 + 10, :] = pltpu.roll(rest, turn, 1)
    rounded = jnp.where(iota((240, SPAN), 1) < 64, pixels[...], edges[...]).astype(BF16)
    picked = None
    x, lane = iota((SPAN, 512), 0), iota((SPAN, 512), 1)
    row, y = iota((176, 240), 0), iota((176, 240), 1)
    for third in range(3):
        j = (lane & 127) - 40 * third
        spread = as_bf16((x == 2 * j + (lane >> 7)) & (j >= 0) & (j < 33))
        channel = (row >> 2) & 3
        lines = as_bf16((y == channel * 80 + 2 * (3 * (row >> 4) + third) + (row & 3)) & (channel < 3))
        moved = dot(rounded, spread).astype(BF16)
        term = dot(lines, moved)
        picked = term if picked is None else picked + term
    picked = picked.astype(BF16)
    for line in range(11):
        for k in range(4):
            stacked[line, k * 16 : k * 16 + 16, :] = picked[line * 16 : line * 16 + 16, k * SPAN : (k + 1) * SPAN]


def pixel_windows(parts):
    return pl.pallas_call(
        pixel_kernel,
        out_shape=jax.ShapeDtypeStruct((11, 64, SPAN), BF16),
        scratch_shapes=[
            pltpu.VMEM((240, SPAN), F32),
            pltpu.VMEM((240, SPAN), F32),
            pltpu.VMEM((PACKED, SPAN), F32),
        ],
        compiler_params=pltpu.CompilerParams(vmem_limit_bytes=VMEM_LIMIT),
        name="pixels",
    )(parts)


def finish_kernel(
    parts_hbm, stacked_hbm, gate_hbm, back_hbm, kernel_hbm, taps_hbm, own_hbm, handed_hbm, before_hbm, after_hbm, bias_hbm,
    out, parts, stacked, gate, back, kernel, taps, own, handed, sides, bias, strips, columns, near, far, semaphores,
):
    pairs = [(parts_hbm.at[:, PACKED:, :], parts), (own_hbm, own), (bias_hbm, bias), (handed_hbm, handed)]
    pairs += [(before_hbm, sides.at[0]), (after_hbm, sides.at[1]), (taps_hbm, taps), (kernel_hbm, kernel)]
    pairs += [(stacked_hbm, stacked), (gate_hbm, gate), (back_hbm, back)]
    copies = fetch(semaphores, pairs)
    for copy in copies[:9]:
        copy.wait()
    rings = ring_gates(parts, own, handed, sides, bias, taps, strips)
    columns[0] = rings[2]
    columns[1] = rings[3]
    copies[9].wait()
    at = iota((PITCH, 512), 0)
    for line in range(11):
        act = dot(stacked[line], kernel[...], TN)
        for third in range(3):
            index = line * 3 + third
            if index == 0:
                scale = rings[0]
            elif index == 32:
                scale = rings[1]
            else:
                scale = gate[index * PITCH : (index + 1) * PITCH, :].astype(F32)
                scale = jnp.where(at == 0, columns[0, index : index + 1, :], scale)
                scale = jnp.where(at == 32, columns[1, index : index + 1, :], scale)
            grad = act[third * 40 : third * 40 + 40] * scale[0:40]
            near[index * 32 : (index + 1) * 32, :] = grad[0:32].astype(BF16)
            far[index * 32 : (index + 1) * 32, :] = grad[1:33].astype(BF16)
    copies[10].wait()
    for chunk in range(4):
        stack = []
        for p in range(2):
            pieces = []
            for a in range(3):
                step, parity = divmod(p + 2 - a, 2)
                start = chunk * 256 + step * 32
                for source in (near, far):
                    pieces.append(source[start : start + 256, parity * 256 : (parity + 1) * 256])
            stack.append(jnp.concatenate(pieces, axis=1))
        found = dot(jnp.concatenate(stack, axis=0), back[...])
        plus, minus = found[:256] + found[256:], found[:256] - found[256:]
        bands = [
            plus[:, :128] + plus[:, 128:],
            minus[:, :128] + minus[:, 128:],
            plus[:, :128] - plus[:, 128:],
            minus[:, :128] - minus[:, 128:],
        ]
        for k, band in enumerate(bands):
            out[chunk * 8 : chunk * 8 + 8, :, k * 128 : (k + 1) * 128] = (0.5 * band).astype(BF16).reshape(8, 32, 128)


def finish(*operands):
    return pl.pallas_call(
        finish_kernel,
        out_shape=jax.ShapeDtypeStruct((32, 32, 512), BF16),
        in_specs=[IN_HBM] * 11,
        scratch_shapes=[
            pltpu.VMEM((8, FAR + CORNERS, SPAN), BF16),
            pltpu.VMEM((11, 64, SPAN), BF16),
            pltpu.VMEM((33 * PITCH, 512), BF16),
            pltpu.VMEM((1536, 256), BF16),
            pltpu.VMEM((64, 512), BF16),
            pltpu.VMEM((1536, 256), BF16),
            pltpu.VMEM((6, 32, 512), BF16),
            pltpu.VMEM((1, FAR, SPAN), BF16),
            pltpu.VMEM((2, 32, 512), BF16),
            pltpu.VMEM((1, 128), F32),
            pltpu.VMEM((8, 56, 512), F32),
            pltpu.VMEM((2, PITCH, 512), F32),
            pltpu.VMEM((33 * 32, 512), BF16),
            pltpu.VMEM((33 * 32, 512), BF16),
            pltpu.SemaphoreType.DMA((11,)),
        ],
        compiler_params=pltpu.CompilerParams(vmem_limit_bytes=WHOLE_VMEM),
        name="finish",
    )(*operands)


SWAP = [(0, 1), (1, 0)]
ROW = ("zhi", "core")


def on_device(reward_grad, embed_weight, crop_offsets, features, conv_weight, conv_bias, out_weight):
    mine = lax.all_to_all(view_pairs(reward_grad), "tok", split_axis=0, concat_axis=0, tiled=True)
    coarse = features[0]
    top, bottom, embed_weight = lax.optimization_barrier((coarse[:1], coarse[31:], embed_weight))
    partner_top = lax.ppermute(top, "core", SWAP)
    partner_bottom = lax.ppermute(bottom, "core", SWAP)
    other_weight = lax.ppermute(embed_weight, "core", SWAP)
    spread, own, ends = edges_of(coarse, embed_weight, other_weight, partner_top, partner_bottom)
    mine, spread, ends, own = lax.optimization_barrier((mine, spread, ends, own))
    partials = place_partials(crop_offsets.T, mine, lax.ppermute(mine, "core", SWAP), spread, ends)
    partials, coarse, own = lax.optimization_barrier((partials, coarse, own))
    parts = lax.all_to_all(partials, ("zhi", "seq"), split_axis=0, concat_axis=0, tiled=True)
    before = lax.ppermute(own[3], "seq", [(i, i + 1) for i in range(3)])
    after = lax.ppermute(own[2], "seq", [(i + 1, i) for i in range(3)])
    small = out_weight.transpose(0, 1, 3, 2).reshape(9, 3, 128)
    bias = conv_bias[None]
    gate = gates(coarse, conv_weight, bias, small)
    parts, gate, before, after = lax.optimization_barrier((parts, gate, before, after))
    slot = (1 - lax.axis_index("zhi")) * 4 + lax.axis_index("seq")
    handed = lax.ppermute(lax.dynamic_slice(parts, (slot, PACKED, 0), (1, FAR, SPAN)), "core", SWAP)
    return finish(parts, pixel_windows(parts), *gate, own, handed, before, after, bias)[None]


def solution(mesh):
    split = Mesh(mesh.devices.reshape(16, 2, 2, 4), ("tok", "zhi", "core", "seq"))
    placed = (
        P(None, "tok", ("zhi", "core", "seq")),
        P(("zhi", "core", "seq"), None),
        P("tok", None),
        P("tok", ROW, "seq", None),
        P(),
        P(),
        P(),
    )
    return jax.shard_map(
        on_device,
        mesh=split,
        in_specs=placed,
        out_specs=P("tok", ROW, "seq", None),
        check_vma=False,
    )
```

```python
import jax
import jax.numpy as jnp
from jax import lax
from jax.experimental import pallas as pl
from jax.experimental.pallas import tpu as pltpu
from jax.sharding import Mesh
from jax.sharding import PartitionSpec as P

PIXEL_STD = (0.26862954, 0.26130258, 0.27577711)
BF16 = jnp.bfloat16
F32 = jnp.float32
VIEWS = 4
TILE_PIX = 68
SPAN = 128
HALF_TILE = 34
BAND = 80
PACKED = 112
FAR = 64
CORNERS = 16
PITCH = 48
NT = (((1,), (1,)), ((), ()))
TN = (((0,), (0,)), ((), ()))
VMEM_LIMIT = 16 * 2**20
WHOLE_VMEM = 60 * 2**20
IN_HBM = pl.BlockSpec(memory_space=pltpu.HBM)
IN_VMEM = pl.BlockSpec(memory_space=pltpu.VMEM)


def iota(shape, axis):
    return lax.broadcasted_iota(jnp.int32, shape, axis)


def dot(a, b, dims=(((1,), (0,)), ((), ()))):
    return lax.dot_general(a, b, dims, preferred_element_type=F32)


def fetch(semaphores, pairs):
    copies = [pltpu.make_async_copy(src, dst, semaphores.at[k]) for k, (src, dst) in enumerate(pairs)]
    for copy in copies:
        copy.start()
    return copies


def as_bf16(mask):
    return jnp.where(mask, 1.0, 0.0).astype(BF16)


def pair_kernel(reward, out):
    for pair in range(32):
        out[pair] = jnp.concatenate([reward[2 * pair], reward[2 * pair + 1]], axis=1)


def view_pairs(reward):
    return pl.pallas_call(
        pair_kernel,
        out_shape=jax.ShapeDtypeStruct((32, 16, SPAN), BF16),
        compiler_params=pltpu.CompilerParams(vmem_limit_bytes=WHOLE_VMEM),
        name="pairs",
    )(reward)


def place_kernel(offsets, reward, other, spread, ends, out, flat, left, strips, across, canvas, packed, rows):
    own, theirs = [each[...].astype(F32).reshape(512, SPAN) for each in (reward, other)]
    low = iota((512, SPAN), 1) < 64
    flat[0] = jnp.where(low, own, pltpu.roll(theirs, 64, 1))
    flat[1] = jnp.where(low, pltpu.roll(own, 64, 1), theirs)
    for view in range(VIEWS):
        for patch in range(16):
            top = (patch // 4) * 64 + view * 16
            side = (patch % 4) * SPAN
            values = flat[view % 2, pl.ds((view // 2) * 16 + patch, 16, stride=32), :]
            left[top : top + 16, side : side + SPAN] = values.astype(BF16)
    low = iota((64, SPAN), 1) < 64
    own_group = ((iota((256, 512), 0) >> 4) & 3) == (iota((256, 512), 1) >> 7)
    for quad in range(11):
        blocks = [jnp.concatenate([spread[4 * quad + k]] * 4, axis=0) for k in range(4)]
        weights = jnp.concatenate([jnp.concatenate(blocks, axis=0)] * 4, axis=1)
        part = dot(left[...], jnp.where(own_group, weights, jnp.zeros((256, 512), BF16)), NT)
        for member in range(2):
            own = [part[64 * h : 64 * h + 64, member * SPAN : (member + 1) * SPAN] for h in range(4)]
            turned = [pltpu.roll(piece, 64, 1) for piece in own]
            for odd in range(2):
                start = (4 * quad + 2 * member + odd) * 16
                for side in range(2):
                    a, b = 2 * side, 2 * side + 1
                    if odd == 0:
                        joined = jnp.where(low, own[a], turned[b]).astype(BF16)
                    else:
                        joined = jnp.where(low, turned[a], own[b]).astype(BF16)
                    for view in range(VIEWS):
                        strips[view, start : start + 16, side * SPAN : (side + 1) * SPAN] = joined[
                            view * 16 : view * 16 + 16
                        ]
    slot, lane = iota((256, 512), 0), iota((256, 512), 1)
    gap = (lane >> 7) * 64 - 2 + (lane & 127) - (slot >> 4) * 14 - (slot & 15)
    gap = jnp.where(((slot & 15) < 14) & ((lane & 127) < TILE_PIX), gap, -1000)
    for view in range(VIEWS):
        cols = as_bf16(gap == offsets[1, view])
        for channel in range(3):
            across[channel, view * 224 : (view + 1) * 224, :] = dot(
                strips[view, channel * 224 : (channel + 1) * 224, :], cols
            ).astype(BF16)
    step, index = iota((BAND, 896), 0), iota((1, 896), 1)
    local, corner = index, jnp.zeros((1, 896), jnp.int32) + offsets[0, 0]
    for view in range(1, VIEWS):
        local = jnp.where(index >= 224 * view, index - 224 * view, local)
        corner = jnp.where(index >= 224 * view, offsets[0, view], corner)
    first = corner + 14 * (local & 15) + (local >> 4)
    core = lax.axis_index("core")
    for high in range(2):
        y = step + (64 * (2 * high + core) - 2)
        hit = as_bf16((y == first) & (step < TILE_PIX))
        rows[high * BAND : (high + 1) * BAND, :] = hit
    for channel in range(3):
        canvas[channel] = dot(rows[...], across[channel])
    lane = iota((HALF_TILE, SPAN), 1)
    wide_lane = iota((BAND, SPAN), 1)
    for high in range(2):
        for column in range(4):
            side = slice(column * SPAN, (column + 1) * SPAN)
            top = high * BAND
            for channel in range(3):
                upper = canvas[channel, top : top + HALF_TILE, side]
                lower = pltpu.roll(canvas[channel, top + HALF_TILE : top + 2 * HALF_TILE, side], 64, 1)
                packed[channel * HALF_TILE : (channel + 1) * HALF_TILE, :] = jnp.where(lane < 64, upper, lower)
            last = [canvas[channel, top : top + BAND, side] for channel in range(3)]
            joined = jnp.where(wide_lane < 68, last[0], pltpu.roll(last[1], 4, 1))
            joined = jnp.where(wide_lane < 72, joined, pltpu.roll(last[2], 8, 1))
            rest = None
            for block in range(7):
                piece = pltpu.roll(joined[block * 10 : block * 10 + 10], (64 + block * 12) % SPAN, 1)
                rest = piece if block == 0 else jnp.where(wide_lane[:10] < block * 12, rest, piece)
            packed[3 * HALF_TILE :, :] = rest
            out[high * 4 + column, 0:PACKED, :] = packed[...].astype(BF16)
            out[high * 4 + column, PACKED:, :] = ends[high * 4 + column]


def place_partials(offsets, reward, other, spread, ends):
    return pl.pallas_call(
        place_kernel,
        out_shape=jax.ShapeDtypeStruct((8, PACKED + FAR + CORNERS, SPAN), BF16),
        in_specs=[pl.BlockSpec(memory_space=pltpu.SMEM)] + [IN_VMEM] * 4,
        scratch_shapes=[
            pltpu.VMEM((2, 512, SPAN), F32),
            pltpu.VMEM((256, 512), BF16),
            pltpu.VMEM((VIEWS, 704, 256), BF16),
            pltpu.VMEM((3, 896, 512), BF16),
            pltpu.VMEM((3, 2 * BAND, 512), F32),
            pltpu.VMEM((PACKED, SPAN), F32),
            pltpu.VMEM((2 * BAND, 896), BF16),
        ],
        compiler_params=pltpu.CompilerParams(vmem_limit_bytes=VMEM_LIMIT),
        name="place",
    )(offsets, reward, other, spread, ends)


def edge_kernel(
    features_hbm, weight_hbm, other_hbm, top_hbm, bottom_hbm,
    spread, own, out, features, weights, halves, semaphores,
):
    high, core, column = lax.axis_index("zhi"), lax.axis_index("core"), lax.axis_index("seq")
    pairs = [(weight_hbm, weights.at[0]), (other_hbm, weights.at[1])]
    pairs += [(top_hbm, own.at[4:5]), (bottom_hbm, own.at[5:6]), (features_hbm, features)]
    copies = fetch(semaphores, pairs)
    copies[0].wait()
    copies[1].wait()
    slot = iota((704, 588), 0)
    pick = as_bf16(((slot >> 4) * 14 + (slot & 15) == iota((704, 588), 1)) & ((slot & 15) < 14))
    both = jnp.concatenate([weights[0], weights[1]], axis=0)
    spread[...] = dot(pick, both, NT).astype(BF16).reshape(44, 16, SPAN)
    for copy in copies[2:]:
        copy.wait()
    top, bottom = own[4].astype(F32), own[5].astype(F32)
    far = jnp.where(core == 0, bottom, top)
    nothing = jnp.zeros((8, SPAN), F32)

    def put_ends(slot, above, below):
        rows = [each[:, k * SPAN : (k + 1) * SPAN] for k in range(4) for each in (above, below)]
        out[slot, FAR:, :] = jnp.concatenate(rows + [nothing], axis=0).astype(BF16)

    out[...] = jnp.zeros_like(out)
    own[0] = features[0]
    own[1] = features[31]
    across = jnp.where(
        high == 0,
        jnp.where(core == 0, bottom, own[1].astype(F32)),
        jnp.where(core == 1, top, own[0].astype(F32)),
    )
    half = jnp.where(core == high, across[0:16], across[16:32]).astype(BF16)
    for k in range(4):
        out[(1 - high) * 4 + column, 16 * k : 16 * k + 16, :] = half[:, k * SPAN : (k + 1) * SPAN]
    for index, (step, side, row, end) in enumerate(((-1, 0, 0, 0), (1, 16, 15, 31))):
        parts = []
        for k in range(4):
            lanes = slice(k * SPAN, (k + 1) * SPAN)
            halves[k] = features[:, side : side + 16, lanes].astype(F32).reshape(512, SPAN)
            parts.append(halves[k, pl.ds(row, 32, stride=16), :])
        own[2 + index] = jnp.concatenate(parts, axis=1).astype(BF16)
        there = jnp.clip(column + step, 0, 3)

        @pl.when(there != column)
        def _():
            put_ends(high * 4 + there, bottom[end : end + 1], top[end : end + 1])
            put_ends((1 - high) * 4 + there, far[end : end + 1], far[end : end + 1])


def edges_of(features, weight, other_weight, partner_top, partner_bottom):
    return pl.pallas_call(
        edge_kernel,
        out_shape=(
            jax.ShapeDtypeStruct((44, 16, SPAN), BF16),
            jax.ShapeDtypeStruct((6, 32, 512), BF16),
            jax.ShapeDtypeStruct((8, FAR + CORNERS, SPAN), BF16),
        ),
        in_specs=[IN_HBM] * 5,
        scratch_shapes=[
            pltpu.VMEM((32, 32, 512), BF16),
            pltpu.VMEM((2, 64, 588), BF16),
            pltpu.VMEM((4, 512, SPAN), F32),
            pltpu.SemaphoreType.DMA((5,)),
        ],
        compiler_params=pltpu.CompilerParams(vmem_limit_bytes=48 * 2**20),
        name="edges",
    )(features, weight, other_weight, partner_top, partner_bottom)


def inverse_haar(values):
    smooth, vertical, horizontal, diagonal = [values[:, k * 128 : (k + 1) * 128].astype(F32) for k in range(4)]
    upper_sum = smooth + vertical
    lower_sum = smooth - vertical
    upper_diff = horizontal + diagonal
    lower_diff = horizontal - diagonal
    return [
        0.5 * (upper_sum + upper_diff),
        0.5 * (upper_sum - upper_diff),
        0.5 * (lower_sum + lower_diff),
        0.5 * (lower_sum - lower_diff),
    ]


def slope_of(pre):
    sigmoid = 0.5 + 0.5 * jnp.tanh(0.5 * pre)
    return sigmoid * (1.0 + pre * (1.0 - sigmoid))


def gate_kernel(
    features_hbm, weight_hbm, bias, out_weight,
    out, back, kernel, taps, features, weight, fine, near, far, small, semaphores,
):
    copies = fetch(semaphores, [(features_hbm, features), (weight_hbm, weight)])
    copies[0].wait()

    @pl.loop(0, 32, unroll=4)
    def _(line):
        for k, phase in enumerate(inverse_haar(features[line])):
            fine[line + 1, 8:40, k * 128 : (k + 1) * 128] = phase

    copies[1].wait()

    @pl.loop(0, 34, unroll=2)
    def _(line):
        start = pl.multiple_of(line * PITCH, PITCH)
        near[pl.ds(start, PITCH), :] = fine[line, 7:55, :].astype(BF16)
        far[pl.ds(start, PITCH), :] = fine[line, 8:56, :].astype(BF16)

    nothing = jnp.zeros((128, 128), BF16)
    for a in range(3):
        for u in range(4):
            start = (a * 4 + u) * 128
            taps[start : start + 128, 0:128] = weight[a, u] if u < 3 else nothing
            taps[start : start + 128, 128:] = weight[a, u - 1] if u > 0 else nothing
    wide_bias = jnp.concatenate([bias[...], bias[...]], axis=1)
    count = 11 * PITCH
    for chunk in range(3):
        for phase in range(2):
            pieces = []
            for a in range(3):
                lines, parity = divmod(phase + a, 2)
                start = chunk * count + lines * PITCH
                for source in (near, far):
                    pieces.append(source[start : start + count, parity * 256 : (parity + 1) * 256])
            slope = slope_of(dot(jnp.concatenate(pieces, axis=1), taps[...]) + wide_bias)
            here = chunk * count
            out[here : here + count, phase * 256 : (phase + 1) * 256] = slope.astype(BF16)
    for a in range(3):
        for u in range(4):
            start = (a * 4 + u) * 128
            for q in range(2):
                b = q + 2 - u
                block = weight[a, b].astype(F32).T.astype(BF16) if 0 <= b <= 2 else nothing
                back[start : start + 128, q * 128 : (q + 1) * 128] = block
    slot = iota((64, 32), 0)
    small[...] = jnp.zeros_like(small)
    for k in range(9):
        small[3 * k : 3 * k + 3, :] = out_weight[k].astype(F32)
    for k in range(4):
        a, b = k // 2 + 2 - (slot & 3), k % 2 + 2 - (slot >> 4)
        channel = (slot >> 2) & 3
        valid = (a >= 0) & (a <= 2) & (b >= 0) & (b <= 2) & (channel < 3)
        window = as_bf16((iota((64, 32), 1) == a * 9 + b * 3 + channel) & valid)
        kernel[:, k * 128 : (k + 1) * 128] = dot(window, small[...].astype(BF16)).astype(BF16)


def gates(features, weight, bias, out_weight):
    return pl.pallas_call(
        gate_kernel,
        out_shape=(
            jax.ShapeDtypeStruct((33 * PITCH, 512), BF16),
            jax.ShapeDtypeStruct((1536, 256), BF16),
            jax.ShapeDtypeStruct((64, 512), BF16),
            jax.ShapeDtypeStruct((1536, 256), BF16),
        ),
        in_specs=[IN_HBM] * 2 + [IN_VMEM] * 2,
        scratch_shapes=[
            pltpu.VMEM((32, 32, 512), BF16),
            pltpu.VMEM((3, 3, 128, 128), BF16),
            pltpu.VMEM((34, 56, 512), F32),
            pltpu.VMEM((34 * PITCH, 512), BF16),
            pltpu.VMEM((34 * PITCH, 512), BF16),
            pltpu.VMEM((32, 128), F32),
            pltpu.SemaphoreType.DMA((2,)),
        ],
        compiler_params=pltpu.CompilerParams(vmem_limit_bytes=WHOLE_VMEM),
        cost_estimate=pl.CostEstimate(flops=5 * 10**9, bytes_accessed=4 * 10**6, transcendentals=2 * 10**6),
        name="gate",
    )(features, weight, bias, out_weight)


def ring_gates(parts, own, handed, sides, bias, taps, strips):
    high, core, column = lax.axis_index("zhi"), lax.axis_index("core"), lax.axis_index("seq")
    other = (1 - high) * 4

    def ends(slot):
        rows = parts[slot, FAR:, :].astype(F32)
        return [jnp.concatenate([rows[2 * k + e : 2 * k + e + 1] for k in range(4)], axis=1) for e in range(2)]

    def only(condition, values):
        return jnp.where(condition, values, 0.0)

    lines = [own[k].astype(F32) for k in range(6)]
    halves = []
    for k in range(4):
        first = parts[other + column, 16 * k : 16 * k + 16, :].astype(F32)
        halves.append(jnp.concatenate([first, handed[0, 16 * k : 16 * k + 16, :].astype(F32)], axis=0))
    distant = jnp.concatenate(halves, axis=1)
    above = jnp.where(core == 1, lines[5], only(high == 1, distant))
    below = jnp.where(core == 0, lines[4], only(high == 0, distant))
    sides = [sides[k].astype(F32) for k in range(2)]
    corners = []
    for step in (-1, 1):
        there = jnp.clip(column + step, 0, 3)
        inside = there != column
        near_ends, far_ends = ends(high * 4 + there), ends(other + there)
        corners.append(
            [
                only(inside, jnp.where(core == 1, near_ends[0], only(high == 1, far_ends[0]))),
                only(inside, jnp.where(core == 0, near_ends[1], only(high == 0, far_ends[1]))),
            ]
        )
    put = [
        (above, corners[0][0], corners[1][0]),
        (lines[0], sides[0][0:1], sides[1][0:1]),
        (lines[1], sides[0][31:32], sides[1][31:32]),
        (below, corners[0][1], corners[1][1]),
        (sides[0], corners[0][0], corners[0][1]),
        (lines[2], above[0:1], below[0:1]),
        (lines[3], above[31:32], below[31:32]),
        (sides[1], corners[1][0], corners[1][1]),
    ]
    for k, (middle, first, last) in enumerate(put):
        strips[k, 0:8, :] = jnp.zeros((8, 512), F32)
        strips[k, 40:56, :] = jnp.zeros((16, 512), F32)
        for at, values in ((8, middle), (7, first), (40, last)):
            for q, phase in enumerate(inverse_haar(values)):
                strips[k, at : at + values.shape[0], q * 128 : (q + 1) * 128] = phase
    shifted = [[strips[k, 7 + d : 55 + d, :].astype(BF16) for d in range(2)] for k in range(8)]
    wide_bias = jnp.concatenate([bias[...], bias[...]], axis=1)
    found = []
    for phase in range(2):
        stack = []
        for strip in range(4):
            pieces = []
            for a in range(3):
                step, parity = divmod(phase + a, 2)
                for turn in range(2):
                    if strip < 2:
                        source = shifted[2 * strip + step][turn]
                    else:
                        source = shifted[2 * strip + turn][step]
                    pieces.append(source[:, parity * 256 : (parity + 1) * 256])
            stack.append(jnp.concatenate(pieces, axis=1))
        found.append(slope_of(dot(jnp.concatenate(stack, axis=0), taps[...]) + wide_bias))
    rings = [
        jnp.concatenate([each[strip * PITCH : (strip + 1) * PITCH] for each in found], axis=1) for strip in range(4)
    ]
    at, lane = iota((PITCH, 512), 0), iota((PITCH, 512), 1)
    even, upper = (lane & 255) < 128, lane < 256
    left = (column == 0) & even
    right = (column == 3) & jnp.logical_not(even)
    beside = (left & (at == 0)) | (right & (at == 32))
    first_line = (high == 0) & (core == 0) & upper
    last_line = (high == 1) & (core == 1) & jnp.logical_not(upper)
    masks = [beside | first_line, beside | last_line, left, right]
    return [jnp.where(mask, 0.0, ring) for mask, ring in zip(masks, rings)]


def pixel_kernel(parts, stacked, pixels, edges, total):
    sums = parts[0, 0:PACKED, :].astype(F32)
    for source in range(1, 8):
        sums = sums + parts[source, 0:PACKED, :].astype(F32)
    total[...] = sums
    pixels[...] = jnp.zeros_like(pixels)
    edges[...] = jnp.zeros_like(edges)
    for channel in range(3):
        top = channel * 80
        half = total[channel * HALF_TILE : (channel + 1) * HALF_TILE, :] / PIXEL_STD[channel]
        pixels[top : top + HALF_TILE, :] = half
        pixels[top + HALF_TILE : top + 2 * HALF_TILE, :] = pltpu.roll(half, 64, 1)
        rest = total[3 * HALF_TILE :, :] / PIXEL_STD[channel]
        for block in range(7):
            turn = (64 - block * 12 - channel * 4) % SPAN
            edges[top + block * 10 : top + block * 10 + 10, :] = pltpu.roll(rest, turn, 1)
    rounded = jnp.where(iota((240, SPAN), 1) < 64, pixels[...], edges[...]).astype(BF16)
    picked = None
    x, lane = iota((SPAN, 512), 0), iota((SPAN, 512), 1)
    row, y = iota((176, 240), 0), iota((176, 240), 1)
    for third in range(3):
        j = (lane & 127) - 40 * third
        spread = as_bf16((x == 2 * j + (lane >> 7)) & (j >= 0) & (j < 33))
        channel = (row >> 2) & 3
        lines = as_bf16((y == channel * 80 + 2 * (3 * (row >> 4) + third) + (row & 3)) & (channel < 3))
        moved = dot(rounded, spread).astype(BF16)
        term = dot(lines, moved)
        picked = term if picked is None else picked + term
    picked = picked.astype(BF16)
    for line in range(11):
        for k in range(4):
            stacked[line, k * 16 : k * 16 + 16, :] = picked[line * 16 : line * 16 + 16, k * SPAN : (k + 1) * SPAN]


def pixel_windows(parts):
    return pl.pallas_call(
        pixel_kernel,
        out_shape=jax.ShapeDtypeStruct((11, 64, SPAN), BF16),
        scratch_shapes=[
            pltpu.VMEM((240, SPAN), F32),
            pltpu.VMEM((240, SPAN), F32),
            pltpu.VMEM((PACKED, SPAN), F32),
        ],
        compiler_params=pltpu.CompilerParams(vmem_limit_bytes=VMEM_LIMIT),
        name="pixels",
    )(parts)


def finish_kernel(
    parts_hbm, stacked_hbm, gate_hbm, back_hbm, kernel_hbm, taps_hbm, own_hbm, handed_hbm, before_hbm, after_hbm, bias_hbm,
    out, parts, stacked, gate, back, kernel, taps, own, handed, sides, bias, strips, columns, near, far, result, semaphores, sent,
):
    pairs = [(parts_hbm.at[:, PACKED:, :], parts), (own_hbm, own), (bias_hbm, bias), (handed_hbm, handed)]
    pairs += [(before_hbm, sides.at[0]), (after_hbm, sides.at[1]), (taps_hbm, taps), (kernel_hbm, kernel)]
    pairs += [(stacked_hbm, stacked), (gate_hbm, gate), (back_hbm, back)]
    copies = fetch(semaphores, pairs)
    for copy in copies[:9]:
        copy.wait()
    rings = ring_gates(parts, own, handed, sides, bias, taps, strips)
    columns[0] = rings[2]
    columns[1] = rings[3]
    copies[9].wait()
    at = iota((PITCH, 512), 0)
    for line in range(11):
        act = dot(stacked[line], kernel[...], TN)
        for third in range(3):
            index = line * 3 + third
            if index == 0:
                scale = rings[0]
            elif index == 32:
                scale = rings[1]
            else:
                scale = gate[index * PITCH : (index + 1) * PITCH, :].astype(F32)
                scale = jnp.where(at == 0, columns[0, index : index + 1, :], scale)
                scale = jnp.where(at == 32, columns[1, index : index + 1, :], scale)
            grad = act[third * 40 : third * 40 + 40] * scale[0:40]
            near[index * 32 : (index + 1) * 32, :] = grad[0:32].astype(BF16)
            far[index * 32 : (index + 1) * 32, :] = grad[1:33].astype(BF16)
    copies[10].wait()
    writes = []
    for chunk in range(4):
        stack = []
        for p in range(2):
            pieces = []
            for a in range(3):
                step, parity = divmod(p + 2 - a, 2)
                start = chunk * 256 + step * 32
                for source in (near, far):
                    pieces.append(source[start : start + 256, parity * 256 : (parity + 1) * 256])
            stack.append(jnp.concatenate(pieces, axis=1))
        found = dot(jnp.concatenate(stack, axis=0), back[...])
        plus, minus = found[:256] + found[256:], found[:256] - found[256:]
        bands = [
            plus[:, :128] + plus[:, 128:],
            minus[:, :128] + minus[:, 128:],
            plus[:, :128] - plus[:, 128:],
            minus[:, :128] - minus[:, 128:],
        ]
        for k, band in enumerate(bands):
            result[chunk, :, :, k * 128 : (k + 1) * 128] = (0.5 * band).astype(BF16).reshape(8, 32, 128)
        writes.append(pltpu.make_async_copy(result.at[chunk], out.at[chunk * 8 : chunk * 8 + 8], sent.at[chunk]))
        writes[-1].start()
    for write in writes:
        write.wait()


def finish(*operands):
    return pl.pallas_call(
        finish_kernel,
        out_shape=jax.ShapeDtypeStruct((32, 32, 512), BF16),
        in_specs=[IN_HBM] * 11,
        out_specs=IN_HBM,
        scratch_shapes=[
            pltpu.VMEM((8, FAR + CORNERS, SPAN), BF16),
            pltpu.VMEM((11, 64, SPAN), BF16),
            pltpu.VMEM((33 * PITCH, 512), BF16),
            pltpu.VMEM((1536, 256), BF16),
            pltpu.VMEM((64, 512), BF16),
            pltpu.VMEM((1536, 256), BF16),
            pltpu.VMEM((6, 32, 512), BF16),
            pltpu.VMEM((1, FAR, SPAN), BF16),
            pltpu.VMEM((2, 32, 512), BF16),
            pltpu.VMEM((1, 128), F32),
            pltpu.VMEM((8, 56, 512), F32),
            pltpu.VMEM((2, PITCH, 512), F32),
            pltpu.VMEM((33 * 32, 512), BF16),
            pltpu.VMEM((33 * 32, 512), BF16),
            pltpu.VMEM((4, 8, 32, 512), BF16),
            pltpu.SemaphoreType.DMA((11,)),
            pltpu.SemaphoreType.DMA((4,)),
        ],
        compiler_params=pltpu.CompilerParams(vmem_limit_bytes=WHOLE_VMEM),
        name="finish",
    )(*operands)


SWAP = [(0, 1), (1, 0)]
ROW = ("zhi", "core")


def on_device(reward_grad, embed_weight, crop_offsets, features, conv_weight, conv_bias, out_weight):
    mine = lax.all_to_all(view_pairs(reward_grad), "tok", split_axis=0, concat_axis=0, tiled=True)
    coarse = features[0]
    top, bottom, embed_weight = lax.optimization_barrier((coarse[:1], coarse[31:], embed_weight))
    partner_top = lax.ppermute(top, "core", SWAP)
    partner_bottom = lax.ppermute(bottom, "core", SWAP)
    other_weight = lax.ppermute(embed_weight, "core", SWAP)
    spread, own, ends = edges_of(coarse, embed_weight, other_weight, partner_top, partner_bottom)
    mine, spread, ends, own = lax.optimization_barrier((mine, spread, ends, own))
    partials = place_partials(crop_offsets.T, mine, lax.ppermute(mine, "core", SWAP), spread, ends)
    partials, coarse, own = lax.optimization_barrier((partials, coarse, own))
    parts = lax.all_to_all(partials, ("zhi", "seq"), split_axis=0, concat_axis=0, tiled=True)
    before = lax.ppermute(own[3], "seq", [(i, i + 1) for i in range(3)])
    after = lax.ppermute(own[2], "seq", [(i + 1, i) for i in range(3)])
    small = out_weight.transpose(0, 1, 3, 2).reshape(9, 3, 128)
    bias = conv_bias[None]
    gate = gates(coarse, conv_weight, bias, small)
    parts, gate, before, after = lax.optimization_barrier((parts, gate, before, after))
    slot = (1 - lax.axis_index("zhi")) * 4 + lax.axis_index("seq")
    handed = lax.ppermute(lax.dynamic_slice(parts, (slot, PACKED, 0), (1, FAR, SPAN)), "core", SWAP)
    return finish(parts, pixel_windows(parts), *gate, own, handed, before, after, bias)[None]


def solution(mesh):
    split = Mesh(mesh.devices.reshape(16, 2, 2, 4), ("tok", "zhi", "core", "seq"))
    placed = (
        P(None, "tok", ("zhi", "core", "seq")),
        P(("zhi", "core", "seq"), None),
        P("tok", None),
        P("tok", ROW, "seq", None),
        P(),
        P(),
        P(),
    )
    return jax.shard_map(
        on_device,
        mesh=split,
        in_specs=placed,
        out_specs=P("tok", ROW, "seq", None),
        check_vma=False,
    )
```

```python
import jax
import jax.numpy as jnp
from jax import lax
from jax.experimental import pallas as pl
from jax.experimental.pallas import tpu as pltpu
from jax.sharding import Mesh
from jax.sharding import PartitionSpec as P

PIXEL_STD = (0.26862954, 0.26130258, 0.27577711)
BF16 = jnp.bfloat16
F32 = jnp.float32
VIEWS = 4
TILE_PIX = 68
SPAN = 128
HALF_TILE = 34
BAND = 80
PACKED = 112
FAR = 64
CORNERS = 16
PITCH = 48
NT = (((1,), (1,)), ((), ()))
TN = (((0,), (0,)), ((), ()))
VMEM_LIMIT = 16 * 2**20
WHOLE_VMEM = 60 * 2**20
IN_HBM = pl.BlockSpec(memory_space=pltpu.HBM)
IN_VMEM = pl.BlockSpec(memory_space=pltpu.VMEM)


def iota(shape, axis):
    return lax.broadcasted_iota(jnp.int32, shape, axis)


def dot(a, b, dims=(((1,), (0,)), ((), ()))):
    return lax.dot_general(a, b, dims, preferred_element_type=F32)


def fetch(semaphores, pairs):
    copies = [pltpu.make_async_copy(src, dst, semaphores.at[k]) for k, (src, dst) in enumerate(pairs)]
    for copy in copies:
        copy.start()
    return copies


def as_bf16(mask):
    return jnp.where(mask, 1.0, 0.0).astype(BF16)


def pair_kernel(reward, out):
    for pair in range(32):
        out[pair] = jnp.concatenate([reward[2 * pair], reward[2 * pair + 1]], axis=1)


def view_pairs(reward):
    return pl.pallas_call(
        pair_kernel,
        out_shape=jax.ShapeDtypeStruct((32, 16, SPAN), BF16),
        compiler_params=pltpu.CompilerParams(vmem_limit_bytes=VMEM_LIMIT),
        name="pairs",
    )(reward)


def place_kernel(offsets, reward, other, spread, ends, out, flat, left, strips, across, canvas, packed, rows):
    own, theirs = [each[...].astype(F32).reshape(512, SPAN) for each in (reward, other)]
    low = iota((512, SPAN), 1) < 64
    flat[0] = jnp.where(low, own, pltpu.roll(theirs, 64, 1))
    flat[1] = jnp.where(low, pltpu.roll(own, 64, 1), theirs)
    for view in range(VIEWS):
        for patch in range(16):
            top = (patch // 4) * 64 + view * 16
            side = (patch % 4) * SPAN
            values = flat[view % 2, pl.ds((view // 2) * 16 + patch, 16, stride=32), :]
            left[top : top + 16, side : side + SPAN] = values.astype(BF16)
    low = iota((64, SPAN), 1) < 64
    own_group = ((iota((256, 512), 0) >> 4) & 3) == (iota((256, 512), 1) >> 7)
    for quad in range(11):
        blocks = [jnp.concatenate([spread[4 * quad + k]] * 4, axis=0) for k in range(4)]
        weights = jnp.concatenate([jnp.concatenate(blocks, axis=0)] * 4, axis=1)
        part = dot(left[...], jnp.where(own_group, weights, jnp.zeros((256, 512), BF16)), NT)
        for member in range(2):
            own = [part[64 * h : 64 * h + 64, member * SPAN : (member + 1) * SPAN] for h in range(4)]
            turned = [pltpu.roll(piece, 64, 1) for piece in own]
            for odd in range(2):
                start = (4 * quad + 2 * member + odd) * 16
                for side in range(2):
                    a, b = 2 * side, 2 * side + 1
                    if odd == 0:
                        joined = jnp.where(low, own[a], turned[b]).astype(BF16)
                    else:
                        joined = jnp.where(low, turned[a], own[b]).astype(BF16)
                    for view in range(VIEWS):
                        strips[view, start : start + 16, side * SPAN : (side + 1) * SPAN] = joined[
                            view * 16 : view * 16 + 16
                        ]
    slot, lane = iota((256, 512), 0), iota((256, 512), 1)
    gap = (lane >> 7) * 64 - 2 + (lane & 127) - (slot >> 4) * 14 - (slot & 15)
    gap = jnp.where(((slot & 15) < 14) & ((lane & 127) < TILE_PIX), gap, -1000)
    for view in range(VIEWS):
        cols = as_bf16(gap == offsets[1, view])
        for channel in range(3):
            across[channel, view * 224 : (view + 1) * 224, :] = dot(
                strips[view, channel * 224 : (channel + 1) * 224, :], cols
            ).astype(BF16)
    step, index = iota((BAND, 896), 0), iota((1, 896), 1)
    local, corner = index, jnp.zeros((1, 896), jnp.int32) + offsets[0, 0]
    for view in range(1, VIEWS):
        local = jnp.where(index >= 224 * view, index - 224 * view, local)
        corner = jnp.where(index >= 224 * view, offsets[0, view], corner)
    first = corner + 14 * (local & 15) + (local >> 4)
    core = lax.axis_index("core")
    for high in range(2):
        y = step + (64 * (2 * high + core) - 2)
        hit = as_bf16((y == first) & (step < TILE_PIX))
        rows[high * BAND : (high + 1) * BAND, :] = hit
    for channel in range(3):
        canvas[channel] = dot(rows[...], across[channel])
    lane = iota((HALF_TILE, SPAN), 1)
    wide_lane = iota((BAND, SPAN), 1)
    for high in range(2):
        for column in range(4):
            side = slice(column * SPAN, (column + 1) * SPAN)
            top = high * BAND
            for channel in range(3):
                upper = canvas[channel, top : top + HALF_TILE, side]
                lower = pltpu.roll(canvas[channel, top + HALF_TILE : top + 2 * HALF_TILE, side], 64, 1)
                packed[channel * HALF_TILE : (channel + 1) * HALF_TILE, :] = jnp.where(lane < 64, upper, lower)
            last = [canvas[channel, top : top + BAND, side] for channel in range(3)]
            joined = jnp.where(wide_lane < 68, last[0], pltpu.roll(last[1], 4, 1))
            joined = jnp.where(wide_lane < 72, joined, pltpu.roll(last[2], 8, 1))
            rest = None
            for block in range(7):
                piece = pltpu.roll(joined[block * 10 : block * 10 + 10], (64 + block * 12) % SPAN, 1)
                rest = piece if block == 0 else jnp.where(wide_lane[:10] < block * 12, rest, piece)
            packed[3 * HALF_TILE :, :] = rest
            out[high * 4 + column, 0:PACKED, :] = packed[...].astype(BF16)
            out[high * 4 + column, PACKED:, :] = ends[high * 4 + column]


def place_partials(offsets, reward, other, spread, ends):
    return pl.pallas_call(
        place_kernel,
        out_shape=jax.ShapeDtypeStruct((8, PACKED + FAR + CORNERS, SPAN), BF16),
        in_specs=[pl.BlockSpec(memory_space=pltpu.SMEM)] + [IN_VMEM] * 4,
        scratch_shapes=[
            pltpu.VMEM((2, 512, SPAN), F32),
            pltpu.VMEM((256, 512), BF16),
            pltpu.VMEM((VIEWS, 704, 256), BF16),
            pltpu.VMEM((3, 896, 512), BF16),
            pltpu.VMEM((3, 2 * BAND, 512), F32),
            pltpu.VMEM((PACKED, SPAN), F32),
            pltpu.VMEM((2 * BAND, 896), BF16),
        ],
        compiler_params=pltpu.CompilerParams(vmem_limit_bytes=VMEM_LIMIT),
        name="place",
    )(offsets, reward, other, spread, ends)


def edge_kernel(
    features_hbm, weight_hbm, other_hbm, top_hbm, bottom_hbm,
    spread, own, out, features, weights, halves, semaphores,
):
    high, core, column = lax.axis_index("zhi"), lax.axis_index("core"), lax.axis_index("seq")
    pairs = [(weight_hbm, weights.at[0]), (other_hbm, weights.at[1])]
    pairs += [(top_hbm, own.at[4:5]), (bottom_hbm, own.at[5:6]), (features_hbm, features)]
    copies = fetch(semaphores, pairs)
    copies[0].wait()
    copies[1].wait()
    slot = iota((704, 588), 0)
    pick = as_bf16(((slot >> 4) * 14 + (slot & 15) == iota((704, 588), 1)) & ((slot & 15) < 14))
    both = jnp.concatenate([weights[0], weights[1]], axis=0)
    spread[...] = dot(pick, both, NT).astype(BF16).reshape(44, 16, SPAN)
    for copy in copies[2:]:
        copy.wait()
    top, bottom = own[4].astype(F32), own[5].astype(F32)
    far = jnp.where(core == 0, bottom, top)
    nothing = jnp.zeros((8, SPAN), F32)

    def put_ends(slot, above, below):
        rows = [each[:, k * SPAN : (k + 1) * SPAN] for k in range(4) for each in (above, below)]
        out[slot, FAR:, :] = jnp.concatenate(rows + [nothing], axis=0).astype(BF16)

    out[...] = jnp.zeros_like(out)
    own[0] = features[0]
    own[1] = features[31]
    across = jnp.where(
        high == 0,
        jnp.where(core == 0, bottom, own[1].astype(F32)),
        jnp.where(core == 1, top, own[0].astype(F32)),
    )
    half = jnp.where(core == high, across[0:16], across[16:32]).astype(BF16)
    for k in range(4):
        out[(1 - high) * 4 + column, 16 * k : 16 * k + 16, :] = half[:, k * SPAN : (k + 1) * SPAN]
    for index, (step, side, row, end) in enumerate(((-1, 0, 0, 0), (1, 16, 15, 31))):
        parts = []
        for k in range(4):
            lanes = slice(k * SPAN, (k + 1) * SPAN)
            halves[k] = features[:, side : side + 16, lanes].astype(F32).reshape(512, SPAN)
            parts.append(halves[k, pl.ds(row, 32, stride=16), :])
        own[2 + index] = jnp.concatenate(parts, axis=1).astype(BF16)
        there = jnp.clip(column + step, 0, 3)

        @pl.when(there != column)
        def _():
            put_ends(high * 4 + there, bottom[end : end + 1], top[end : end + 1])
            put_ends((1 - high) * 4 + there, far[end : end + 1], far[end : end + 1])


def edges_of(features, weight, other_weight, partner_top, partner_bottom):
    return pl.pallas_call(
        edge_kernel,
        out_shape=(
            jax.ShapeDtypeStruct((44, 16, SPAN), BF16),
            jax.ShapeDtypeStruct((6, 32, 512), BF16),
            jax.ShapeDtypeStruct((8, FAR + CORNERS, SPAN), BF16),
        ),
        in_specs=[IN_HBM] * 5,
        scratch_shapes=[
            pltpu.VMEM((32, 32, 512), BF16),
            pltpu.VMEM((2, 64, 588), BF16),
            pltpu.VMEM((4, 512, SPAN), F32),
            pltpu.SemaphoreType.DMA((5,)),
        ],
        compiler_params=pltpu.CompilerParams(vmem_limit_bytes=48 * 2**20),
        name="edges",
    )(features, weight, other_weight, partner_top, partner_bottom)


def inverse_haar(values):
    smooth, vertical, horizontal, diagonal = [values[:, k * 128 : (k + 1) * 128].astype(F32) for k in range(4)]
    upper_sum = smooth + vertical
    lower_sum = smooth - vertical
    upper_diff = horizontal + diagonal
    lower_diff = horizontal - diagonal
    return [
        0.5 * (upper_sum + upper_diff),
        0.5 * (upper_sum - upper_diff),
        0.5 * (lower_sum + lower_diff),
        0.5 * (lower_sum - lower_diff),
    ]


def slope_of(pre):
    sigmoid = 0.5 + 0.5 * jnp.tanh(0.5 * pre)
    return sigmoid * (1.0 + pre * (1.0 - sigmoid))


def gate_kernel(
    features_hbm, weight_hbm, bias, out_weight,
    out, back, kernel, taps, features, weight, fine, near, far, small, semaphores,
):
    copies = fetch(semaphores, [(features_hbm, features), (weight_hbm, weight)])
    copies[0].wait()

    @pl.loop(0, 32, unroll=4)
    def _(line):
        for k, phase in enumerate(inverse_haar(features[line])):
            fine[line + 1, 8:40, k * 128 : (k + 1) * 128] = phase

    copies[1].wait()

    @pl.loop(0, 34, unroll=2)
    def _(line):
        start = pl.multiple_of(line * PITCH, PITCH)
        near[pl.ds(start, PITCH), :] = fine[line, 7:55, :].astype(BF16)
        far[pl.ds(start, PITCH), :] = fine[line, 8:56, :].astype(BF16)

    nothing = jnp.zeros((128, 128), BF16)
    for a in range(3):
        for u in range(4):
            start = (a * 4 + u) * 128
            taps[start : start + 128, 0:128] = weight[a, u] if u < 3 else nothing
            taps[start : start + 128, 128:] = weight[a, u - 1] if u > 0 else nothing
    wide_bias = jnp.concatenate([bias[...], bias[...]], axis=1)
    count = 11 * PITCH
    for chunk in range(3):
        for phase in range(2):
            pieces = []
            for a in range(3):
                lines, parity = divmod(phase + a, 2)
                start = chunk * count + lines * PITCH
                for source in (near, far):
                    pieces.append(source[start : start + count, parity * 256 : (parity + 1) * 256])
            slope = slope_of(dot(jnp.concatenate(pieces, axis=1), taps[...]) + wide_bias)
            here = chunk * count
            out[here : here + count, phase * 256 : (phase + 1) * 256] = slope.astype(BF16)
    for a in range(3):
        for u in range(4):
            start = (a * 4 + u) * 128
            for q in range(2):
                b = q + 2 - u
                block = weight[a, b].astype(F32).T.astype(BF16) if 0 <= b <= 2 else nothing
                back[start : start + 128, q * 128 : (q + 1) * 128] = block
    slot = iota((64, 32), 0)
    small[...] = jnp.zeros_like(small)
    for k in range(9):
        small[3 * k : 3 * k + 3, :] = out_weight[k].astype(F32)
    for k in range(4):
        a, b = k // 2 + 2 - (slot & 3), k % 2 + 2 - (slot >> 4)
        channel = (slot >> 2) & 3
        valid = (a >= 0) & (a <= 2) & (b >= 0) & (b <= 2) & (channel < 3)
        window = as_bf16((iota((64, 32), 1) == a * 9 + b * 3 + channel) & valid)
        kernel[:, k * 128 : (k + 1) * 128] = dot(window, small[...].astype(BF16)).astype(BF16)


def gates(features, weight, bias, out_weight):
    return pl.pallas_call(
        gate_kernel,
        out_shape=(
            jax.ShapeDtypeStruct((33 * PITCH, 512), BF16),
            jax.ShapeDtypeStruct((1536, 256), BF16),
            jax.ShapeDtypeStruct((64, 512), BF16),
            jax.ShapeDtypeStruct((1536, 256), BF16),
        ),
        in_specs=[IN_HBM] * 2 + [IN_VMEM] * 2,
        scratch_shapes=[
            pltpu.VMEM((32, 32, 512), BF16),
            pltpu.VMEM((3, 3, 128, 128), BF16),
            pltpu.VMEM((34, 56, 512), F32),
            pltpu.VMEM((34 * PITCH, 512), BF16),
            pltpu.VMEM((34 * PITCH, 512), BF16),
            pltpu.VMEM((32, 128), F32),
            pltpu.SemaphoreType.DMA((2,)),
        ],
        compiler_params=pltpu.CompilerParams(vmem_limit_bytes=WHOLE_VMEM),
        cost_estimate=pl.CostEstimate(flops=5 * 10**9, bytes_accessed=4 * 10**6, transcendentals=2 * 10**6),
        name="gate",
    )(features, weight, bias, out_weight)


def ring_gates(parts, own, handed, sides, bias, taps, strips):
    high, core, column = lax.axis_index("zhi"), lax.axis_index("core"), lax.axis_index("seq")
    other = (1 - high) * 4

    def ends(slot):
        rows = parts[slot, FAR:, :].astype(F32)
        return [jnp.concatenate([rows[2 * k + e : 2 * k + e + 1] for k in range(4)], axis=1) for e in range(2)]

    def only(condition, values):
        return jnp.where(condition, values, 0.0)

    lines = [own[k].astype(F32) for k in range(6)]
    halves = []
    for k in range(4):
        first = parts[other + column, 16 * k : 16 * k + 16, :].astype(F32)
        halves.append(jnp.concatenate([first, handed[0, 16 * k : 16 * k + 16, :].astype(F32)], axis=0))
    distant = jnp.concatenate(halves, axis=1)
    above = jnp.where(core == 1, lines[5], only(high == 1, distant))
    below = jnp.where(core == 0, lines[4], only(high == 0, distant))
    sides = [sides[k].astype(F32) for k in range(2)]
    corners = []
    for step in (-1, 1):
        there = jnp.clip(column + step, 0, 3)
        inside = there != column
        near_ends, far_ends = ends(high * 4 + there), ends(other + there)
        corners.append(
            [
                only(inside, jnp.where(core == 1, near_ends[0], only(high == 1, far_ends[0]))),
                only(inside, jnp.where(core == 0, near_ends[1], only(high == 0, far_ends[1]))),
            ]
        )
    put = [
        (above, corners[0][0], corners[1][0]),
        (lines[0], sides[0][0:1], sides[1][0:1]),
        (lines[1], sides[0][31:32], sides[1][31:32]),
        (below, corners[0][1], corners[1][1]),
        (sides[0], corners[0][0], corners[0][1]),
        (lines[2], above[0:1], below[0:1]),
        (lines[3], above[31:32], below[31:32]),
        (sides[1], corners[1][0], corners[1][1]),
    ]
    for k, (middle, first, last) in enumerate(put):
        strips[k, 0:8, :] = jnp.zeros((8, 512), F32)
        strips[k, 40:56, :] = jnp.zeros((16, 512), F32)
        for at, values in ((8, middle), (7, first), (40, last)):
            for q, phase in enumerate(inverse_haar(values)):
                strips[k, at : at + values.shape[0], q * 128 : (q + 1) * 128] = phase
    shifted = [[strips[k, 7 + d : 55 + d, :].astype(BF16) for d in range(2)] for k in range(8)]
    wide_bias = jnp.concatenate([bias[...], bias[...]], axis=1)
    found = []
    for phase in range(2):
        stack = []
        for strip in range(4):
            pieces = []
            for a in range(3):
                step, parity = divmod(phase + a, 2)
                for turn in range(2):
                    if strip < 2:
                        source = shifted[2 * strip + step][turn]
                    else:
                        source = shifted[2 * strip + turn][step]
                    pieces.append(source[:, parity * 256 : (parity + 1) * 256])
            stack.append(jnp.concatenate(pieces, axis=1))
        found.append(slope_of(dot(jnp.concatenate(stack, axis=0), taps[...]) + wide_bias))
    rings = [
        jnp.concatenate([each[strip * PITCH : (strip + 1) * PITCH] for each in found], axis=1) for strip in range(4)
    ]
    at, lane = iota((PITCH, 512), 0), iota((PITCH, 512), 1)
    even, upper = (lane & 255) < 128, lane < 256
    left = (column == 0) & even
    right = (column == 3) & jnp.logical_not(even)
    beside = (left & (at == 0)) | (right & (at == 32))
    first_line = (high == 0) & (core == 0) & upper
    last_line = (high == 1) & (core == 1) & jnp.logical_not(upper)
    masks = [beside | first_line, beside | last_line, left, right]
    return [jnp.where(mask, 0.0, ring) for mask, ring in zip(masks, rings)]


def pixel_kernel(parts, stacked, pixels, edges, total):
    sums = parts[0, 0:PACKED, :].astype(F32)
    for source in range(1, 8):
        sums = sums + parts[source, 0:PACKED, :].astype(F32)
    total[...] = sums
    pixels[...] = jnp.zeros_like(pixels)
    edges[...] = jnp.zeros_like(edges)
    for channel in range(3):
        top = channel * 80
        half = total[channel * HALF_TILE : (channel + 1) * HALF_TILE, :] / PIXEL_STD[channel]
        pixels[top : top + HALF_TILE, :] = half
        pixels[top + HALF_TILE : top + 2 * HALF_TILE, :] = pltpu.roll(half, 64, 1)
        rest = total[3 * HALF_TILE :, :] / PIXEL_STD[channel]
        for block in range(7):
            turn = (64 - block * 12 - channel * 4) % SPAN
            edges[top + block * 10 : top + block * 10 + 10, :] = pltpu.roll(rest, turn, 1)
    rounded = jnp.where(iota((240, SPAN), 1) < 64, pixels[...], edges[...]).astype(BF16)
    picked = None
    x, lane = iota((SPAN, 512), 0), iota((SPAN, 512), 1)
    row, y = iota((176, 240), 0), iota((176, 240), 1)
    for third in range(3):
        j = (lane & 127) - 40 * third
        spread = as_bf16((x == 2 * j + (lane >> 7)) & (j >= 0) & (j < 33))
        channel = (row >> 2) & 3
        lines = as_bf16((y == channel * 80 + 2 * (3 * (row >> 4) + third) + (row & 3)) & (channel < 3))
        moved = dot(rounded, spread).astype(BF16)
        term = dot(lines, moved)
        picked = term if picked is None else picked + term
    picked = picked.astype(BF16)
    for line in range(11):
        for k in range(4):
            stacked[line, k * 16 : k * 16 + 16, :] = picked[line * 16 : line * 16 + 16, k * SPAN : (k + 1) * SPAN]


def pixel_windows(parts):
    return pl.pallas_call(
        pixel_kernel,
        out_shape=jax.ShapeDtypeStruct((11, 64, SPAN), BF16),
        scratch_shapes=[
            pltpu.VMEM((240, SPAN), F32),
            pltpu.VMEM((240, SPAN), F32),
            pltpu.VMEM((PACKED, SPAN), F32),
        ],
        compiler_params=pltpu.CompilerParams(vmem_limit_bytes=VMEM_LIMIT),
        name="pixels",
    )(parts)


def finish_kernel(
    parts_hbm, stacked_hbm, gate_hbm, back_hbm, kernel_hbm, taps_hbm, own_hbm, handed_hbm, before_hbm, after_hbm, bias_hbm,
    out, parts, stacked, gate, back, kernel, taps, own, handed, sides, bias, strips, columns, near, far, semaphores,
):
    pairs = [(parts_hbm.at[:, PACKED:, :], parts), (own_hbm, own), (bias_hbm, bias), (handed_hbm, handed)]
    pairs += [(before_hbm, sides.at[0]), (after_hbm, sides.at[1]), (taps_hbm, taps), (kernel_hbm, kernel)]
    pairs += [(stacked_hbm, stacked), (gate_hbm, gate), (back_hbm, back)]
    copies = fetch(semaphores, pairs)
    for copy in copies[:9]:
        copy.wait()
    rings = ring_gates(parts, own, handed, sides, bias, taps, strips)
    columns[0] = rings[2]
    columns[1] = rings[3]
    copies[9].wait()
    at = iota((PITCH, 512), 0)
    for line in range(11):
        act = dot(stacked[line], kernel[...], TN)
        for third in range(3):
            index = line * 3 + third
            if index == 0:
                scale = rings[0]
            elif index == 32:
                scale = rings[1]
            else:
                scale = gate[index * PITCH : (index + 1) * PITCH, :].astype(F32)
                scale = jnp.where(at == 0, columns[0, index : index + 1, :], scale)
                scale = jnp.where(at == 32, columns[1, index : index + 1, :], scale)
            grad = act[third * 40 : third * 40 + 40] * scale[0:40]
            near[index * 32 : (index + 1) * 32, :] = grad[0:32].astype(BF16)
            far[index * 32 : (index + 1) * 32, :] = grad[1:33].astype(BF16)
    copies[10].wait()
    for chunk in range(4):
        stack = []
        for p in range(2):
            pieces = []
            for a in range(3):
                step, parity = divmod(p + 2 - a, 2)
                start = chunk * 256 + step * 32
                for source in (near, far):
                    pieces.append(source[start : start + 256, parity * 256 : (parity + 1) * 256])
            stack.append(jnp.concatenate(pieces, axis=1))
        found = dot(jnp.concatenate(stack, axis=0), back[...])
        plus, minus = found[:256] + found[256:], found[:256] - found[256:]
        bands = [
            plus[:, :128] + plus[:, 128:],
            minus[:, :128] + minus[:, 128:],
            plus[:, :128] - plus[:, 128:],
            minus[:, :128] - minus[:, 128:],
        ]
        for k, band in enumerate(bands):
            out[chunk * 8 : chunk * 8 + 8, :, k * 128 : (k + 1) * 128] = (0.5 * band).astype(BF16).reshape(8, 32, 128)


def finish(*operands):
    return pl.pallas_call(
        finish_kernel,
        out_shape=jax.ShapeDtypeStruct((32, 32, 512), BF16),
        in_specs=[IN_HBM] * 11,
        scratch_shapes=[
            pltpu.VMEM((8, FAR + CORNERS, SPAN), BF16),
            pltpu.VMEM((11, 64, SPAN), BF16),
            pltpu.VMEM((33 * PITCH, 512), BF16),
            pltpu.VMEM((1536, 256), BF16),
            pltpu.VMEM((64, 512), BF16),
            pltpu.VMEM((1536, 256), BF16),
            pltpu.VMEM((6, 32, 512), BF16),
            pltpu.VMEM((1, FAR, SPAN), BF16),
            pltpu.VMEM((2, 32, 512), BF16),
            pltpu.VMEM((1, 128), F32),
            pltpu.VMEM((8, 56, 512), F32),
            pltpu.VMEM((2, PITCH, 512), F32),
            pltpu.VMEM((33 * 32, 512), BF16),
            pltpu.VMEM((33 * 32, 512), BF16),
            pltpu.SemaphoreType.DMA((11,)),
        ],
        compiler_params=pltpu.CompilerParams(vmem_limit_bytes=WHOLE_VMEM),
        name="finish",
    )(*operands)


SWAP = [(0, 1), (1, 0)]
ROW = ("zhi", "core")


def on_device(reward_grad, embed_weight, crop_offsets, features, conv_weight, conv_bias, out_weight):
    mine = lax.all_to_all(view_pairs(reward_grad), "tok", split_axis=0, concat_axis=0, tiled=True)
    coarse = features[0]
    top, bottom, embed_weight = lax.optimization_barrier((coarse[:1], coarse[31:], embed_weight))
    partner_top = lax.ppermute(top, "core", SWAP)
    partner_bottom = lax.ppermute(bottom, "core", SWAP)
    other_weight = lax.ppermute(embed_weight, "core", SWAP)
    spread, own, ends = edges_of(coarse, embed_weight, other_weight, partner_top, partner_bottom)
    before = lax.ppermute(own[3], "seq", [(i, i + 1) for i in range(3)])
    after = lax.ppermute(own[2], "seq", [(i + 1, i) for i in range(3)])
    mine, spread, ends, own, before, after = lax.optimization_barrier((mine, spread, ends, own, before, after))
    partials = place_partials(crop_offsets.T, mine, lax.ppermute(mine, "core", SWAP), spread, ends)
    partials, coarse = lax.optimization_barrier((partials, coarse))
    parts = lax.all_to_all(partials, ("zhi", "seq"), split_axis=0, concat_axis=0, tiled=True)
    small = out_weight.transpose(0, 1, 3, 2).reshape(9, 3, 128)
    bias = conv_bias[None]
    gate = gates(coarse, conv_weight, bias, small)
    parts, gate, before, after = lax.optimization_barrier((parts, gate, before, after))
    slot = (1 - lax.axis_index("zhi")) * 4 + lax.axis_index("seq")
    handed = lax.ppermute(lax.dynamic_slice(parts, (slot, PACKED, 0), (1, FAR, SPAN)), "core", SWAP)
    return finish(parts, pixel_windows(parts), *gate, own, handed, before, after, bias)[None]


def solution(mesh):
    split = Mesh(mesh.devices.reshape(16, 2, 2, 4), ("tok", "zhi", "core", "seq"))
    placed = (
        P(None, "tok", ("zhi", "core", "seq")),
        P(("zhi", "core", "seq"), None),
        P("tok", None),
        P("tok", ROW, "seq", None),
        P(),
        P(),
        P(),
    )
    return jax.shard_map(
        on_device,
        mesh=split,
        in_specs=placed,
        out_specs=P("tok", ROW, "seq", None),
        check_vma=False,
    )
```

```python
import jax
import jax.numpy as jnp
from jax import lax
from jax.experimental import pallas as pl
from jax.experimental.pallas import tpu as pltpu
from jax.sharding import Mesh
from jax.sharding import PartitionSpec as P

PIXEL_STD = (0.26862954, 0.26130258, 0.27577711)
BF16 = jnp.bfloat16
F32 = jnp.float32
VIEWS = 4
TILE_PIX = 68
SPAN = 128
HALF_TILE = 34
BAND = 80
PACKED = 112
FAR = 64
PITCH = 48
NT = (((1,), (1,)), ((), ()))
TN = (((0,), (0,)), ((), ()))
VMEM_LIMIT = 16 * 2**20
WHOLE_VMEM = 60 * 2**20
IN_HBM = pl.BlockSpec(memory_space=pltpu.HBM)
IN_VMEM = pl.BlockSpec(memory_space=pltpu.VMEM)


def iota(shape, axis):
    return lax.broadcasted_iota(jnp.int32, shape, axis)


def dot(a, b, dims=(((1,), (0,)), ((), ()))):
    return lax.dot_general(a, b, dims, preferred_element_type=F32)


def fetch(semaphores, pairs):
    copies = [pltpu.make_async_copy(src, dst, semaphores.at[k]) for k, (src, dst) in enumerate(pairs)]
    for copy in copies:
        copy.start()
    return copies


def as_bf16(mask):
    return jnp.where(mask, 1.0, 0.0).astype(BF16)


def pair_kernel(reward, out):
    for pair in range(32):
        out[pair] = jnp.concatenate([reward[2 * pair], reward[2 * pair + 1]], axis=1)


def view_pairs(reward):
    return pl.pallas_call(
        pair_kernel,
        out_shape=jax.ShapeDtypeStruct((32, 16, SPAN), BF16),
        compiler_params=pltpu.CompilerParams(vmem_limit_bytes=VMEM_LIMIT),
        name="pairs",
    )(reward)


def place_kernel(offsets, reward, other, spread, ends, out, flat, left, strips, across, canvas, packed, rows):
    own, theirs = [each[...].astype(F32).reshape(512, SPAN) for each in (reward, other)]
    low = iota((512, SPAN), 1) < 64
    flat[0] = jnp.where(low, own, pltpu.roll(theirs, 64, 1))
    flat[1] = jnp.where(low, pltpu.roll(own, 64, 1), theirs)
    for view in range(VIEWS):
        for patch in range(16):
            top = (patch // 4) * 64 + view * 16
            side = (patch % 4) * SPAN
            values = flat[view % 2, pl.ds((view // 2) * 16 + patch, 16, stride=32), :]
            left[top : top + 16, side : side + SPAN] = values.astype(BF16)
    low = iota((64, SPAN), 1) < 64
    own_group = ((iota((256, 512), 0) >> 4) & 3) == (iota((256, 512), 1) >> 7)
    for quad in range(11):
        blocks = [jnp.concatenate([spread[4 * quad + k]] * 4, axis=0) for k in range(4)]
        weights = jnp.concatenate([jnp.concatenate(blocks, axis=0)] * 4, axis=1)
        part = dot(left[...], jnp.where(own_group, weights, jnp.zeros((256, 512), BF16)), NT)
        for member in range(2):
            own = [part[64 * h : 64 * h + 64, member * SPAN : (member + 1) * SPAN] for h in range(4)]
            turned = [pltpu.roll(piece, 64, 1) for piece in own]
            for odd in range(2):
                start = (4 * quad + 2 * member + odd) * 16
                for side in range(2):
                    a, b = 2 * side, 2 * side + 1
                    if odd == 0:
                        joined = jnp.where(low, own[a], turned[b]).astype(BF16)
                    else:
                        joined = jnp.where(low, turned[a], own[b]).astype(BF16)
                    for view in range(VIEWS):
                        strips[view, start : start + 16, side * SPAN : (side + 1) * SPAN] = joined[
                            view * 16 : view * 16 + 16
                        ]
    slot, lane = iota((256, 512), 0), iota((256, 512), 1)
    gap = (lane >> 7) * 64 - 2 + (lane & 127) - (slot >> 4) * 14 - (slot & 15)
    gap = jnp.where(((slot & 15) < 14) & ((lane & 127) < TILE_PIX), gap, -1000)
    for view in range(VIEWS):
        cols = as_bf16(gap == offsets[1, view])
        for channel in range(3):
            across[channel, view * 224 : (view + 1) * 224, :] = dot(
                strips[view, channel * 224 : (channel + 1) * 224, :], cols
            ).astype(BF16)
    step, index = iota((BAND, 896), 0), iota((1, 896), 1)
    local, corner = index, jnp.zeros((1, 896), jnp.int32) + offsets[0, 0]
    for view in range(1, VIEWS):
        local = jnp.where(index >= 224 * view, index - 224 * view, local)
        corner = jnp.where(index >= 224 * view, offsets[0, view], corner)
    first = corner + 14 * (local & 15) + (local >> 4)
    core = lax.axis_index("core")
    for high in range(2):
        y = step + (64 * (2 * high + core) - 2)
        hit = as_bf16((y == first) & (step < TILE_PIX))
        rows[high * BAND : (high + 1) * BAND, :] = hit
    for channel in range(3):
        canvas[channel] = dot(rows[...], across[channel])
    lane = iota((HALF_TILE, SPAN), 1)
    wide_lane = iota((BAND, SPAN), 1)
    for high in range(2):
        for column in range(4):
            side = slice(column * SPAN, (column + 1) * SPAN)
            top = high * BAND
            for channel in range(3):
                upper = canvas[channel, top : top + HALF_TILE, side]
                lower = pltpu.roll(canvas[channel, top + HALF_TILE : top + 2 * HALF_TILE, side], 64, 1)
                packed[channel * HALF_TILE : (channel + 1) * HALF_TILE, :] = jnp.where(lane < 64, upper, lower)
            last = [canvas[channel, top : top + BAND, side] for channel in range(3)]
            joined = jnp.where(wide_lane < 68, last[0], pltpu.roll(last[1], 4, 1))
            joined = jnp.where(wide_lane < 72, joined, pltpu.roll(last[2], 8, 1))
            rest = None
            for block in range(7):
                piece = pltpu.roll(joined[block * 10 : block * 10 + 10], (64 + block * 12) % SPAN, 1)
                rest = piece if block == 0 else jnp.where(wide_lane[:10] < block * 12, rest, piece)
            packed[3 * HALF_TILE :, :] = rest
            out[high * 4 + column, 0:PACKED, :] = packed[...].astype(BF16)
            out[high * 4 + column, PACKED:, :] = ends[high * 4 + column]


def place_partials(offsets, reward, other, spread, ends):
    return pl.pallas_call(
        place_kernel,
        out_shape=jax.ShapeDtypeStruct((8, PACKED + FAR, SPAN), BF16),
        in_specs=[pl.BlockSpec(memory_space=pltpu.SMEM)] + [IN_VMEM] * 4,
        scratch_shapes=[
            pltpu.VMEM((2, 512, SPAN), F32),
            pltpu.VMEM((256, 512), BF16),
            pltpu.VMEM((VIEWS, 704, 256), BF16),
            pltpu.VMEM((3, 896, 512), BF16),
            pltpu.VMEM((3, 2 * BAND, 512), F32),
            pltpu.VMEM((PACKED, SPAN), F32),
            pltpu.VMEM((2 * BAND, 896), BF16),
        ],
        compiler_params=pltpu.CompilerParams(vmem_limit_bytes=VMEM_LIMIT),
        name="place",
    )(offsets, reward, other, spread, ends)


def edge_kernel(
    features_hbm, weight_hbm, other_hbm, top_hbm, bottom_hbm,
    spread, own, out, features, weights, halves, semaphores,
):
    high, core, column = lax.axis_index("zhi"), lax.axis_index("core"), lax.axis_index("seq")
    pairs = [(weight_hbm, weights.at[0]), (other_hbm, weights.at[1])]
    pairs += [(top_hbm, own.at[4:5]), (bottom_hbm, own.at[5:6]), (features_hbm, features)]
    copies = fetch(semaphores, pairs)
    copies[0].wait()
    copies[1].wait()
    slot = iota((704, 588), 0)
    pick = as_bf16(((slot >> 4) * 14 + (slot & 15) == iota((704, 588), 1)) & ((slot & 15) < 14))
    both = jnp.concatenate([weights[0], weights[1]], axis=0)
    spread[...] = dot(pick, both, NT).astype(BF16).reshape(44, 16, SPAN)
    for copy in copies[2:]:
        copy.wait()
    top, bottom = own[4].astype(F32), own[5].astype(F32)
    far = jnp.where(core == 0, bottom, top)
    nothing = jnp.zeros((8, SPAN), F32)

    def put_ends(slot, above, below):
        rows = [each[:, k * SPAN : (k + 1) * SPAN] for k in range(4) for each in (above, below)]
        out[slot, 0:16, :] = jnp.concatenate(rows + [nothing], axis=0).astype(BF16)

    out[...] = jnp.zeros_like(out)
    own[0] = features[0]
    own[1] = features[31]
    across = jnp.where(
        high == 0,
        jnp.where(core == 0, bottom, own[1].astype(F32)),
        jnp.where(core == 1, top, own[0].astype(F32)),
    )
    half = jnp.where(core == high, across[0:16], across[16:32]).astype(BF16)
    for k in range(4):
        out[(1 - high) * 4 + column, 16 * k : 16 * k + 16, :] = half[:, k * SPAN : (k + 1) * SPAN]
    for index, (step, side, row, end) in enumerate(((-1, 0, 0, 0), (1, 16, 15, 31))):
        parts = []
        for k in range(4):
            lanes = slice(k * SPAN, (k + 1) * SPAN)
            halves[k] = features[:, side : side + 16, lanes].astype(F32).reshape(512, SPAN)
            parts.append(halves[k, pl.ds(row, 32, stride=16), :])
        own[2 + index] = jnp.concatenate(parts, axis=1).astype(BF16)
        there = jnp.clip(column + step, 0, 3)

        @pl.when(there != column)
        def _():
            put_ends(high * 4 + there, bottom[end : end + 1], top[end : end + 1])
            put_ends((1 - high) * 4 + there, far[end : end + 1], far[end : end + 1])


def edges_of(features, weight, other_weight, partner_top, partner_bottom):
    return pl.pallas_call(
        edge_kernel,
        out_shape=(
            jax.ShapeDtypeStruct((44, 16, SPAN), BF16),
            jax.ShapeDtypeStruct((6, 32, 512), BF16),
            jax.ShapeDtypeStruct((8, FAR, SPAN), BF16),
        ),
        in_specs=[IN_HBM] * 5,
        scratch_shapes=[
            pltpu.VMEM((32, 32, 512), BF16),
            pltpu.VMEM((2, 64, 588), BF16),
            pltpu.VMEM((4, 512, SPAN), F32),
            pltpu.SemaphoreType.DMA((5,)),
        ],
        compiler_params=pltpu.CompilerParams(vmem_limit_bytes=48 * 2**20),
        name="edges",
    )(features, weight, other_weight, partner_top, partner_bottom)


def inverse_haar(values):
    smooth, vertical, horizontal, diagonal = [values[:, k * 128 : (k + 1) * 128].astype(F32) for k in range(4)]
    upper_sum = smooth + vertical
    lower_sum = smooth - vertical
    upper_diff = horizontal + diagonal
    lower_diff = horizontal - diagonal
    return [
        0.5 * (upper_sum + upper_diff),
        0.5 * (upper_sum - upper_diff),
        0.5 * (lower_sum + lower_diff),
        0.5 * (lower_sum - lower_diff),
    ]


def slope_of(pre):
    sigmoid = 0.5 + 0.5 * jnp.tanh(0.5 * pre)
    return sigmoid * (1.0 + pre * (1.0 - sigmoid))


def gate_kernel(
    features_hbm, weight_hbm, bias, out_weight,
    out, back, kernel, taps, features, weight, fine, near, far, small, semaphores,
):
    copies = fetch(semaphores, [(features_hbm, features), (weight_hbm, weight)])
    copies[0].wait()

    @pl.loop(0, 32, unroll=4)
    def _(line):
        for k, phase in enumerate(inverse_haar(features[line])):
            fine[line + 1, 8:40, k * 128 : (k + 1) * 128] = phase

    copies[1].wait()

    @pl.loop(0, 34, unroll=2)
    def _(line):
        start = pl.multiple_of(line * PITCH, PITCH)
        near[pl.ds(start, PITCH), :] = fine[line, 7:55, :].astype(BF16)
        far[pl.ds(start, PITCH), :] = fine[line, 8:56, :].astype(BF16)

    nothing = jnp.zeros((128, 128), BF16)
    for a in range(3):
        for u in range(4):
            start = (a * 4 + u) * 128
            taps[start : start + 128, 0:128] = weight[a, u] if u < 3 else nothing
            taps[start : start + 128, 128:] = weight[a, u - 1] if u > 0 else nothing
    wide_bias = jnp.concatenate([bias[...], bias[...]], axis=1)
    count = 11 * PITCH
    for chunk in range(3):
        for phase in range(2):
            pieces = []
            for a in range(3):
                lines, parity = divmod(phase + a, 2)
                start = chunk * count + lines * PITCH
                for source in (near, far):
                    pieces.append(source[start : start + count, parity * 256 : (parity + 1) * 256])
            slope = slope_of(dot(jnp.concatenate(pieces, axis=1), taps[...]) + wide_bias)
            here = chunk * count
            out[here : here + count, phase * 256 : (phase + 1) * 256] = slope.astype(BF16)
    for a in range(3):
        for u in range(4):
            start = (a * 4 + u) * 128
            for q in range(2):
                b = q + 2 - u
                block = weight[a, b].astype(F32).T.astype(BF16) if 0 <= b <= 2 else nothing
                back[start : start + 128, q * 128 : (q + 1) * 128] = block
    slot = iota((64, 32), 0)
    small[...] = jnp.zeros_like(small)
    for k in range(9):
        small[3 * k : 3 * k + 3, :] = out_weight[k].astype(F32)
    for k in range(4):
        a, b = k // 2 + 2 - (slot & 3), k % 2 + 2 - (slot >> 4)
        channel = (slot >> 2) & 3
        valid = (a >= 0) & (a <= 2) & (b >= 0) & (b <= 2) & (channel < 3)
        window = as_bf16((iota((64, 32), 1) == a * 9 + b * 3 + channel) & valid)
        kernel[:, k * 128 : (k + 1) * 128] = dot(window, small[...].astype(BF16)).astype(BF16)


def gates(features, weight, bias, out_weight):
    return pl.pallas_call(
        gate_kernel,
        out_shape=(
            jax.ShapeDtypeStruct((33 * PITCH, 512), BF16),
            jax.ShapeDtypeStruct((1536, 256), BF16),
            jax.ShapeDtypeStruct((64, 512), BF16),
            jax.ShapeDtypeStruct((1536, 256), BF16),
        ),
        in_specs=[IN_HBM] * 2 + [IN_VMEM] * 2,
        scratch_shapes=[
            pltpu.VMEM((32, 32, 512), BF16),
            pltpu.VMEM((3, 3, 128, 128), BF16),
            pltpu.VMEM((34, 56, 512), F32),
            pltpu.VMEM((34 * PITCH, 512), BF16),
            pltpu.VMEM((34 * PITCH, 512), BF16),
            pltpu.VMEM((32, 128), F32),
            pltpu.SemaphoreType.DMA((2,)),
        ],
        compiler_params=pltpu.CompilerParams(vmem_limit_bytes=WHOLE_VMEM),
        cost_estimate=pl.CostEstimate(flops=5 * 10**9, bytes_accessed=4 * 10**6, transcendentals=2 * 10**6),
        name="gate",
    )(features, weight, bias, out_weight)


def ring_gates(parts, own, handed, sides, bias, taps, strips):
    high, core, column = lax.axis_index("zhi"), lax.axis_index("core"), lax.axis_index("seq")
    other = (1 - high) * 4

    def ends(slot):
        rows = parts[slot, 0:16, :].astype(F32)
        return [jnp.concatenate([rows[2 * k + e : 2 * k + e + 1] for k in range(4)], axis=1) for e in range(2)]

    def only(condition, values):
        return jnp.where(condition, values, 0.0)

    lines = [own[k].astype(F32) for k in range(6)]
    halves = []
    for k in range(4):
        first = parts[other + column, 16 * k : 16 * k + 16, :].astype(F32)
        halves.append(jnp.concatenate([first, handed[0, 16 * k : 16 * k + 16, :].astype(F32)], axis=0))
    distant = jnp.concatenate(halves, axis=1)
    above = jnp.where(core == 1, lines[5], only(high == 1, distant))
    below = jnp.where(core == 0, lines[4], only(high == 0, distant))
    sides = [sides[k].astype(F32) for k in range(2)]
    corners = []
    for step in (-1, 1):
        there = jnp.clip(column + step, 0, 3)
        inside = there != column
        near_ends, far_ends = ends(high * 4 + there), ends(other + there)
        corners.append(
            [
                only(inside, jnp.where(core == 1, near_ends[0], only(high == 1, far_ends[0]))),
                only(inside, jnp.where(core == 0, near_ends[1], only(high == 0, far_ends[1]))),
            ]
        )
    put = [
        (above, corners[0][0], corners[1][0]),
        (lines[0], sides[0][0:1], sides[1][0:1]),
        (lines[1], sides[0][31:32], sides[1][31:32]),
        (below, corners[0][1], corners[1][1]),
        (sides[0], corners[0][0], corners[0][1]),
        (lines[2], above[0:1], below[0:1]),
        (lines[3], above[31:32], below[31:32]),
        (sides[1], corners[1][0], corners[1][1]),
    ]
    for k, (middle, first, last) in enumerate(put):
        strips[k, 0:8, :] = jnp.zeros((8, 512), F32)
        strips[k, 40:56, :] = jnp.zeros((16, 512), F32)
        for at, values in ((8, middle), (7, first), (40, last)):
            for q, phase in enumerate(inverse_haar(values)):
                strips[k, at : at + values.shape[0], q * 128 : (q + 1) * 128] = phase
    shifted = [[strips[k, 7 + d : 55 + d, :].astype(BF16) for d in range(2)] for k in range(8)]
    wide_bias = jnp.concatenate([bias[...], bias[...]], axis=1)
    found = []
    for phase in range(2):
        stack = []
        for strip in range(4):
            pieces = []
            for a in range(3):
                step, parity = divmod(phase + a, 2)
                for turn in range(2):
                    if strip < 2:
                        source = shifted[2 * strip + step][turn]
                    else:
                        source = shifted[2 * strip + turn][step]
                    pieces.append(source[:, parity * 256 : (parity + 1) * 256])
            stack.append(jnp.concatenate(pieces, axis=1))
        found.append(slope_of(dot(jnp.concatenate(stack, axis=0), taps[...]) + wide_bias))
    rings = [
        jnp.concatenate([each[strip * PITCH : (strip + 1) * PITCH] for each in found], axis=1) for strip in range(4)
    ]
    at, lane = iota((PITCH, 512), 0), iota((PITCH, 512), 1)
    even, upper = (lane & 255) < 128, lane < 256
    left = (column == 0) & even
    right = (column == 3) & jnp.logical_not(even)
    beside = (left & (at == 0)) | (right & (at == 32))
    first_line = (high == 0) & (core == 0) & upper
    last_line = (high == 1) & (core == 1) & jnp.logical_not(upper)
    masks = [beside | first_line, beside | last_line, left, right]
    return [jnp.where(mask, 0.0, ring) for mask, ring in zip(masks, rings)]


def pixel_kernel(parts, stacked, pixels, edges, total):
    sums = parts[0, 0:PACKED, :].astype(F32)
    for source in range(1, 8):
        sums = sums + parts[source, 0:PACKED, :].astype(F32)
    total[...] = sums
    pixels[...] = jnp.zeros_like(pixels)
    edges[...] = jnp.zeros_like(edges)
    for channel in range(3):
        top = channel * 80
        half = total[channel * HALF_TILE : (channel + 1) * HALF_TILE, :] / PIXEL_STD[channel]
        pixels[top : top + HALF_TILE, :] = half
        pixels[top + HALF_TILE : top + 2 * HALF_TILE, :] = pltpu.roll(half, 64, 1)
        rest = total[3 * HALF_TILE :, :] / PIXEL_STD[channel]
        for block in range(7):
            turn = (64 - block * 12 - channel * 4) % SPAN
            edges[top + block * 10 : top + block * 10 + 10, :] = pltpu.roll(rest, turn, 1)
    rounded = jnp.where(iota((240, SPAN), 1) < 64, pixels[...], edges[...]).astype(BF16)
    picked = None
    x, lane = iota((SPAN, 512), 0), iota((SPAN, 512), 1)
    row, y = iota((176, 240), 0), iota((176, 240), 1)
    for third in range(3):
        j = (lane & 127) - 40 * third
        spread = as_bf16((x == 2 * j + (lane >> 7)) & (j >= 0) & (j < 33))
        channel = (row >> 2) & 3
        lines = as_bf16((y == channel * 80 + 2 * (3 * (row >> 4) + third) + (row & 3)) & (channel < 3))
        moved = dot(rounded, spread).astype(BF16)
        term = dot(lines, moved)
        picked = term if picked is None else picked + term
    picked = picked.astype(BF16)
    for line in range(11):
        for k in range(4):
            stacked[line, k * 16 : k * 16 + 16, :] = picked[line * 16 : line * 16 + 16, k * SPAN : (k + 1) * SPAN]


def pixel_windows(parts):
    return pl.pallas_call(
        pixel_kernel,
        out_shape=jax.ShapeDtypeStruct((11, 64, SPAN), BF16),
        scratch_shapes=[
            pltpu.VMEM((240, SPAN), F32),
            pltpu.VMEM((240, SPAN), F32),
            pltpu.VMEM((PACKED, SPAN), F32),
        ],
        compiler_params=pltpu.CompilerParams(vmem_limit_bytes=VMEM_LIMIT),
        name="pixels",
    )(parts)


def finish_kernel(
    parts_hbm, stacked_hbm, gate_hbm, back_hbm, kernel_hbm, taps_hbm, own_hbm, handed_hbm, before_hbm, after_hbm, bias_hbm,
    out, parts, stacked, gate, back, kernel, taps, own, handed, sides, bias, strips, columns, near, far, semaphores,
):
    pairs = [(parts_hbm.at[:, PACKED:, :], parts), (own_hbm, own), (bias_hbm, bias), (handed_hbm, handed)]
    pairs += [(before_hbm, sides.at[0]), (after_hbm, sides.at[1]), (taps_hbm, taps), (kernel_hbm, kernel)]
    pairs += [(stacked_hbm, stacked), (gate_hbm, gate), (back_hbm, back)]
    copies = fetch(semaphores, pairs)
    for copy in copies[:9]:
        copy.wait()
    rings = ring_gates(parts, own, handed, sides, bias, taps, strips)
    columns[0] = rings[2]
    columns[1] = rings[3]
    copies[9].wait()
    at = iota((PITCH, 512), 0)
    for line in range(11):
        act = dot(stacked[line], kernel[...], TN)
        for third in range(3):
            index = line * 3 + third
            if index == 0:
                scale = rings[0]
            elif index == 32:
                scale = rings[1]
            else:
                scale = gate[index * PITCH : (index + 1) * PITCH, :].astype(F32)
                scale = jnp.where(at == 0, columns[0, index : index + 1, :], scale)
                scale = jnp.where(at == 32, columns[1, index : index + 1, :], scale)
            grad = act[third * 40 : third * 40 + 40] * scale[0:40]
            near[index * 32 : (index + 1) * 32, :] = grad[0:32].astype(BF16)
            far[index * 32 : (index + 1) * 32, :] = grad[1:33].astype(BF16)
    copies[10].wait()
    for chunk in range(4):
        stack = []
        for p in range(2):
            pieces = []
            for a in range(3):
                step, parity = divmod(p + 2 - a, 2)
                start = chunk * 256 + step * 32
                for source in (near, far):
                    pieces.append(source[start : start + 256, parity * 256 : (parity + 1) * 256])
            stack.append(jnp.concatenate(pieces, axis=1))
        found = dot(jnp.concatenate(stack, axis=0), back[...])
        plus, minus = found[:256] + found[256:], found[:256] - found[256:]
        bands = [
            plus[:, :128] + plus[:, 128:],
            minus[:, :128] + minus[:, 128:],
            plus[:, :128] - plus[:, 128:],
            minus[:, :128] - minus[:, 128:],
        ]
        for k, band in enumerate(bands):
            out[chunk * 8 : chunk * 8 + 8, :, k * 128 : (k + 1) * 128] = (0.5 * band).astype(BF16).reshape(8, 32, 128)


def finish(*operands):
    return pl.pallas_call(
        finish_kernel,
        out_shape=jax.ShapeDtypeStruct((32, 32, 512), BF16),
        in_specs=[IN_HBM] * 11,
        scratch_shapes=[
            pltpu.VMEM((8, FAR, SPAN), BF16),
            pltpu.VMEM((11, 64, SPAN), BF16),
            pltpu.VMEM((33 * PITCH, 512), BF16),
            pltpu.VMEM((1536, 256), BF16),
            pltpu.VMEM((64, 512), BF16),
            pltpu.VMEM((1536, 256), BF16),
            pltpu.VMEM((6, 32, 512), BF16),
            pltpu.VMEM((1, FAR, SPAN), BF16),
            pltpu.VMEM((2, 32, 512), BF16),
            pltpu.VMEM((1, 128), F32),
            pltpu.VMEM((8, 56, 512), F32),
            pltpu.VMEM((2, PITCH, 512), F32),
            pltpu.VMEM((33 * 32, 512), BF16),
            pltpu.VMEM((33 * 32, 512), BF16),
            pltpu.SemaphoreType.DMA((11,)),
        ],
        compiler_params=pltpu.CompilerParams(vmem_limit_bytes=WHOLE_VMEM),
        name="finish",
    )(*operands)


SWAP = [(0, 1), (1, 0)]
ROW = ("zhi", "core")


def on_device(reward_grad, embed_weight, crop_offsets, features, conv_weight, conv_bias, out_weight):
    mine = lax.all_to_all(view_pairs(reward_grad), "tok", split_axis=0, concat_axis=0, tiled=True)
    coarse = features[0]
    top, bottom, embed_weight = lax.optimization_barrier((coarse[:1], coarse[31:], embed_weight))
    partner_top = lax.ppermute(top, "core", SWAP)
    partner_bottom = lax.ppermute(bottom, "core", SWAP)
    other_weight = lax.ppermute(embed_weight, "core", SWAP)
    spread, own, ends = edges_of(coarse, embed_weight, other_weight, partner_top, partner_bottom)
    mine, spread, ends, own = lax.optimization_barrier((mine, spread, ends, own))
    partials = place_partials(crop_offsets.T, mine, lax.ppermute(mine, "core", SWAP), spread, ends)
    partials, coarse, own = lax.optimization_barrier((partials, coarse, own))
    parts = lax.all_to_all(partials, ("zhi", "seq"), split_axis=0, concat_axis=0, tiled=True)
    before = lax.ppermute(own[3], "seq", [(i, i + 1) for i in range(3)])
    after = lax.ppermute(own[2], "seq", [(i + 1, i) for i in range(3)])
    small = out_weight.transpose(0, 1, 3, 2).reshape(9, 3, 128)
    bias = conv_bias[None]
    gate = gates(coarse, conv_weight, bias, small)
    parts, gate, before, after = lax.optimization_barrier((parts, gate, before, after))
    slot = (1 - lax.axis_index("zhi")) * 4 + lax.axis_index("seq")
    handed = lax.ppermute(lax.dynamic_slice(parts, (slot, PACKED, 0), (1, FAR, SPAN)), "core", SWAP)
    return finish(parts, pixel_windows(parts), *gate, own, handed, before, after, bias)[None]


def solution(mesh):
    split = Mesh(mesh.devices.reshape(16, 2, 2, 4), ("tok", "zhi", "core", "seq"))
    placed = (
        P(None, "tok", ("zhi", "core", "seq")),
        P(("zhi", "core", "seq"), None),
        P("tok", None),
        P("tok", ROW, "seq", None),
        P(),
        P(),
        P(),
    )
    return jax.shard_map(
        on_device,
        mesh=split,
        in_specs=placed,
        out_specs=P("tok", ROW, "seq", None),
        check_vma=False,
    )
```

```python
import jax
import jax.numpy as jnp
from jax import lax
from jax.experimental import pallas as pl
from jax.experimental.pallas import tpu as pltpu
from jax.sharding import Mesh
from jax.sharding import PartitionSpec as P

PIXEL_STD = (0.26862954, 0.26130258, 0.27577711)
BF16 = jnp.bfloat16
F32 = jnp.float32
VIEWS = 4
TILE_PIX = 68
SPAN = 128
HALF_TILE = 34
BAND = 80
PACKED = 112
FAR = 64
PITCH = 48
NT = (((1,), (1,)), ((), ()))
TN = (((0,), (0,)), ((), ()))
VMEM_LIMIT = 16 * 2**20
WHOLE_VMEM = 60 * 2**20
IN_HBM = pl.BlockSpec(memory_space=pltpu.HBM)
IN_VMEM = pl.BlockSpec(memory_space=pltpu.VMEM)


def iota(shape, axis):
    return lax.broadcasted_iota(jnp.int32, shape, axis)


def dot(a, b, dims=(((1,), (0,)), ((), ()))):
    return lax.dot_general(a, b, dims, preferred_element_type=F32)


def fetch(semaphores, pairs):
    copies = [pltpu.make_async_copy(src, dst, semaphores.at[k]) for k, (src, dst) in enumerate(pairs)]
    for copy in copies:
        copy.start()
    return copies


def as_bf16(mask):
    return jnp.where(mask, 1.0, 0.0).astype(BF16)


def pair_kernel(reward, out):
    for pair in range(32):
        out[pair] = jnp.concatenate([reward[2 * pair], reward[2 * pair + 1]], axis=1)


def view_pairs(reward):
    return pl.pallas_call(
        pair_kernel,
        out_shape=jax.ShapeDtypeStruct((32, 16, SPAN), BF16),
        compiler_params=pltpu.CompilerParams(vmem_limit_bytes=VMEM_LIMIT),
        name="pairs",
    )(reward)


def place_kernel(offsets, reward, other, spread, ends, out, flat, left, strips, across, canvas, packed, rows):
    own, theirs = [each[...].astype(F32).reshape(512, SPAN) for each in (reward, other)]
    low = iota((512, SPAN), 1) < 64
    flat[0] = jnp.where(low, own, pltpu.roll(theirs, 64, 1))
    flat[1] = jnp.where(low, pltpu.roll(own, 64, 1), theirs)
    for view in range(VIEWS):
        for patch in range(16):
            top = (patch // 4) * 64 + view * 16
            side = (patch % 4) * SPAN
            values = flat[view % 2, pl.ds((view // 2) * 16 + patch, 16, stride=32), :]
            left[top : top + 16, side : side + SPAN] = values.astype(BF16)
    low = iota((64, SPAN), 1) < 64
    own_group = ((iota((256, 512), 0) >> 4) & 3) == (iota((256, 512), 1) >> 7)
    for quad in range(11):
        blocks = [jnp.concatenate([spread[4 * quad + k]] * 4, axis=0) for k in range(4)]
        weights = jnp.concatenate([jnp.concatenate(blocks, axis=0)] * 4, axis=1)
        part = dot(left[...], jnp.where(own_group, weights, jnp.zeros((256, 512), BF16)), NT)
        for member in range(2):
            own = [part[64 * h : 64 * h + 64, member * SPAN : (member + 1) * SPAN] for h in range(4)]
            turned = [pltpu.roll(piece, 64, 1) for piece in own]
            for odd in range(2):
                start = (4 * quad + 2 * member + odd) * 16
                for side in range(2):
                    a, b = 2 * side, 2 * side + 1
                    if odd == 0:
                        joined = jnp.where(low, own[a], turned[b]).astype(BF16)
                    else:
                        joined = jnp.where(low, turned[a], own[b]).astype(BF16)
                    for view in range(VIEWS):
                        strips[view, start : start + 16, side * SPAN : (side + 1) * SPAN] = joined[
                            view * 16 : view * 16 + 16
                        ]
    slot, lane = iota((256, 512), 0), iota((256, 512), 1)
    gap = (lane >> 7) * 64 - 2 + (lane & 127) - (slot >> 4) * 14 - (slot & 15)
    gap = jnp.where(((slot & 15) < 14) & ((lane & 127) < TILE_PIX), gap, -1000)
    for view in range(VIEWS):
        cols = as_bf16(gap == offsets[1, view])
        for channel in range(3):
            across[channel, view * 224 : (view + 1) * 224, :] = dot(
                strips[view, channel * 224 : (channel + 1) * 224, :], cols
            ).astype(BF16)
    step, index = iota((BAND, 896), 0), iota((1, 896), 1)
    local, corner = index, jnp.zeros((1, 896), jnp.int32) + offsets[0, 0]
    for view in range(1, VIEWS):
        local = jnp.where(index >= 224 * view, index - 224 * view, local)
        corner = jnp.where(index >= 224 * view, offsets[0, view], corner)
    first = corner + 14 * (local & 15) + (local >> 4)
    core = lax.axis_index("core")
    for high in range(2):
        y = step + (64 * (2 * high + core) - 2)
        hit = as_bf16((y == first) & (step < TILE_PIX))
        rows[high * BAND : (high + 1) * BAND, :] = hit
    for channel in range(3):
        canvas[channel] = dot(rows[...], across[channel])
    lane = iota((HALF_TILE, SPAN), 1)
    wide_lane = iota((BAND, SPAN), 1)
    for high in range(2):
        for column in range(4):
            side = slice(column * SPAN, (column + 1) * SPAN)
            top = high * BAND
            for channel in range(3):
                upper = canvas[channel, top : top + HALF_TILE, side]
                lower = pltpu.roll(canvas[channel, top + HALF_TILE : top + 2 * HALF_TILE, side], 64, 1)
                packed[channel * HALF_TILE : (channel + 1) * HALF_TILE, :] = jnp.where(lane < 64, upper, lower)
            last = [canvas[channel, top : top + BAND, side] for channel in range(3)]
            joined = jnp.where(wide_lane < 68, last[0], pltpu.roll(last[1], 4, 1))
            joined = jnp.where(wide_lane < 72, joined, pltpu.roll(last[2], 8, 1))
            rest = None
            for block in range(7):
                piece = pltpu.roll(joined[block * 10 : block * 10 + 10], (64 + block * 12) % SPAN, 1)
                rest = piece if block == 0 else jnp.where(wide_lane[:10] < block * 12, rest, piece)
            packed[3 * HALF_TILE :, :] = rest
            out[high * 4 + column, 0:PACKED, :] = packed[...].astype(BF16)
            out[high * 4 + column, PACKED:, :] = ends[high * 4 + column]


def place_partials(offsets, reward, other, spread, ends):
    return pl.pallas_call(
        place_kernel,
        out_shape=jax.ShapeDtypeStruct((8, PACKED + FAR, SPAN), BF16),
        in_specs=[pl.BlockSpec(memory_space=pltpu.SMEM)] + [IN_VMEM] * 4,
        scratch_shapes=[
            pltpu.VMEM((2, 512, SPAN), F32),
            pltpu.VMEM((256, 512), BF16),
            pltpu.VMEM((VIEWS, 704, 256), BF16),
            pltpu.VMEM((3, 896, 512), BF16),
            pltpu.VMEM((3, 2 * BAND, 512), F32),
            pltpu.VMEM((PACKED, SPAN), F32),
            pltpu.VMEM((2 * BAND, 896), BF16),
        ],
        compiler_params=pltpu.CompilerParams(vmem_limit_bytes=VMEM_LIMIT),
        name="place",
    )(offsets, reward, other, spread, ends)


def edge_kernel(
    features_hbm, weight_hbm, other_hbm, top_hbm, bottom_hbm,
    spread, own, out, features, weights, halves, semaphores,
):
    high, core, column = lax.axis_index("zhi"), lax.axis_index("core"), lax.axis_index("seq")
    pairs = [(weight_hbm, weights.at[0]), (other_hbm, weights.at[1])]
    pairs += [(top_hbm, own.at[4:5]), (bottom_hbm, own.at[5:6]), (features_hbm, features)]
    copies = fetch(semaphores, pairs)
    copies[0].wait()
    copies[1].wait()
    slot = iota((704, 588), 0)
    pick = as_bf16(((slot >> 4) * 14 + (slot & 15) == iota((704, 588), 1)) & ((slot & 15) < 14))
    both = jnp.concatenate([weights[0], weights[1]], axis=0)
    spread[...] = dot(pick, both, NT).astype(BF16).reshape(44, 16, SPAN)
    for copy in copies[2:]:
        copy.wait()
    top, bottom = own[4].astype(F32), own[5].astype(F32)
    far = jnp.where(core == 0, bottom, top)
    nothing = jnp.zeros((8, SPAN), F32)

    def put_ends(slot, above, below):
        rows = [each[:, k * SPAN : (k + 1) * SPAN] for k in range(4) for each in (above, below)]
        out[slot, 0:16, :] = jnp.concatenate(rows + [nothing], axis=0).astype(BF16)

    out[...] = jnp.zeros_like(out)
    own[0] = features[0]
    own[1] = features[31]
    across = jnp.where(
        high == 0,
        jnp.where(core == 0, bottom, own[1].astype(F32)),
        jnp.where(core == 1, top, own[0].astype(F32)),
    )
    half = jnp.where(core == high, across[0:16], across[16:32]).astype(BF16)
    for k in range(4):
        out[(1 - high) * 4 + column, 16 * k : 16 * k + 16, :] = half[:, k * SPAN : (k + 1) * SPAN]
    for index, (step, side, row, end) in enumerate(((-1, 0, 0, 0), (1, 16, 15, 31))):
        parts = []
        for k in range(4):
            lanes = slice(k * SPAN, (k + 1) * SPAN)
            halves[k] = features[:, side : side + 16, lanes].astype(F32).reshape(512, SPAN)
            parts.append(halves[k, pl.ds(row, 32, stride=16), :])
        own[2 + index] = jnp.concatenate(parts, axis=1).astype(BF16)
        there = jnp.clip(column + step, 0, 3)

        @pl.when(there != column)
        def _():
            put_ends(high * 4 + there, bottom[end : end + 1], top[end : end + 1])
            put_ends((1 - high) * 4 + there, far[end : end + 1], far[end : end + 1])


def edges_of(features, weight, other_weight, partner_top, partner_bottom):
    return pl.pallas_call(
        edge_kernel,
        out_shape=(
            jax.ShapeDtypeStruct((44, 16, SPAN), BF16),
            jax.ShapeDtypeStruct((6, 32, 512), BF16),
            jax.ShapeDtypeStruct((8, FAR, SPAN), BF16),
        ),
        in_specs=[IN_HBM] * 5,
        scratch_shapes=[
            pltpu.VMEM((32, 32, 512), BF16),
            pltpu.VMEM((2, 64, 588), BF16),
            pltpu.VMEM((4, 512, SPAN), F32),
            pltpu.SemaphoreType.DMA((5,)),
        ],
        compiler_params=pltpu.CompilerParams(vmem_limit_bytes=48 * 2**20),
        name="edges",
    )(features, weight, other_weight, partner_top, partner_bottom)


def inverse_haar(values):
    smooth, vertical, horizontal, diagonal = [values[:, k * 128 : (k + 1) * 128].astype(F32) for k in range(4)]
    upper_sum = smooth + vertical
    lower_sum = smooth - vertical
    upper_diff = horizontal + diagonal
    lower_diff = horizontal - diagonal
    return [
        0.5 * (upper_sum + upper_diff),
        0.5 * (upper_sum - upper_diff),
        0.5 * (lower_sum + lower_diff),
        0.5 * (lower_sum - lower_diff),
    ]


def slope_of(pre):
    sigmoid = 0.5 + 0.5 * jnp.tanh(0.5 * pre)
    return sigmoid * (1.0 + pre * (1.0 - sigmoid))


def gate_kernel(
    features_hbm, weight_hbm, bias, out_weight,
    out, back, kernel, taps, features, weight, fine, near, far, small, semaphores,
):
    copies = fetch(semaphores, [(features_hbm, features), (weight_hbm, weight)])
    copies[0].wait()

    @pl.loop(0, 32, unroll=4)
    def _(line):
        for k, phase in enumerate(inverse_haar(features[line])):
            fine[line + 1, 8:40, k * 128 : (k + 1) * 128] = phase

    copies[1].wait()

    @pl.loop(0, 34, unroll=2)
    def _(line):
        start = pl.multiple_of(line * PITCH, PITCH)
        near[pl.ds(start, PITCH), :] = fine[line, 7:55, :].astype(BF16)
        far[pl.ds(start, PITCH), :] = fine[line, 8:56, :].astype(BF16)

    nothing = jnp.zeros((128, 128), BF16)
    for a in range(3):
        for u in range(4):
            start = (a * 4 + u) * 128
            taps[start : start + 128, 0:128] = weight[a, u] if u < 3 else nothing
            taps[start : start + 128, 128:] = weight[a, u - 1] if u > 0 else nothing
    wide_bias = jnp.concatenate([bias[...], bias[...]], axis=1)
    count = 11 * PITCH
    for chunk in range(3):
        for phase in range(2):
            pieces = []
            for a in range(3):
                lines, parity = divmod(phase + a, 2)
                start = chunk * count + lines * PITCH
                for source in (near, far):
                    pieces.append(source[start : start + count, parity * 256 : (parity + 1) * 256])
            slope = slope_of(dot(jnp.concatenate(pieces, axis=1), taps[...]) + wide_bias)
            here = chunk * count
            out[here : here + count, phase * 256 : (phase + 1) * 256] = slope.astype(BF16)
    for a in range(3):
        for u in range(4):
            start = (a * 4 + u) * 128
            for q in range(2):
                b = q + 2 - u
                block = weight[a, b].astype(F32).T.astype(BF16) if 0 <= b <= 2 else nothing
                back[start : start + 128, q * 128 : (q + 1) * 128] = block
    slot = iota((64, 32), 0)
    small[...] = jnp.zeros_like(small)
    for k in range(9):
        small[3 * k : 3 * k + 3, :] = out_weight[k].astype(F32)
    for k in range(4):
        a, b = k // 2 + 2 - (slot & 3), k % 2 + 2 - (slot >> 4)
        channel = (slot >> 2) & 3
        valid = (a >= 0) & (a <= 2) & (b >= 0) & (b <= 2) & (channel < 3)
        window = as_bf16((iota((64, 32), 1) == a * 9 + b * 3 + channel) & valid)
        kernel[:, k * 128 : (k + 1) * 128] = dot(window, small[...].astype(BF16)).astype(BF16)


def gates(features, weight, bias, out_weight):
    return pl.pallas_call(
        gate_kernel,
        out_shape=(
            jax.ShapeDtypeStruct((33 * PITCH, 512), BF16),
            jax.ShapeDtypeStruct((1536, 256), BF16),
            jax.ShapeDtypeStruct((64, 512), BF16),
            jax.ShapeDtypeStruct((1536, 256), BF16),
        ),
        in_specs=[IN_HBM] * 2 + [IN_VMEM] * 2,
        scratch_shapes=[
            pltpu.VMEM((32, 32, 512), BF16),
            pltpu.VMEM((3, 3, 128, 128), BF16),
            pltpu.VMEM((34, 56, 512), F32),
            pltpu.VMEM((34 * PITCH, 512), BF16),
            pltpu.VMEM((34 * PITCH, 512), BF16),
            pltpu.VMEM((32, 128), F32),
            pltpu.SemaphoreType.DMA((2,)),
        ],
        compiler_params=pltpu.CompilerParams(vmem_limit_bytes=WHOLE_VMEM),
        cost_estimate=pl.CostEstimate(flops=5 * 10**9, bytes_accessed=4 * 10**6, transcendentals=2 * 10**6),
        name="gate",
    )(features, weight, bias, out_weight)


def ring_gates(parts, own, handed, sides, bias, taps, strips):
    high, core, column = lax.axis_index("zhi"), lax.axis_index("core"), lax.axis_index("seq")
    other = (1 - high) * 4

    def ends(slot):
        rows = parts[slot, 0:16, :].astype(F32)
        return [jnp.concatenate([rows[2 * k + e : 2 * k + e + 1] for k in range(4)], axis=1) for e in range(2)]

    def only(condition, values):
        return jnp.where(condition, values, 0.0)

    lines = [own[k].astype(F32) for k in range(6)]
    halves = []
    for k in range(4):
        first = parts[other + column, 16 * k : 16 * k + 16, :].astype(F32)
        halves.append(jnp.concatenate([first, handed[0, 16 * k : 16 * k + 16, :].astype(F32)], axis=0))
    distant = jnp.concatenate(halves, axis=1)
    above = jnp.where(core == 1, lines[5], only(high == 1, distant))
    below = jnp.where(core == 0, lines[4], only(high == 0, distant))
    sides = [sides[k].astype(F32) for k in range(2)]
    corners = []
    for step in (-1, 1):
        there = jnp.clip(column + step, 0, 3)
        inside = there != column
        near_ends, far_ends = ends(high * 4 + there), ends(other + there)
        corners.append(
            [
                only(inside, jnp.where(core == 1, near_ends[0], only(high == 1, far_ends[0]))),
                only(inside, jnp.where(core == 0, near_ends[1], only(high == 0, far_ends[1]))),
            ]
        )
    put = [
        (above, corners[0][0], corners[1][0]),
        (lines[0], sides[0][0:1], sides[1][0:1]),
        (lines[1], sides[0][31:32], sides[1][31:32]),
        (below, corners[0][1], corners[1][1]),
        (sides[0], corners[0][0], corners[0][1]),
        (lines[2], above[0:1], below[0:1]),
        (lines[3], above[31:32], below[31:32]),
        (sides[1], corners[1][0], corners[1][1]),
    ]
    for k, (middle, first, last) in enumerate(put):
        strips[k, 0:8, :] = jnp.zeros((8, 512), F32)
        strips[k, 40:56, :] = jnp.zeros((16, 512), F32)
        for at, values in ((8, middle), (7, first), (40, last)):
            for q, phase in enumerate(inverse_haar(values)):
                strips[k, at : at + values.shape[0], q * 128 : (q + 1) * 128] = phase
    shifted = [[strips[k, 7 + d : 55 + d, :].astype(BF16) for d in range(2)] for k in range(8)]
    wide_bias = jnp.concatenate([bias[...], bias[...]], axis=1)
    found = []
    for phase in range(2):
        stack = []
        for strip in range(4):
            pieces = []
            for a in range(3):
                step, parity = divmod(phase + a, 2)
                for turn in range(2):
                    if strip < 2:
                        source = shifted[2 * strip + step][turn]
                    else:
                        source = shifted[2 * strip + turn][step]
                    pieces.append(source[:, parity * 256 : (parity + 1) * 256])
            stack.append(jnp.concatenate(pieces, axis=1))
        found.append(slope_of(dot(jnp.concatenate(stack, axis=0), taps[...]) + wide_bias))
    rings = [
        jnp.concatenate([each[strip * PITCH : (strip + 1) * PITCH] for each in found], axis=1) for strip in range(4)
    ]
    at, lane = iota((PITCH, 512), 0), iota((PITCH, 512), 1)
    even, upper = (lane & 255) < 128, lane < 256
    left = (column == 0) & even
    right = (column == 3) & jnp.logical_not(even)
    beside = (left & (at == 0)) | (right & (at == 32))
    first_line = (high == 0) & (core == 0) & upper
    last_line = (high == 1) & (core == 1) & jnp.logical_not(upper)
    masks = [beside | first_line, beside | last_line, left, right]
    return [jnp.where(mask, 0.0, ring) for mask, ring in zip(masks, rings)]


def pixel_kernel(parts, stacked, pixels, edges, total):
    sums = parts[0, 0:PACKED, :].astype(F32)
    for source in range(1, 8):
        sums = sums + parts[source, 0:PACKED, :].astype(F32)
    total[...] = sums
    pixels[...] = jnp.zeros_like(pixels)
    edges[...] = jnp.zeros_like(edges)
    for channel in range(3):
        top = channel * 80
        half = total[channel * HALF_TILE : (channel + 1) * HALF_TILE, :] / PIXEL_STD[channel]
        pixels[top : top + HALF_TILE, :] = half
        pixels[top + HALF_TILE : top + 2 * HALF_TILE, :] = pltpu.roll(half, 64, 1)
        rest = total[3 * HALF_TILE :, :] / PIXEL_STD[channel]
        for block in range(7):
            turn = (64 - block * 12 - channel * 4) % SPAN
            edges[top + block * 10 : top + block * 10 + 10, :] = pltpu.roll(rest, turn, 1)
    rounded = jnp.where(iota((240, SPAN), 1) < 64, pixels[...], edges[...]).astype(BF16)
    picked = None
    x, lane = iota((SPAN, 512), 0), iota((SPAN, 512), 1)
    row, y = iota((176, 240), 0), iota((176, 240), 1)
    for third in range(3):
        j = (lane & 127) - 40 * third
        spread = as_bf16((x == 2 * j + (lane >> 7)) & (j >= 0) & (j < 33))
        channel = (row >> 2) & 3
        lines = as_bf16((y == channel * 80 + 2 * (3 * (row >> 4) + third) + (row & 3)) & (channel < 3))
        moved = dot(rounded, spread).astype(BF16)
        term = dot(lines, moved)
        picked = term if picked is None else picked + term
    picked = picked.astype(BF16)
    for line in range(11):
        for k in range(4):
            stacked[line, k * 16 : k * 16 + 16, :] = picked[line * 16 : line * 16 + 16, k * SPAN : (k + 1) * SPAN]


def pixel_windows(parts):
    return pl.pallas_call(
        pixel_kernel,
        out_shape=jax.ShapeDtypeStruct((11, 64, SPAN), BF16),
        scratch_shapes=[
            pltpu.VMEM((240, SPAN), F32),
            pltpu.VMEM((240, SPAN), F32),
            pltpu.VMEM((PACKED, SPAN), F32),
        ],
        compiler_params=pltpu.CompilerParams(vmem_limit_bytes=VMEM_LIMIT),
        name="pixels",
    )(parts)


def finish_kernel(
    parts_hbm, stacked_hbm, gate_hbm, back_hbm, kernel_hbm, taps_hbm, own_hbm, handed_hbm, before_hbm, after_hbm, bias_hbm,
    out, parts, stacked, gate, back, kernel, taps, own, handed, sides, bias, strips, columns, near, far, semaphores,
):
    pairs = [(parts_hbm.at[:, PACKED:, :], parts), (own_hbm, own), (bias_hbm, bias), (handed_hbm, handed)]
    pairs += [(before_hbm, sides.at[0]), (after_hbm, sides.at[1]), (taps_hbm, taps), (kernel_hbm, kernel)]
    pairs += [(stacked_hbm, stacked), (gate_hbm, gate), (back_hbm, back)]
    copies = fetch(semaphores, pairs)
    for copy in copies[:9]:
        copy.wait()
    rings = ring_gates(parts, own, handed, sides, bias, taps, strips)
    columns[0] = rings[2]
    columns[1] = rings[3]
    copies[9].wait()
    at = iota((PITCH, 512), 0)
    for line in range(11):
        act = dot(stacked[line], kernel[...], TN)
        for third in range(3):
            index = line * 3 + third
            if index == 0:
                scale = rings[0]
            elif index == 32:
                scale = rings[1]
            else:
                scale = gate[index * PITCH : (index + 1) * PITCH, :].astype(F32)
                scale = jnp.where(at == 0, columns[0, index : index + 1, :], scale)
                scale = jnp.where(at == 32, columns[1, index : index + 1, :], scale)
            grad = act[third * 40 : third * 40 + 40] * scale[0:40]
            near[index * 32 : (index + 1) * 32, :] = grad[0:32].astype(BF16)
            far[index * 32 : (index + 1) * 32, :] = grad[1:33].astype(BF16)
    copies[10].wait()
    for chunk in range(4):
        stack = []
        for p in range(2):
            pieces = []
            for a in range(3):
                step, parity = divmod(p + 2 - a, 2)
                start = chunk * 256 + step * 32
                for source in (near, far):
                    pieces.append(source[start : start + 256, parity * 256 : (parity + 1) * 256])
            stack.append(jnp.concatenate(pieces, axis=1))
        found = dot(jnp.concatenate(stack, axis=0), back[...])
        plus, minus = found[:256] + found[256:], found[:256] - found[256:]
        bands = [
            plus[:, :128] + plus[:, 128:],
            minus[:, :128] + minus[:, 128:],
            plus[:, :128] - plus[:, 128:],
            minus[:, :128] - minus[:, 128:],
        ]
        for k, band in enumerate(bands):
            out[chunk * 8 : chunk * 8 + 8, :, k * 128 : (k + 1) * 128] = (0.5 * band).astype(BF16).reshape(8, 32, 128)


def finish(*operands):
    return pl.pallas_call(
        finish_kernel,
        out_shape=jax.ShapeDtypeStruct((32, 32, 512), BF16),
        in_specs=[IN_HBM] * 11,
        scratch_shapes=[
            pltpu.VMEM((8, FAR, SPAN), BF16),
            pltpu.VMEM((11, 64, SPAN), BF16),
            pltpu.VMEM((33 * PITCH, 512), BF16),
            pltpu.VMEM((1536, 256), BF16),
            pltpu.VMEM((64, 512), BF16),
            pltpu.VMEM((1536, 256), BF16),
            pltpu.VMEM((6, 32, 512), BF16),
            pltpu.VMEM((1, FAR, SPAN), BF16),
            pltpu.VMEM((2, 32, 512), BF16),
            pltpu.VMEM((1, 128), F32),
            pltpu.VMEM((8, 56, 512), F32),
            pltpu.VMEM((2, PITCH, 512), F32),
            pltpu.VMEM((33 * 32, 512), BF16),
            pltpu.VMEM((33 * 32, 512), BF16),
            pltpu.SemaphoreType.DMA((11,)),
        ],
        compiler_params=pltpu.CompilerParams(vmem_limit_bytes=52 * 2**20),
        name="finish",
    )(*operands)


SWAP = [(0, 1), (1, 0)]
ROW = ("zhi", "core")


def on_device(reward_grad, embed_weight, crop_offsets, features, conv_weight, conv_bias, out_weight):
    mine = lax.all_to_all(view_pairs(reward_grad), "tok", split_axis=0, concat_axis=0, tiled=True)
    coarse = features[0]
    top, bottom, embed_weight = lax.optimization_barrier((coarse[:1], coarse[31:], embed_weight))
    partner_top = lax.ppermute(top, "core", SWAP)
    partner_bottom = lax.ppermute(bottom, "core", SWAP)
    other_weight = lax.ppermute(embed_weight, "core", SWAP)
    spread, own, ends = edges_of(coarse, embed_weight, other_weight, partner_top, partner_bottom)
    mine, spread, ends, own = lax.optimization_barrier((mine, spread, ends, own))
    partials = place_partials(crop_offsets.T, mine, lax.ppermute(mine, "core", SWAP), spread, ends)
    partials, coarse, own = lax.optimization_barrier((partials, coarse, own))
    parts = lax.all_to_all(partials, ("zhi", "seq"), split_axis=0, concat_axis=0, tiled=True)
    before = lax.ppermute(own[3], "seq", [(i, i + 1) for i in range(3)])
    after = lax.ppermute(own[2], "seq", [(i + 1, i) for i in range(3)])
    small = out_weight.transpose(0, 1, 3, 2).reshape(9, 3, 128)
    bias = conv_bias[None]
    gate = gates(coarse, conv_weight, bias, small)
    parts, gate, before, after = lax.optimization_barrier((parts, gate, before, after))
    slot = (1 - lax.axis_index("zhi")) * 4 + lax.axis_index("seq")
    handed = lax.ppermute(lax.dynamic_slice(parts, (slot, PACKED, 0), (1, FAR, SPAN)), "core", SWAP)
    return finish(parts, pixel_windows(parts), *gate, own, handed, before, after, bias)[None]


def solution(mesh):
    split = Mesh(mesh.devices.reshape(16, 2, 2, 4), ("tok", "zhi", "core", "seq"))
    placed = (
        P(None, "tok", ("zhi", "core", "seq")),
        P(("zhi", "core", "seq"), None),
        P("tok", None),
        P("tok", ROW, "seq", None),
        P(),
        P(),
        P(),
    )
    return jax.shard_map(
        on_device,
        mesh=split,
        in_specs=placed,
        out_specs=P("tok", ROW, "seq", None),
        check_vma=False,
    )
```
